32 devices in a mesh: design: 2 (over y), gx: 4 (over x, core), gy: 4 (over z).
Axes of the slice: x: 2, y: 2, z: 4, core: 2. Of those that a mesh axis runs over, the one named last changes fastest.
Arguments:
- adj_e: float32 [6, 2, 512, 1024], P('design', None, 'gx', 'gy'), parts along dimension 0, may hold values from -6 to 6
- adj_h: float32 [6, 2, 512, 1024], P('design', None, 'gx', 'gy'), parts along dimension 0, may hold values from -6 to 6
- fwd_e: float32 [4, 3, 2, 512, 1024], P('design', None, None, 'gx', 'gy'), parts along dimension 0, may hold values from -6 to 6
- labels: int32 [1024, 1024], P(('design', 'gx'), 'gy'), parts along dimension 0, may hold values from 0 to 7
- eps_table: float32 [8], replicated, may hold values from 1 to 12
- density: float32 [1024, 1024], P(('design', 'gx'), 'gy'), parts along dimension 0, may hold values from 0 to 3
Outputs:
- elec_out: float32 [6, 2, 512, 1024], P('design', None, 'gx', 'gy'), parts along dimension 0
- magn_out: float32 [6, 2, 512, 1024], P('design', None, 'gx', 'gy'), parts along dimension 0
- design_grad: float32 [1024, 1024], P(('design', 'gx'), 'gy'), parts along dimension 0
The draws below stay inside these ranges and needn't reach their ends.
There are 2 independent parts, one for each index of `design`. The reference program is written for one: setup_inputs(seed, part) draws one part's arguments, and reference() takes and returns one part's arrays. A program takes and returns all parts, laid end to end along the dimension named above; an argument that names none is the same for every part. Nothing has to cross between parts.
All inputs are finite; a program needn't handle non-finite values.
Results may differ from the reference program's by a relative error of at most 0.0001.
Values sent between devices are 32-bit elements; how exact they have to be, the bound alone decides.
No kernel may reach another device: no remote copies, remote signals or barrier semaphores. Data moves between devices by JAX's collectives and lax.ppermute only.
A program may use at most 64 MiB of HBM per device.

```python
import jax
import jax.numpy as jnp
from jax import lax

NZ = 2
STEPS = 2
NMAT = 8
FILT = 16
NX = 512
NY = 1024


def draw_adj_e(key, part):
    key = jax.random.fold_in(key, 7)
    own = jax.random.normal(key, (3, NZ, NX, NY), jnp.float32)
    return jnp.clip(own, -6.0, 6.0)


def draw_fwd_e(key, part):
    key = jax.random.fold_in(key, 13)
    own = jax.random.normal(key, (STEPS, 3, NZ, NX, NY), jnp.float32)
    return jnp.clip(own, -6.0, 6.0)


def set_ends(result, key, low, largest):
    extent = result.shape
    spot = [jax.random.randint(jax.random.fold_in(key, axis), (), 0, extent[axis]) for axis in range(len(extent))]
    result = result.at[tuple(spot)].set(low)
    longest = extent.index(max(extent))
    spot[longest] = (spot[longest] + 1) % extent[longest]
    return result.at[tuple(spot)].set(largest)


def level_of(rng, dims, split, least, high):
    gain, own = 1.0, jax.random.fold_in(rng, 6)
    for axis_at, parts in split:
        steps = jnp.exp(jax.random.uniform(jax.random.fold_in(own, axis_at), (parts,), jnp.float32, least / len(split), high / len(split)))
        gain = gain * jnp.repeat(steps, dims[axis_at] // parts).reshape([-1 if axis == axis_at else 1 for axis in range(len(dims))])
    return gain


def bell_draw(stream_key, shape, deviation, most, pieces=(), held_as=jnp.bfloat16):
    factor_of = level_of(stream_key, shape, pieces, -0.22, 0.18) if pieces else 1.0
    array = jax.random.normal(stream_key, shape, jnp.float32) * deviation * factor_of
    return jnp.minimum(jnp.maximum(array, -most), most).astype(held_as)


def setup_inputs(seed: int = 0, part: int = 0) -> dict:
    key_list = jax.random.split(jax.random.key(seed), 7)
    part_splits = jax.random.split(jax.random.fold_in(key_list[6], part), 7)
    adj_e = draw_adj_e(jax.random.fold_in(jax.random.fold_in(key_list[6], part), 71), part)
    adj_h = bell_draw(part_splits[1], (3, NZ, NX, NY), 1.0, 6.0, ((2, 4), (3, 4)), jnp.float32)
    fwd_e = draw_fwd_e(jax.random.fold_in(jax.random.fold_in(key_list[6], part), 71), part)
    labels = set_ends(jax.random.randint(part_splits[3], (NX, NY), 0, NMAT), jax.random.fold_in(part_splits[3], 1), 0, NMAT - 1).astype(jnp.int32)
    eps_table = jnp.clip(jax.random.uniform(key_list[4], (NMAT,), jnp.float32, 1.0, 12.0), 1.0, 12.0)
    density = jnp.clip(3.0 * jax.random.uniform(part_splits[5], (NX, NY), jnp.float32) ** level_of(part_splits[5], (NX, NY), ((0, 4), (1, 4)), -0.2, 0.2), 0.0, 3.0)
    return dict(adj_e=adj_e, adj_h=adj_h, fwd_e=fwd_e, labels=labels, eps_table=eps_table, density=density)


courant = 0.5
spread_ratio = 0.6

def taps(radius):
    offsets = jnp.arange(-radius, radius + 1).astype(jnp.float32)
    spread = spread_ratio * radius
    weights = jnp.exp(-offsets * offsets / (2.0 * spread * spread))
    return weights / jnp.sqrt(jnp.sum(weights * weights))

def lower(field, axis):
    return jnp.roll(field, 1, axis=axis)

def upper(field, axis):
    return jnp.roll(field, -1, axis=axis)

def below_depth(field):
    return jnp.concatenate([jnp.zeros_like(field[:1]), field[:-1]], axis=0)

def above_depth(field):
    return jnp.concatenate([field[1:], jnp.zeros_like(field[:1])], axis=0)

def periodic_filter(values, radius, count, axis):
    weights = taps(radius)
    places = jnp.arange(-radius, radius + 1) % count
    kernel = jnp.zeros((count,), jnp.float32).at[places].set(weights)
    spectrum = jnp.fft.rfft(values, axis=axis) * jnp.expand_dims(jnp.fft.rfft(kernel), 1 - axis)
    return jnp.fft.irfft(spectrum, n=count, axis=axis)

def reference(adj_e, adj_h, fwd_e, labels, eps_table, density):
    choose = labels[None, :, :] == jnp.arange(NMAT, dtype=jnp.int32)[:, None, None]
    permittivity = lax.optimization_barrier(jnp.sum(jnp.where(choose, eps_table[:, None, None], jnp.float32(0.0)), axis=0)) + density
    ratio = courant / permittivity
    electric = [adj_e[0], adj_e[1], adj_e[2]]
    magnetic = [adj_h[0], adj_h[1], adj_h[2]]
    gradient = jnp.zeros(labels.shape, jnp.float32)
    for instant in range(STEPS):
        rotor = [magnetic[2] - lower(magnetic[2], 2) - (magnetic[1] - below_depth(magnetic[1])), magnetic[0] - below_depth(magnetic[0]) - (magnetic[2] - lower(magnetic[2], 1)), magnetic[1] - lower(magnetic[1], 1) - (magnetic[0] - lower(magnetic[0], 2))]
        electric = [electric[component] - ratio[None] * rotor[component] for component in range(3)]
        product = electric[0] * fwd_e[instant, 0] + electric[1] * fwd_e[instant, 1] + electric[2] * fwd_e[instant, 2]
        gradient = gradient + lax.optimization_barrier(jnp.sum(product, axis=0))
        rotor_e = [upper(electric[2], 2) - electric[2] - (above_depth(electric[1]) - electric[1]), above_depth(electric[0]) - electric[0] - (upper(electric[2], 1) - electric[2]), upper(electric[1], 1) - electric[1] - (upper(electric[0], 2) - electric[0])]
        magnetic = [magnetic[component] + courant * rotor_e[component] for component in range(3)]
    filtered = periodic_filter(periodic_filter(gradient, FILT, NX, 0), FILT, NY, 1)
    return (jnp.stack(electric), jnp.stack(magnetic), filtered.astype(jnp.float32))
```

```python
import math

import jax
import jax.numpy as jnp
from jax import lax
from jax.experimental import pallas as pl
from jax.experimental.pallas import tpu as pltpu
from jax.sharding import PartitionSpec as P

STEPS = 2
NMAT = 8
FILT = 16

courant = 0.5
spread_ratio = 0.6

F32 = jnp.float32
HIGHEST = lax.Precision.HIGHEST

LO_G, LO_E1T, LO_E1Z, LO_E2T, LO_E2Z = 0, 16, 18, 20, 22
LO_F0T, LO_F0Z, LO_F1T, LO_F1N, LO_F1Z = 24, 26, 28, 30, 32
LO_W1T, LO_W1Z, LO_R0, LO_R1, LO_ROWS = 34, 36, 38, 39, 40
HI_G, HI_H0T, HI_H0Z, HI_H1T, HI_H1Z = 0, 16, 18, 20, 22
HI_WT, HI_WN, HI_WZ, HI_R, HI_ROWS = 24, 26, 28, 30, 32
LANE_HI = 64
EXT = 24


def tap(distance):
    spread = spread_ratio * FILT
    norm = math.sqrt(sum(math.exp(-d * d / (spread * spread)) for d in range(-FILT, FILT + 1)))
    far = distance.astype(F32)
    value = jnp.exp(-far * far / (2.0 * spread * spread)) / norm
    return jnp.where(jnp.abs(distance) <= FILT, value, F32(0.0))


def iota(shape, dim):
    return lax.broadcasted_iota(jnp.int32, shape, dim)


def local_solve(e0, h0, fwd, ratio):
    n, m = ratio.shape
    row, col = iota((n, m), 0), iota((n, m), 1)
    nz = len(e0[0])

    def lx(f):
        return jnp.where(row == 0, 0.0, pltpu.roll(f, 1, 0))

    def ux(f):
        return jnp.where(row == n - 1, 0.0, pltpu.roll(f, n - 1, 0))

    def ly(f):
        return jnp.where(col == 0, 0.0, pltpu.roll(f, 1, 1))

    def uy(f):
        return jnp.where(col == m - 1, 0.0, pltpu.roll(f, m - 1, 1))

    def electric(e, h):
        out = [[None] * nz for _ in range(3)]
        for z in range(nz):
            hx, hy, hz = h[0][z], h[1][z], h[2][z]
            dzx = hx - h[0][z - 1] if z > 0 else hx
            dzy = hy - h[1][z - 1] if z > 0 else hy
            out[0][z] = e[0][z] - ratio * ((hz - ly(hz)) - dzy)
            out[1][z] = e[1][z] - ratio * (dzx - (hz - lx(hz)))
            out[2][z] = e[2][z] - ratio * ((hy - lx(hy)) - (hx - ly(hx)))
        return out

    def magnetic(e, h):
        out = [[None] * nz for _ in range(3)]
        for z in range(nz):
            ex, ey, ez = e[0][z], e[1][z], e[2][z]
            dzx = e[0][z + 1] - ex if z < nz - 1 else -ex
            dzy = e[1][z + 1] - ey if z < nz - 1 else -ey
            out[0][z] = h[0][z] + courant * ((uy(ez) - ez) - dzy)
            out[1][z] = h[1][z] + courant * (dzx - (ux(ez) - ez))
            out[2][z] = h[2][z] + courant * ((ux(ey) - ey) - (uy(ex) - ex))
        return out

    def product(e, f):
        total = None
        for c in range(3):
            for z in range(nz):
                term = e[c][z] * f[c][z]
                total = term if total is None else total + term
        return total

    e1 = electric(e0, h0)
    grad = product(e1, fwd[0])
    h1 = magnetic(e1, h0)
    e2 = electric(e1, h1)
    grad = grad + product(e2, fwd[1])
    h2 = magnetic(e2, h1)
    return e1, h1, e2, h2, grad


def seam(sgn, a, b, up, down):
    odd = iota(a["h0t"].shape, 0) % 2 == 1
    half = sgn * courant

    def uz(f):
        return jnp.where(odd, 0.0, pltpu.roll(f, 7, 0))

    def lz(f):
        return jnp.where(odd, pltpu.roll(f, 1, 0), 0.0)

    rb, rb1, ra = sgn * b["r0"], sgn * b["r1"], sgn * a["r"]
    d = {}
    e1t = rb * a["h0z"]
    e1z = -rb * a["h0t"]
    e1t_b = b["e1t"] + e1t
    e1z_b = b["e1z"] + e1z
    ah1t = half * e1z_b
    ah1z = -half * e1t_b
    h1t_a = a["h1t"] + ah1t
    h1z_a = a["h1z"] + ah1z
    bh1t = -half * e1z
    bh1n = half * ((uz(e1t) - e1t) - (up(e1z) - e1z))
    bh1z = half * e1t
    e2t = e1t - rb * ((bh1z - h1z_a) - (bh1n - lz(bh1n)))
    e2n = -rb * ((bh1t - lz(bh1t)) - (bh1z - down(bh1z)))
    e2z = e1z - rb * ((bh1n - down(bh1n)) - (bh1t - h1t_a))
    f2t = rb1 * bh1z
    f2z = -rb1 * bh1t
    at = ah1z
    an = (ah1t - lz(ah1t)) - (ah1z - down(ah1z))
    az = -ah1t
    g2t, g2n, g2z = -ra * at, -ra * an, -ra * az
    gb0 = b["f0t"] * e1t + b["f0z"] * e1z + b["f1t"] * e2t + b["f1n"] * e2n + b["f1z"] * e2z
    gb1 = sgn * (b["w1t"] * bh1z - b["w1z"] * bh1t)
    ga = -sgn * (a["wt"] * at + a["wn"] * an + a["wz"] * az)
    e2t_b = b["e2t"] + e2t
    e2z_b = b["e2z"] + e2z
    d["b_e1z"], d["b_h1n"], d["b_h1z"], d["a_h1z"] = e1z, bh1n, bh1z, ah1z
    none = jnp.zeros_like(e1t)
    d["e"] = {"t": (none, g2t, e2t, f2t), "n": (none, g2n, e2n, none), "z": (none, g2z, e2z, f2z)}
    d["h"] = {
        "t": (
            half * g2z,
            ah1t + half * ((e2z_b - g2z) - (uz(g2n) - g2n)),
            bh1t + half * ((f2z - e2z) - (uz(e2n) - e2n)),
            -half * f2z,
        ),
        "n": (
            none,
            half * ((uz(g2t) - g2t) - (up(g2z) - g2z)),
            bh1n + half * ((uz(e2t) - e2t) - (up(e2z) - e2z)),
            half * ((uz(f2t) - f2t) - (up(f2z) - f2z)),
        ),
        "z": (
            -half * g2t,
            ah1z + half * ((up(g2n) - g2n) - (e2t_b - g2t)),
            bh1z + half * ((up(e2n) - e2n) - (f2t - e2t)),
            half * f2t,
        ),
    }
    d["gb0"], d["gb1"], d["ga"] = (g + pltpu.roll(g, 7, 0) for g in (gb0, gb1, ga))
    return d


def two(first, second, at, count=2):
    if count == 1:
        one, other = first[at : at + 1], second[at : at + 1]
        parts = [one, one, other, other]
    else:
        parts = [first[at : at + 2], second[at : at + 2]]
    parts.append(jnp.zeros((4, first.shape[1]), F32))
    return jnp.concatenate(parts, axis=0)


def seam_inputs(left_hi, my_hi, my_lo, right_lo):
    a = {
        "h0t": two(left_hi, my_hi, HI_H0T),
        "h0z": two(left_hi, my_hi, HI_H0Z),
        "h1t": two(left_hi, my_hi, HI_H1T),
        "h1z": two(left_hi, my_hi, HI_H1Z),
        "wt": two(left_hi, my_hi, HI_WT),
        "wn": two(left_hi, my_hi, HI_WN),
        "wz": two(left_hi, my_hi, HI_WZ),
        "r": two(left_hi, my_hi, HI_R, 1),
    }
    b = {
        "e1t": two(my_lo, right_lo, LO_E1T),
        "e1z": two(my_lo, right_lo, LO_E1Z),
        "e2t": two(my_lo, right_lo, LO_E2T),
        "e2z": two(my_lo, right_lo, LO_E2Z),
        "f0t": two(my_lo, right_lo, LO_F0T),
        "f0z": two(my_lo, right_lo, LO_F0Z),
        "f1t": two(my_lo, right_lo, LO_F1T),
        "f1n": two(my_lo, right_lo, LO_F1N),
        "f1z": two(my_lo, right_lo, LO_F1Z),
        "w1t": two(my_lo, right_lo, LO_W1T),
        "w1z": two(my_lo, right_lo, LO_W1Z),
        "r0": two(my_lo, right_lo, LO_R0, 1),
        "r1": two(my_lo, right_lo, LO_R1, 1),
    }
    return a, b


def even(axis):
    return lax.axis_index(axis) % 2 == 0


def solve_kernel(e_ref, h_ref, f_ref, lab_ref, den_ref, eps_ref,
                 a_ref, b_ref, lo_ref, hi_ref, pack_ref, grad_ref, e2_ref, h2_ref):
    n, m = lab_ref.shape
    nz = e_ref.shape[1]
    labels = lab_ref[...]
    eps = jnp.full((n, m), eps_ref[0], F32)
    for k in range(1, NMAT):
        eps = jnp.where(labels == k, eps_ref[k], eps)
    ratio = courant / (eps + den_ref[...])
    e0 = [[e_ref[c, z] for z in range(nz)] for c in range(3)]
    h0 = [[h_ref[c, z] for z in range(nz)] for c in range(3)]
    fwd = [[[f_ref[s, c, z] for z in range(nz)] for c in range(3)] for s in range(STEPS)]
    e1, h1, e2, h2, grad = local_solve(e0, h0, fwd, ratio)
    for c in range(3):
        for z in range(nz):
            e2_ref[c, z] = e2[c][z]
            h2_ref[c, z] = h2[c][z]
    grad_ref[...] = grad

    def lists(t, nrm):
        zs = range(nz)
        lo = (
            [(e1[c][z], 0) for c in (t, 2) for z in zs]
            + [(e2[c][z], 0) for c in (t, 2) for z in zs]
            + [(fwd[0][c][z], 0) for c in (t, 2) for z in zs]
            + [(fwd[1][c][z], 0) for c in (t, nrm, 2) for z in zs]
            + [((ratio, fwd[1][c][z]), 1) for c in (t, 2) for z in zs]
            + [(ratio, 0), (ratio, 1)]
        )
        hi = (
            [(h0[c][z], -1) for c in (t, 2) for z in zs]
            + [(h1[c][z], -1) for c in (t, 2) for z in zs]
            + [((ratio, fwd[1][c][z]), -1) for c in (t, nrm, 2) for z in zs]
            + [(ratio, -1)]
        )
        return lo, hi

    def line(item, at):
        if isinstance(item, tuple):
            return line(item[0], at) * line(item[1], at)
        at = at % n
        return item[at : at + 1]

    lo, hi = lists(1, 0)
    lo_ref[0:FILT] = grad[0:FILT]
    for k, (item, at) in enumerate(lo):
        lo_ref[FILT + k : FILT + k + 1] = line(item, at)
    hi_ref[0:FILT] = grad[n - FILT : n]
    for k, (item, at) in enumerate(hi):
        hi_ref[FILT + k : FILT + k + 1] = line(item, at)
    hi_ref[HI_ROWS - 1 : HI_ROWS] = jnp.zeros((1, m), F32)

    lane = iota((n, 128), 1)
    lo, hi = lists(0, 1)
    first, last = grad[:, 0:128], grad[:, m - 128 : m]
    pack = jnp.where(lane < FILT, first, 0.0)
    moved = pltpu.roll(last, LANE_HI + FILT, 1)
    pack = jnp.where((lane >= LANE_HI) & (lane < LANE_HI + FILT), moved, pack)

    def tile(item, at):
        if isinstance(item, tuple):
            return tile(item[0], at) * tile(item[1], at)
        return item[:, m - 128 : m] if at < 0 else item[:, 0:128]

    for group, start in ((lo, FILT), (hi, LANE_HI + FILT)):
        for k, (item, at) in enumerate(group):
            pack = jnp.where(lane == start + k, pltpu.roll(tile(item, at), (start + k - at) % 128, 1), pack)
    pack_ref[...] = pack

    def corner(rows):
        low = jnp.concatenate([rows[0:8], rows[8:16]], axis=1)
        high = jnp.concatenate([rows[16:24], jnp.zeros((8, m - 128), F32)], axis=1)
        return jnp.concatenate([low, high], axis=0)

    lo_all = jnp.concatenate([lo_ref[...], corner(pack[0:EXT])], axis=0)
    hi_all = jnp.concatenate([hi_ref[...], jnp.zeros((LO_ROWS - HI_ROWS, m), F32), corner(pack[n - EXT : n])], axis=0)
    first_even = even("gx")
    a_ref[...] = jnp.where(first_even, hi_all, lo_all)
    b_ref[...] = jnp.where(first_even, lo_all, hi_all)


def x_kernel(ra_ref, rb_ref, lo_ref, hi_ref, pack_ref, grad_ref,
             a_ref, b_ref, ylo_ref, yhi_ref, ext_ref, dr_ref):
    n, m = grad_ref.shape
    first_even = even("gx")
    right = jnp.where(first_even, ra_ref[...], rb_ref[...])
    left = jnp.where(first_even, rb_ref[...], ra_ref[...])
    a, b = seam_inputs(left, hi_ref[...], lo_ref[...], right)
    col = iota((8, m), 1)
    d = seam(
        -1.0, a, b,
        lambda f: jnp.where(col == m - 1, 0.0, pltpu.roll(f, m - 1, 1)),
        lambda f: jnp.where(col == 0, 0.0, pltpu.roll(f, 1, 1)),
    )
    for f, field in enumerate(("e", "h")):
        for c, name in enumerate(("n", "t", "z")):
            before, end, begin, after = d[field][name]
            for z in range(2):
                p = 4 * (6 * f + 2 * c + z)
                dr_ref[p : p + 1] = before[2 + z : 3 + z]
                dr_ref[p + 1 : p + 2] = end[2 + z : 3 + z]
                dr_ref[p + 2 : p + 3] = begin[z : z + 1]
                dr_ref[p + 3 : p + 4] = after[z : z + 1]
    gb0, gb1, ga = d["gb0"], d["gb1"], d["ga"]
    top = iota((8, m), 0)
    ext_ref[0:n] = grad_ref[...]
    ext_ref[0:8] = grad_ref[0:8] + jnp.where(top == 0, gb0[0:1], jnp.where(top == 1, gb1[0:1], 0.0))
    ext_ref[n - 8 : n] = grad_ref[n - 8 : n] + jnp.where(top == 7, ga[2:3], 0.0)
    ext_ref[n : n + 8] = right[0:8] + jnp.where(top == 0, gb0[2:3], jnp.where(top == 1, gb1[2:3], 0.0))
    ext_ref[n + 8 : n + 16] = right[8:16]
    ext_ref[n + 16 : 2 * n - 16] = jnp.zeros((n - 32, m), F32)
    ext_ref[2 * n - 16 : 2 * n - 8] = left[0:8]
    ext_ref[2 * n - 8 : 2 * n] = left[8:16] + jnp.where(top == 7, ga[0:1], 0.0)

    lane = iota((1, 128), 1)

    def strips(g):
        out = jnp.where(lane < FILT, g[:, 0:128], 0.0)
        moved = pltpu.roll(g[:, m - 128 : m], LANE_HI + FILT, 1)
        return jnp.where((lane >= LANE_HI) & (lane < LANE_HI + FILT), moved, out)

    def put(row_vec, at, value, seam_row, c):
        for z in range(2):
            one = value[seam_row + z : seam_row + z + 1, c : c + 1]
            row_vec = jnp.where(lane == at + z, one, row_vec)
        return row_vec

    hi = LANE_HI
    row0 = strips(gb0[0:1])
    row0 = put(row0, LO_E1Z, d["b_e1z"], 0, 0)
    row0 = put(row0, LO_E2T, d["e"]["n"][2], 0, 0)
    row0 = put(row0, LO_E2Z, d["e"]["z"][2], 0, 0)
    row0 = put(row0, hi + HI_H1T, d["b_h1n"], 0, m - 1)
    row0 = put(row0, hi + HI_H1Z, d["b_h1z"], 0, m - 1)
    row1 = strips(gb1[0:1])
    row1 = put(row1, LO_E2Z, d["e"]["z"][3], 0, 0)
    end = strips(ga[2:3])
    end = put(end, LO_E2T, d["e"]["n"][1], 2, 0)
    end = put(end, LO_E2Z, d["e"]["z"][1], 2, 0)
    end = put(end, hi + HI_H1Z, d["a_h1z"], 2, m - 1)
    out0 = strips(gb0[2:3])
    out0 = put(out0, LO_E1Z, d["b_e1z"], 2, 0)
    out0 = put(out0, hi + HI_H1T, d["b_h1n"], 2, m - 1)
    out0 = put(out0, hi + HI_H1Z, d["b_h1z"], 2, m - 1)
    out1 = strips(gb1[2:3])
    before = strips(ga[0:1])
    before = put(before, hi + HI_H1Z, d["a_h1z"], 0, m - 1)

    sub = iota((8, 128), 0)

    def corner(message):
        return [message[40:48, 0:128], message[40:48, 128:256], message[48:56, 0:128]]

    above, below = corner(right), corner(left)
    above[0] = above[0] + jnp.where(sub == 0, out0, jnp.where(sub == 1, out1, 0.0))
    below[2] = below[2] + jnp.where(sub == 7, before, 0.0)
    head = pack_ref[0:8] + jnp.where(sub == 0, row0, jnp.where(sub == 1, row1, 0.0))
    tail = pack_ref[n - 8 : n] + jnp.where(sub == 7, end, 0.0)
    inner = jnp.concatenate([head, pack_ref[8 : n - 8], tail], axis=0)
    outer = jnp.concatenate(above + [jnp.zeros((n - 2 * EXT, 128), F32)] + below, axis=0)
    packed = jnp.concatenate([inner.T, outer.T], axis=1)
    lo, hi_part = packed[0:LO_ROWS], packed[LANE_HI : LANE_HI + LO_ROWS]
    ylo_ref[...] = lo
    yhi_ref[...] = hi_part
    y_even = even("gy")
    a_ref[...] = jnp.where(y_even, hi_part, lo)
    b_ref[...] = jnp.where(y_even, lo, hi_part)


def inner_kernel(ext_ref, out_ref):
    rows, m = ext_ref.shape
    n = out_ref.shape[0]
    d = iota((n, rows), 1) - iota((n, rows), 0)
    d = jnp.where(d > rows // 2, d - rows, jnp.where(d < -(rows // 2), d + rows, d))
    along = jnp.dot(tap(d), ext_ref[...], precision=HIGHEST, preferred_element_type=F32)
    e = iota((m, m), 0) - iota((m, m), 1)
    out_ref[...] = jnp.dot(along, tap(e), precision=HIGHEST, preferred_element_type=F32)


def y_kernel(ra_ref, rb_ref, lo_ref, hi_ref, dr_ref, e2_ref, h2_ref, inner_ref,
             e_ref, h_ref, out_ref, gt_ref, dc_ref):
    n, m = inner_ref.shape
    y_even = even("gy")
    right = jnp.where(y_even, ra_ref[...], rb_ref[...])
    left = jnp.where(y_even, rb_ref[...], ra_ref[...])
    rows = right.shape[1]
    a, b = seam_inputs(left, hi_ref[...], lo_ref[...], right)
    d = seam(1.0, a, b, lambda f: pltpu.roll(f, rows - 1, 1), lambda f: pltpu.roll(f, 1, 1))

    gb0, gb1, ga = d["gb0"], d["gb1"], d["ga"]
    top = iota((8, rows), 0)
    gt_ref[0:8] = right[0:8] + jnp.where(top == 0, gb0[2:3], jnp.where(top == 1, gb1[2:3], 0.0))
    gt_ref[8:16] = right[8:16]
    gt_ref[16:24] = left[0:8]
    gt_ref[24:32] = left[8:16] + jnp.where(top == 7, ga[0:1], 0.0)
    gt_ref[32:40] = jnp.where(top == 0, gb0[0:1], jnp.where(top == 1, gb1[0:1], jnp.where(top == 2, ga[2:3], 0.0)))

    for f, field in enumerate(("e", "h")):
        for c, name in enumerate(("t", "n", "z")):
            before, end, begin, after = d[field][name]
            for z in range(2):
                p = 4 * (6 * f + 2 * c + z)
                dc_ref[p : p + 1] = before[2 + z : 3 + z, 0:n]
                dc_ref[p + 1 : p + 2] = end[2 + z : 3 + z, 0:n]
                dc_ref[p + 2 : p + 3] = begin[z : z + 1, 0:n]
                dc_ref[p + 3 : p + 4] = after[z : z + 1, 0:n]
    dc_ref[48:128] = jnp.zeros((80, n), F32)
    columns = dc_ref[...].T
    lane = iota((n, 128), 1)
    sub = iota((8, m), 0)
    for f, (src, dst) in enumerate(((e2_ref, e_ref), (h2_ref, h_ref))):
        for c in range(3):
            for z in range(2):
                p = 4 * (6 * f + 2 * c + z)
                moved = pltpu.roll(columns, (126 - p) % 128, 1)
                low = src[c, z, :, 0:128] + jnp.where(lane < 2, moved, 0.0)
                high = src[c, z, :, m - 128 : m] + jnp.where(lane >= 126, moved, 0.0)
                dst[c, z, :, 0:128] = low
                dst[c, z, :, m - 128 : m] = high
                dst[c, z, 0:8] += jnp.where(sub == 0, dr_ref[p + 2 : p + 3], jnp.where(sub == 1, dr_ref[p + 3 : p + 4], 0.0))
                dst[c, z, n - 8 : n] += jnp.where(sub == 6, dr_ref[p : p + 1], jnp.where(sub == 7, dr_ref[p + 1 : p + 2], 0.0))

    d = iota((rows, n), 0) - iota((rows, n), 1)
    d = jnp.where(d > rows // 2, d - rows, jnp.where(d < -(rows // 2), d + rows, d))
    along = jnp.dot(gt_ref[...], tap(d), precision=HIGHEST, preferred_element_type=F32)
    k = iota((40, m), 0)
    place = jnp.where(k < 16, m + k, jnp.where(k < 32, k - 32, jnp.where(k < 34, k - 32, m - 1)))
    spread = jnp.where(k < 35, tap(place - iota((40, m), 1)), 0.0)
    extra = lax.dot_general(along, spread, (((0,), (0,)), ((), ())), precision=HIGHEST, preferred_element_type=F32)
    out_ref[...] = inner_ref[...] + extra


def swap_pairs(count, which):
    if which == 0:
        return [(i, i ^ 1) for i in range(count)]
    return [(i, (i - 1) % count if i % 2 == 0 else (i + 1) % count) for i in range(count)]


def call(kernel, shapes, ins, scratch=()):
    vmem = pl.BlockSpec(memory_space=pltpu.VMEM)
    return pl.pallas_call(
        kernel,
        out_shape=[jax.ShapeDtypeStruct(s, F32) for s in shapes],
        in_specs=[pl.BlockSpec(memory_space=pltpu.SMEM) if x.shape == (NMAT,) else vmem for x in ins],
        out_specs=[vmem] * len(shapes),
        scratch_shapes=[pltpu.VMEM(s, F32) for s in scratch],
        compiler_params=pltpu.CompilerParams(vmem_limit_bytes=40 * 1024 * 1024),
    )(*ins)


def body(adj_e, adj_h, fwd_e, labels, eps_table, density):
    n, m = labels.shape
    block = adj_e.shape
    message = (LO_ROWS + 16, m)
    xa, xb, lo, hi, pack, grad, e2, h2 = call(
        solve_kernel,
        [message, message, (LO_ROWS, m), (HI_ROWS, m), (n, 128), (n, m), block, block],
        [adj_e, adj_h, fwd_e, labels, density, eps_table],
    )
    gx, gy = lax.axis_size("gx"), lax.axis_size("gy")
    got_a = lax.ppermute(xa, "gx", swap_pairs(gx, 0))
    got_b = lax.ppermute(xb, "gx", swap_pairs(gx, 1))
    column = (LO_ROWS, 2 * n)
    ya, yb, ylo, yhi, ext, dr = call(
        x_kernel,
        [column, column, column, column, (2 * n, m), (48, m)],
        [got_a, got_b, lo, hi, pack, grad],
    )
    got_a = lax.ppermute(ya, "gy", swap_pairs(gy, 0))
    got_b = lax.ppermute(yb, "gy", swap_pairs(gy, 1))
    (inner,) = call(inner_kernel, [(n, m)], [ext])
    return tuple(
        call(
            y_kernel,
            [block, block, (n, m)],
            [got_a, got_b, ylo, yhi, dr, e2, h2, inner],
            [(40, 2 * n), (128, n)],
        )
    )


def solution(mesh):
    return jax.shard_map(
        body,
        mesh=mesh,
        in_specs=(
            P("design", None, "gx", "gy"),
            P("design", None, "gx", "gy"),
            P("design", None, None, "gx", "gy"),
            P(("design", "gx"), "gy"),
            P(),
            P(("design", "gx"), "gy"),
        ),
        out_specs=(
            P("design", None, "gx", "gy"),
            P("design", None, "gx", "gy"),
            P(("design", "gx"), "gy"),
        ),
        check_vma=False,
    )
```

```python
import math

import jax
import jax.numpy as jnp
from jax import lax
from jax.experimental import pallas as pl
from jax.experimental.pallas import tpu as pltpu
from jax.sharding import PartitionSpec as P

STEPS = 2
NMAT = 8
FILT = 16

courant = 0.5
spread_ratio = 0.6

F32 = jnp.float32
HIGHEST = lax.Precision.HIGHEST

LO_G, LO_E1T, LO_E1Z, LO_E2T, LO_E2Z = 0, 16, 18, 20, 22
LO_F0T, LO_F0Z, LO_F1T, LO_F1N, LO_F1Z = 24, 26, 28, 30, 32
LO_W1T, LO_W1Z, LO_R0, LO_R1, LO_ROWS = 34, 36, 38, 39, 40
HI_G, HI_H0T, HI_H0Z, HI_H1T, HI_H1Z = 0, 16, 18, 20, 22
HI_WT, HI_WN, HI_WZ, HI_R, HI_ROWS = 24, 26, 28, 30, 32
LANE_HI = 64
EXT = 24


def tap(distance):
    spread = spread_ratio * FILT
    norm = math.sqrt(sum(math.exp(-d * d / (spread * spread)) for d in range(-FILT, FILT + 1)))
    far = distance.astype(F32)
    value = jnp.exp(-far * far / (2.0 * spread * spread)) / norm
    return jnp.where(jnp.abs(distance) <= FILT, value, F32(0.0))


def iota(shape, dim):
    return lax.broadcasted_iota(jnp.int32, shape, dim)


def updates(n, m, nz):
    row, col = iota((n, m), 0), iota((n, m), 1)

    def lx(f):
        return jnp.where(row == 0, 0.0, pltpu.roll(f, 1, 0))

    def ux(f):
        return jnp.where(row == n - 1, 0.0, pltpu.roll(f, n - 1, 0))

    def ly(f):
        return jnp.where(col == 0, 0.0, pltpu.roll(f, 1, 1))

    def uy(f):
        return jnp.where(col == m - 1, 0.0, pltpu.roll(f, m - 1, 1))

    def electric(e, h, ratio):
        out = [[None] * nz for _ in range(3)]
        for z in range(nz):
            hx, hy, hz = h[0][z], h[1][z], h[2][z]
            dzx = hx - h[0][z - 1] if z > 0 else hx
            dzy = hy - h[1][z - 1] if z > 0 else hy
            out[0][z] = e[0][z] - ratio * ((hz - ly(hz)) - dzy)
            out[1][z] = e[1][z] - ratio * (dzx - (hz - lx(hz)))
            out[2][z] = e[2][z] - ratio * ((hy - lx(hy)) - (hx - ly(hx)))
        return out

    def magnetic(e, h):
        out = [[None] * nz for _ in range(3)]
        for z in range(nz):
            ex, ey, ez = e[0][z], e[1][z], e[2][z]
            dzx = e[0][z + 1] - ex if z < nz - 1 else -ex
            dzy = e[1][z + 1] - ey if z < nz - 1 else -ey
            out[0][z] = h[0][z] + courant * ((uy(ez) - ez) - dzy)
            out[1][z] = h[1][z] + courant * (dzx - (ux(ez) - ez))
            out[2][z] = h[2][z] + courant * ((ux(ey) - ey) - (uy(ex) - ex))
        return out

    return electric, magnetic


def product(e, f):
    total = None
    for c in range(3):
        for z in range(len(e[c])):
            term = e[c][z] * f[c][z]
            total = term if total is None else total + term
    return total


def local_solve(e0, h0, saved, ratio):
    electric, magnetic = updates(*ratio.shape, len(e0[0]))
    e1 = electric(e0, h0, ratio)
    h1 = magnetic(e1, h0)
    fwd = [saved(0)]
    grad = product(e1, fwd[0])
    e2 = electric(e1, h1, ratio)
    fwd.append(saved(1))
    grad = grad + product(e2, fwd[1])
    return e1, h1, e2, grad, fwd


def seam(sgn, a, b, up, down):
    odd = iota(a["h0t"].shape, 0) % 2 == 1
    half = sgn * courant

    def uz(f):
        return jnp.where(odd, 0.0, pltpu.roll(f, 7, 0))

    def lz(f):
        return jnp.where(odd, pltpu.roll(f, 1, 0), 0.0)

    rb, rb1, ra = sgn * b["r0"], sgn * b["r1"], sgn * a["r"]
    d = {}
    e1t = rb * a["h0z"]
    e1z = -rb * a["h0t"]
    e1t_b = b["e1t"] + e1t
    e1z_b = b["e1z"] + e1z
    ah1t = half * e1z_b
    ah1z = -half * e1t_b
    h1t_a = a["h1t"] + ah1t
    h1z_a = a["h1z"] + ah1z
    bh1t = -half * e1z
    bh1n = half * ((uz(e1t) - e1t) - (up(e1z) - e1z))
    bh1z = half * e1t
    e2t = e1t - rb * ((bh1z - h1z_a) - (bh1n - lz(bh1n)))
    e2n = -rb * ((bh1t - lz(bh1t)) - (bh1z - down(bh1z)))
    e2z = e1z - rb * ((bh1n - down(bh1n)) - (bh1t - h1t_a))
    f2t = rb1 * bh1z
    f2z = -rb1 * bh1t
    at = ah1z
    an = (ah1t - lz(ah1t)) - (ah1z - down(ah1z))
    az = -ah1t
    g2t, g2n, g2z = -ra * at, -ra * an, -ra * az
    gb0 = b["f0t"] * e1t + b["f0z"] * e1z + b["f1t"] * e2t + b["f1n"] * e2n + b["f1z"] * e2z
    gb1 = sgn * (b["w1t"] * bh1z - b["w1z"] * bh1t)
    ga = -sgn * (a["wt"] * at + a["wn"] * an + a["wz"] * az)
    e2t_b = b["e2t"] + e2t
    e2z_b = b["e2z"] + e2z
    d["b_e1z"], d["b_h1n"], d["b_h1z"], d["a_h1z"] = e1z, bh1n, bh1z, ah1z
    none = jnp.zeros_like(e1t)
    d["e"] = {"t": (none, g2t, e2t, f2t), "n": (none, g2n, e2n, none), "z": (none, g2z, e2z, f2z)}
    d["h"] = {
        "t": (
            half * g2z,
            ah1t + half * ((e2z_b - g2z) - (uz(g2n) - g2n)),
            bh1t + half * ((f2z - e2z) - (uz(e2n) - e2n)),
            -half * f2z,
        ),
        "n": (
            none,
            half * ((uz(g2t) - g2t) - (up(g2z) - g2z)),
            bh1n + half * ((uz(e2t) - e2t) - (up(e2z) - e2z)),
            half * ((uz(f2t) - f2t) - (up(f2z) - f2z)),
        ),
        "z": (
            -half * g2t,
            ah1z + half * ((up(g2n) - g2n) - (e2t_b - g2t)),
            bh1z + half * ((up(e2n) - e2n) - (f2t - e2t)),
            half * f2t,
        ),
    }
    d["gb0"], d["gb1"], d["ga"] = (g + pltpu.roll(g, 7, 0) for g in (gb0, gb1, ga))
    return d


def two(first, second, at, count=2):
    if count == 1:
        one, other = first[at : at + 1], second[at : at + 1]
        parts = [one, one, other, other]
    else:
        parts = [first[at : at + 2], second[at : at + 2]]
    parts.append(jnp.zeros((4, first.shape[1]), F32))
    return jnp.concatenate(parts, axis=0)


def seam_inputs(left_hi, my_hi, my_lo, right_lo):
    a = {
        "h0t": two(left_hi, my_hi, HI_H0T),
        "h0z": two(left_hi, my_hi, HI_H0Z),
        "h1t": two(left_hi, my_hi, HI_H1T),
        "h1z": two(left_hi, my_hi, HI_H1Z),
        "wt": two(left_hi, my_hi, HI_WT),
        "wn": two(left_hi, my_hi, HI_WN),
        "wz": two(left_hi, my_hi, HI_WZ),
        "r": two(left_hi, my_hi, HI_R, 1),
    }
    b = {
        "e1t": two(my_lo, right_lo, LO_E1T),
        "e1z": two(my_lo, right_lo, LO_E1Z),
        "e2t": two(my_lo, right_lo, LO_E2T),
        "e2z": two(my_lo, right_lo, LO_E2Z),
        "f0t": two(my_lo, right_lo, LO_F0T),
        "f0z": two(my_lo, right_lo, LO_F0Z),
        "f1t": two(my_lo, right_lo, LO_F1T),
        "f1n": two(my_lo, right_lo, LO_F1N),
        "f1z": two(my_lo, right_lo, LO_F1Z),
        "w1t": two(my_lo, right_lo, LO_W1T),
        "w1z": two(my_lo, right_lo, LO_W1Z),
        "r0": two(my_lo, right_lo, LO_R0, 1),
        "r1": two(my_lo, right_lo, LO_R1, 1),
    }
    return a, b


def even(axis):
    return lax.axis_index(axis) % 2 == 0


def ratio_of(labels, density, eps_ref):
    eps = jnp.full(labels.shape, eps_ref[0], F32)
    for k in range(1, NMAT):
        eps = jnp.where(labels == k, eps_ref[k], eps)
    return courant / (eps + density)


def planes(ref, *lead):
    return [[ref[(*lead, c, z)] for z in range(ref.shape[-3])] for c in range(3)]


def edge_lists(t, nrm, e1, h0, h1, e2, fwd, ratio):
    zs = range(len(e1[0]))
    lo = (
        [(e1[c][z], 0) for c in (t, 2) for z in zs]
        + [(e2[c][z], 0) for c in (t, 2) for z in zs]
        + [(fwd[0][c][z], 0) for c in (t, 2) for z in zs]
        + [(fwd[1][c][z], 0) for c in (t, nrm, 2) for z in zs]
        + [((ratio, fwd[1][c][z]), 1) for c in (t, 2) for z in zs]
        + [(ratio, 0), (ratio, 1)]
    )
    hi = (
        [(h0[c][z], -1) for c in (t, 2) for z in zs]
        + [(h1[c][z], -1) for c in (t, 2) for z in zs]
        + [((ratio, fwd[1][c][z]), -1) for c in (t, nrm, 2) for z in zs]
        + [(ratio, -1)]
    )
    return lo, hi


def pack_columns(grad, lo, hi):
    n, m = grad.shape
    lane = iota((n, 128), 1)
    first, last = grad[:, 0:128], grad[:, m - 128 : m]
    pack = jnp.where(lane < FILT, first, 0.0)
    moved = pltpu.roll(last, LANE_HI + FILT, 1)
    pack = jnp.where((lane >= LANE_HI) & (lane < LANE_HI + FILT), moved, pack)

    def tile(item, at):
        if isinstance(item, tuple):
            return tile(item[0], at) * tile(item[1], at)
        return item[:, m - 128 : m] if at < 0 else item[:, 0:128]

    for group, start in ((lo, FILT), (hi, LANE_HI + FILT)):
        for k, (item, at) in enumerate(group):
            pack = jnp.where(lane == start + k, pltpu.roll(tile(item, at), (start + k - at) % 128, 1), pack)
    return pack


def edge_kernel(e_hbm, h_hbm, f_hbm, lab_hbm, den_hbm, eps_hbm,
                a_ref, b_ref, lo_ref, hi_ref,
                e_ref, h_ref, f_ref, lab_ref, den_ref, tab_ref, sems):
    n, m = lab_hbm.shape
    copies = []

    def fetch(src, dst, lead):
        for at, start in ((0, 0), (EXT, n - EXT)):
            index = (*lead, pl.ds(start, EXT))
            copy = pltpu.make_async_copy(src.at[index], dst.at[(*lead, pl.ds(at, EXT))], sems.at[len(copies) - 1])
            copy.start()
            copies.append(copy)

    every = slice(None)
    table = pltpu.make_async_copy(eps_hbm, tab_ref, sems.at[12])
    table.start()
    copies.append(table)
    fetch(lab_hbm, lab_ref, ())
    fetch(den_hbm, den_ref, ())
    fetch(h_hbm, h_ref, (every, every))
    fetch(e_hbm, e_ref, (every, every))
    for step in range(STEPS):
        fetch(f_hbm, f_ref, (step, every, every))
    for copy in copies[:9]:
        copy.wait()
    ratio = ratio_of(lab_ref[...], den_ref[...], tab_ref)
    h0 = planes(h_ref)

    def saved(step):
        for copy in copies[9 + 2 * step : 11 + 2 * step]:
            copy.wait()
        return planes(f_ref, step)

    e1, h1, e2, grad, fwd = local_solve(planes(e_ref), h0, saved, ratio)
    rows = 2 * EXT

    def line(item, at):
        if isinstance(item, tuple):
            return line(item[0], at) * line(item[1], at)
        at = at % rows
        return item[at : at + 1]

    lo, hi = edge_lists(1, 0, e1, h0, h1, e2, fwd, ratio)
    lo_ref[0:FILT] = grad[0:FILT]
    for k, (item, at) in enumerate(lo):
        lo_ref[FILT + k : FILT + k + 1] = line(item, at)
    hi_ref[0:FILT] = grad[rows - FILT : rows]
    for k, (item, at) in enumerate(hi):
        hi_ref[FILT + k : FILT + k + 1] = line(item, at)
    hi_ref[HI_ROWS - 1 : HI_ROWS] = jnp.zeros((1, m), F32)
    pack = pack_columns(grad, *edge_lists(0, 1, e1, h0, h1, e2, fwd, ratio))

    def corner(part):
        low = jnp.concatenate([part[0:8], part[8:16]], axis=1)
        high = jnp.concatenate([part[16:24], jnp.zeros((8, m - 128), F32)], axis=1)
        return jnp.concatenate([low, high], axis=0)

    lo_all = jnp.concatenate([lo_ref[...], corner(pack[0:EXT])], axis=0)
    hi_all = jnp.concatenate([hi_ref[...], jnp.zeros((LO_ROWS - HI_ROWS, m), F32), corner(pack[EXT:rows])], axis=0)
    first_even = even("gx")
    a_ref[...] = jnp.where(first_even, hi_all, lo_all)
    b_ref[...] = jnp.where(first_even, lo_all, hi_all)


def solve_kernel(e_ref, h_ref, f_ref, lab_ref, den_ref, eps_ref, pack_ref, grad_ref, e2_ref, h1_ref):
    ratio = ratio_of(lab_ref[...], den_ref[...], eps_ref)
    h0 = planes(h_ref)
    e1, h1, e2, grad, fwd = local_solve(planes(e_ref), h0, lambda step: planes(f_ref, step), ratio)
    for c in range(3):
        for z in range(e_ref.shape[1]):
            e2_ref[c, z] = e2[c][z]
            h1_ref[c, z] = h1[c][z]
    grad_ref[...] = grad
    pack_ref[...] = pack_columns(grad, *edge_lists(0, 1, e1, h0, h1, e2, fwd, ratio))


def x_kernel(ra_ref, rb_ref, lo_ref, hi_ref, pack_ref, grad_ref,
             a_ref, b_ref, ylo_ref, yhi_ref, ext_ref, dr_ref):
    n, m = grad_ref.shape
    first_even = even("gx")
    right = jnp.where(first_even, ra_ref[...], rb_ref[...])
    left = jnp.where(first_even, rb_ref[...], ra_ref[...])
    a, b = seam_inputs(left, hi_ref[...], lo_ref[...], right)
    col = iota((8, m), 1)
    d = seam(
        -1.0, a, b,
        lambda f: jnp.where(col == m - 1, 0.0, pltpu.roll(f, m - 1, 1)),
        lambda f: jnp.where(col == 0, 0.0, pltpu.roll(f, 1, 1)),
    )
    for f, field in enumerate(("e", "h")):
        for c, name in enumerate(("n", "t", "z")):
            before, end, begin, after = d[field][name]
            for z in range(2):
                p = 4 * (6 * f + 2 * c + z)
                dr_ref[p : p + 1] = before[2 + z : 3 + z]
                dr_ref[p + 1 : p + 2] = end[2 + z : 3 + z]
                dr_ref[p + 2 : p + 3] = begin[z : z + 1]
                dr_ref[p + 3 : p + 4] = after[z : z + 1]
    gb0, gb1, ga = d["gb0"], d["gb1"], d["ga"]
    top = iota((8, m), 0)
    ext_ref[0:n] = grad_ref[...]
    ext_ref[0:8] = grad_ref[0:8] + jnp.where(top == 0, gb0[0:1], jnp.where(top == 1, gb1[0:1], 0.0))
    ext_ref[n - 8 : n] = grad_ref[n - 8 : n] + jnp.where(top == 7, ga[2:3], 0.0)
    ext_ref[n : n + 8] = right[0:8] + jnp.where(top == 0, gb0[2:3], jnp.where(top == 1, gb1[2:3], 0.0))
    ext_ref[n + 8 : n + 16] = right[8:16]
    ext_ref[n + 16 : 2 * n - 16] = jnp.zeros((n - 32, m), F32)
    ext_ref[2 * n - 16 : 2 * n - 8] = left[0:8]
    ext_ref[2 * n - 8 : 2 * n] = left[8:16] + jnp.where(top == 7, ga[0:1], 0.0)

    lane = iota((1, 128), 1)

    def strips(g):
        out = jnp.where(lane < FILT, g[:, 0:128], 0.0)
        moved = pltpu.roll(g[:, m - 128 : m], LANE_HI + FILT, 1)
        return jnp.where((lane >= LANE_HI) & (lane < LANE_HI + FILT), moved, out)

    def put(row_vec, at, value, seam_row, c):
        for z in range(2):
            one = value[seam_row + z : seam_row + z + 1, c : c + 1]
            row_vec = jnp.where(lane == at + z, one, row_vec)
        return row_vec

    hi = LANE_HI
    row0 = strips(gb0[0:1])
    row0 = put(row0, LO_E1Z, d["b_e1z"], 0, 0)
    row0 = put(row0, LO_E2T, d["e"]["n"][2], 0, 0)
    row0 = put(row0, LO_E2Z, d["e"]["z"][2], 0, 0)
    row0 = put(row0, hi + HI_H1T, d["b_h1n"], 0, m - 1)
    row0 = put(row0, hi + HI_H1Z, d["b_h1z"], 0, m - 1)
    row1 = strips(gb1[0:1])
    row1 = put(row1, LO_E2Z, d["e"]["z"][3], 0, 0)
    end = strips(ga[2:3])
    end = put(end, LO_E2T, d["e"]["n"][1], 2, 0)
    end = put(end, LO_E2Z, d["e"]["z"][1], 2, 0)
    end = put(end, hi + HI_H1Z, d["a_h1z"], 2, m - 1)
    out0 = strips(gb0[2:3])
    out0 = put(out0, LO_E1Z, d["b_e1z"], 2, 0)
    out0 = put(out0, hi + HI_H1T, d["b_h1n"], 2, m - 1)
    out0 = put(out0, hi + HI_H1Z, d["b_h1z"], 2, m - 1)
    out1 = strips(gb1[2:3])
    before = strips(ga[0:1])
    before = put(before, hi + HI_H1Z, d["a_h1z"], 0, m - 1)

    sub = iota((8, 128), 0)

    def corner(message):
        return [message[40:48, 0:128], message[40:48, 128:256], message[48:56, 0:128]]

    above, below = corner(right), corner(left)
    above[0] = above[0] + jnp.where(sub == 0, out0, jnp.where(sub == 1, out1, 0.0))
    below[2] = below[2] + jnp.where(sub == 7, before, 0.0)
    head = pack_ref[0:8] + jnp.where(sub == 0, row0, jnp.where(sub == 1, row1, 0.0))
    tail = pack_ref[n - 8 : n] + jnp.where(sub == 7, end, 0.0)
    inner = jnp.concatenate([head, pack_ref[8 : n - 8], tail], axis=0)
    outer = jnp.concatenate(above + [jnp.zeros((n - 2 * EXT, 128), F32)] + below, axis=0)
    packed = jnp.concatenate([inner.T, outer.T], axis=1)
    lo, hi_part = packed[0:LO_ROWS], packed[LANE_HI : LANE_HI + LO_ROWS]
    ylo_ref[...] = lo
    yhi_ref[...] = hi_part
    y_even = even("gy")
    a_ref[...] = jnp.where(y_even, hi_part, lo)
    b_ref[...] = jnp.where(y_even, lo, hi_part)


def inner_kernel(ext_ref, e2_ref, h1_ref, out_ref, h2_ref):
    nz = e2_ref.shape[1]
    _, magnetic = updates(*out_ref.shape, nz)
    h2 = magnetic(planes(e2_ref), planes(h1_ref))
    for c in range(3):
        for z in range(nz):
            h2_ref[c, z] = h2[c][z]
    rows, m = ext_ref.shape
    n = out_ref.shape[0]
    d = iota((n, rows), 1) - iota((n, rows), 0)
    d = jnp.where(d > rows // 2, d - rows, jnp.where(d < -(rows // 2), d + rows, d))
    along = jnp.dot(tap(d), ext_ref[...], precision=HIGHEST, preferred_element_type=F32)
    e = iota((m, m), 0) - iota((m, m), 1)
    out_ref[...] = jnp.dot(along, tap(e), precision=HIGHEST, preferred_element_type=F32)


def y_kernel(ra_ref, rb_ref, lo_ref, hi_ref, dr_ref, e2_ref, h2_ref, inner_ref,
             e_ref, h_ref, out_ref, gt_ref, dc_ref):
    n, m = inner_ref.shape
    y_even = even("gy")
    right = jnp.where(y_even, ra_ref[...], rb_ref[...])
    left = jnp.where(y_even, rb_ref[...], ra_ref[...])
    rows = right.shape[1]
    a, b = seam_inputs(left, hi_ref[...], lo_ref[...], right)
    d = seam(1.0, a, b, lambda f: pltpu.roll(f, rows - 1, 1), lambda f: pltpu.roll(f, 1, 1))

    gb0, gb1, ga = d["gb0"], d["gb1"], d["ga"]
    top = iota((8, rows), 0)
    gt_ref[0:8] = right[0:8] + jnp.where(top == 0, gb0[2:3], jnp.where(top == 1, gb1[2:3], 0.0))
    gt_ref[8:16] = right[8:16]
    gt_ref[16:24] = left[0:8]
    gt_ref[24:32] = left[8:16] + jnp.where(top == 7, ga[0:1], 0.0)
    gt_ref[32:40] = jnp.where(top == 0, gb0[0:1], jnp.where(top == 1, gb1[0:1], jnp.where(top == 2, ga[2:3], 0.0)))

    for f, field in enumerate(("e", "h")):
        for c, name in enumerate(("t", "n", "z")):
            before, end, begin, after = d[field][name]
            for z in range(2):
                p = 4 * (6 * f + 2 * c + z)
                dc_ref[p : p + 1] = before[2 + z : 3 + z, 0:n]
                dc_ref[p + 1 : p + 2] = end[2 + z : 3 + z, 0:n]
                dc_ref[p + 2 : p + 3] = begin[z : z + 1, 0:n]
                dc_ref[p + 3 : p + 4] = after[z : z + 1, 0:n]
    dc_ref[48:128] = jnp.zeros((80, n), F32)
    columns = dc_ref[...].T
    lane = iota((n, 128), 1)
    sub = iota((8, m), 0)
    for f, (src, dst) in enumerate(((e2_ref, e_ref), (h2_ref, h_ref))):
        for c in range(3):
            for z in range(2):
                p = 4 * (6 * f + 2 * c + z)
                moved = pltpu.roll(columns, (126 - p) % 128, 1)
                low = src[c, z, :, 0:128] + jnp.where(lane < 2, moved, 0.0)
                high = src[c, z, :, m - 128 : m] + jnp.where(lane >= 126, moved, 0.0)
                dst[c, z, :, 0:128] = low
                dst[c, z, :, m - 128 : m] = high
                dst[c, z, 0:8] += jnp.where(sub == 0, dr_ref[p + 2 : p + 3], jnp.where(sub == 1, dr_ref[p + 3 : p + 4], 0.0))
                dst[c, z, n - 8 : n] += jnp.where(sub == 6, dr_ref[p : p + 1], jnp.where(sub == 7, dr_ref[p + 1 : p + 2], 0.0))

    d = iota((rows, n), 0) - iota((rows, n), 1)
    d = jnp.where(d > rows // 2, d - rows, jnp.where(d < -(rows // 2), d + rows, d))
    along = jnp.dot(gt_ref[...], tap(d), precision=HIGHEST, preferred_element_type=F32)
    k = iota((40, m), 0)
    place = jnp.where(k < 16, m + k, jnp.where(k < 32, k - 32, jnp.where(k < 34, k - 32, m - 1)))
    spread = jnp.where(k < 35, tap(place - iota((40, m), 1)), 0.0)
    extra = lax.dot_general(along, spread, (((0,), (0,)), ((), ())), precision=HIGHEST, preferred_element_type=F32)
    out_ref[...] = inner_ref[...] + extra


def swap_pairs(count, which):
    if which == 0:
        return [(i, i ^ 1) for i in range(count)]
    return [(i, (i - 1) % count if i % 2 == 0 else (i + 1) % count) for i in range(count)]


def call(kernel, shapes, ins, scratch=(), far=(), sems=0):
    vmem = pl.BlockSpec(memory_space=pltpu.VMEM)
    hbm = pl.BlockSpec(memory_space=pltpu.HBM)
    smem = pl.BlockSpec(memory_space=pltpu.SMEM)
    ins = [pltpu.with_memory_space_constraint(x, pltpu.HBM) if k in far else x for k, x in enumerate(ins)]
    scratches = [s if hasattr(s, "dtype") else pltpu.VMEM(s, F32) for s in scratch]
    if sems:
        scratches.append(pltpu.SemaphoreType.DMA((sems,)))
    return pl.pallas_call(
        kernel,
        out_shape=[jax.ShapeDtypeStruct(s, F32) for s in shapes],
        in_specs=[hbm if k in far else smem if x.shape == (NMAT,) else vmem for k, x in enumerate(ins)],
        out_specs=[vmem] * len(shapes),
        scratch_shapes=scratches,
        compiler_params=pltpu.CompilerParams(vmem_limit_bytes=24 * 1024 * 1024),
    )(*ins)


def body(adj_e, adj_h, fwd_e, labels, eps_table, density):
    n, m = labels.shape
    block = adj_e.shape
    nz = block[1]
    ins = [adj_e, adj_h, fwd_e, labels, density, eps_table]
    message = (LO_ROWS + 16, m)
    strip = (2 * EXT, m)
    xa, xb, lo, hi = call(
        edge_kernel,
        [message, message, (LO_ROWS, m), (HI_ROWS, m)],
        ins,
        [(3, nz, *strip), (3, nz, *strip), (STEPS, 3, nz, *strip), pltpu.VMEM(strip, jnp.int32), strip, pltpu.SMEM((NMAT,), F32)],
        range(6),
        13,
    )
    gx, gy = lax.axis_size("gx"), lax.axis_size("gy")
    got_a = lax.ppermute(xa, "gx", swap_pairs(gx, 0))
    got_b = lax.ppermute(xb, "gx", swap_pairs(gx, 1))
    pack, grad, e2, h1 = call(solve_kernel, [(n, 128), (n, m), block, block], ins)
    column = (LO_ROWS, 2 * n)
    ya, yb, ylo, yhi, ext, dr = call(
        x_kernel,
        [column, column, column, column, (2 * n, m), (48, m)],
        [got_a, got_b, lo, hi, pack, grad],
    )
    got_b = lax.ppermute(yb, "gy", swap_pairs(gy, 1))
    got_a = lax.ppermute(ya, "gy", swap_pairs(gy, 0))
    inner, h2 = call(inner_kernel, [(n, m), block], [ext, e2, h1])
    return tuple(
        call(
            y_kernel,
            [block, block, (n, m)],
            [got_a, got_b, ylo, yhi, dr, e2, h2, inner],
            [(40, 2 * n), (128, n)],
        )
    )


def solution(mesh):
    return jax.shard_map(
        body,
        mesh=mesh,
        in_specs=(
            P("design", None, "gx", "gy"),
            P("design", None, "gx", "gy"),
            P("design", None, None, "gx", "gy"),
            P(("design", "gx"), "gy"),
            P(),
            P(("design", "gx"), "gy"),
        ),
        out_specs=(
            P("design", None, "gx", "gy"),
            P("design", None, "gx", "gy"),
            P(("design", "gx"), "gy"),
        ),
        check_vma=False,
    )
```

```python
import math

import jax
import jax.numpy as jnp
from jax import lax
from jax.experimental import pallas as pl
from jax.experimental.pallas import tpu as pltpu
from jax.sharding import PartitionSpec as P

STEPS = 2
NMAT = 8
FILT = 16

courant = 0.5
spread_ratio = 0.6

F32 = jnp.float32
HIGHEST = lax.Precision.HIGHEST

LO_G, LO_E1T, LO_E1Z, LO_E2T, LO_E2Z = 0, 16, 18, 20, 22
LO_F0T, LO_F0Z, LO_F1T, LO_F1N, LO_F1Z = 24, 26, 28, 30, 32
LO_W1T, LO_W1Z, LO_R0, LO_R1, LO_ROWS = 34, 36, 38, 39, 40
HI_G, HI_H0T, HI_H0Z, HI_H1T, HI_H1Z = 0, 16, 18, 20, 22
HI_WT, HI_WN, HI_WZ, HI_R, HI_ROWS = 24, 26, 28, 30, 32
LANE_HI = 64
EXT = 24


def tap(distance):
    spread = spread_ratio * FILT
    norm = math.sqrt(sum(math.exp(-d * d / (spread * spread)) for d in range(-FILT, FILT + 1)))
    far = distance.astype(F32)
    value = jnp.exp(-far * far / (2.0 * spread * spread)) / norm
    return jnp.where(jnp.abs(distance) <= FILT, value, F32(0.0))


def iota(shape, dim):
    return lax.broadcasted_iota(jnp.int32, shape, dim)


def updates(n, m, nz):
    row, col = iota((n, m), 0), iota((n, m), 1)

    def lx(f):
        return jnp.where(row == 0, 0.0, pltpu.roll(f, 1, 0))

    def ux(f):
        return jnp.where(row == n - 1, 0.0, pltpu.roll(f, n - 1, 0))

    def ly(f):
        return jnp.where(col == 0, 0.0, pltpu.roll(f, 1, 1))

    def uy(f):
        return jnp.where(col == m - 1, 0.0, pltpu.roll(f, m - 1, 1))

    def electric(e, h, ratio):
        out = [[None] * nz for _ in range(3)]
        for z in range(nz):
            hx, hy, hz = h[0][z], h[1][z], h[2][z]
            dzx = hx - h[0][z - 1] if z > 0 else hx
            dzy = hy - h[1][z - 1] if z > 0 else hy
            out[0][z] = e[0][z] - ratio * ((hz - ly(hz)) - dzy)
            out[1][z] = e[1][z] - ratio * (dzx - (hz - lx(hz)))
            out[2][z] = e[2][z] - ratio * ((hy - lx(hy)) - (hx - ly(hx)))
        return out

    def magnetic(e, h):
        out = [[None] * nz for _ in range(3)]
        for z in range(nz):
            ex, ey, ez = e[0][z], e[1][z], e[2][z]
            dzx = e[0][z + 1] - ex if z < nz - 1 else -ex
            dzy = e[1][z + 1] - ey if z < nz - 1 else -ey
            out[0][z] = h[0][z] + courant * ((uy(ez) - ez) - dzy)
            out[1][z] = h[1][z] + courant * (dzx - (ux(ez) - ez))
            out[2][z] = h[2][z] + courant * ((ux(ey) - ey) - (uy(ex) - ex))
        return out

    return electric, magnetic


def product(e, f):
    total = None
    for c in range(3):
        for z in range(len(e[c])):
            term = e[c][z] * f[c][z]
            total = term if total is None else total + term
    return total


def local_solve(e0, h0, saved, ratio):
    electric, magnetic = updates(*ratio.shape, len(e0[0]))
    e1 = electric(e0, h0, ratio)
    h1 = magnetic(e1, h0)
    fwd = [saved(0)]
    grad = product(e1, fwd[0])
    e2 = electric(e1, h1, ratio)
    fwd.append(saved(1))
    grad = grad + product(e2, fwd[1])
    return e1, h1, e2, grad, fwd


def seam(sgn, a, b, up, down):
    odd = iota(a["h0t"].shape, 0) % 2 == 1
    half = sgn * courant

    def uz(f):
        return jnp.where(odd, 0.0, pltpu.roll(f, 7, 0))

    def lz(f):
        return jnp.where(odd, pltpu.roll(f, 1, 0), 0.0)

    rb, rb1, ra = sgn * b["r0"], sgn * b["r1"], sgn * a["r"]
    d = {}
    e1t = rb * a["h0z"]
    e1z = -rb * a["h0t"]
    e1t_b = b["e1t"] + e1t
    e1z_b = b["e1z"] + e1z
    ah1t = half * e1z_b
    ah1z = -half * e1t_b
    h1t_a = a["h1t"] + ah1t
    h1z_a = a["h1z"] + ah1z
    bh1t = -half * e1z
    bh1n = half * ((uz(e1t) - e1t) - (up(e1z) - e1z))
    bh1z = half * e1t
    e2t = e1t - rb * ((bh1z - h1z_a) - (bh1n - lz(bh1n)))
    e2n = -rb * ((bh1t - lz(bh1t)) - (bh1z - down(bh1z)))
    e2z = e1z - rb * ((bh1n - down(bh1n)) - (bh1t - h1t_a))
    f2t = rb1 * bh1z
    f2z = -rb1 * bh1t
    at = ah1z
    an = (ah1t - lz(ah1t)) - (ah1z - down(ah1z))
    az = -ah1t
    g2t, g2n, g2z = -ra * at, -ra * an, -ra * az
    gb0 = b["f0t"] * e1t + b["f0z"] * e1z + b["f1t"] * e2t + b["f1n"] * e2n + b["f1z"] * e2z
    gb1 = sgn * (b["w1t"] * bh1z - b["w1z"] * bh1t)
    ga = -sgn * (a["wt"] * at + a["wn"] * an + a["wz"] * az)
    e2t_b = b["e2t"] + e2t
    e2z_b = b["e2z"] + e2z
    d["b_e1z"], d["b_h1n"], d["b_h1z"], d["a_h1z"] = e1z, bh1n, bh1z, ah1z
    none = jnp.zeros_like(e1t)
    d["e"] = {"t": (none, g2t, e2t, f2t), "n": (none, g2n, e2n, none), "z": (none, g2z, e2z, f2z)}
    d["h"] = {
        "t": (
            half * g2z,
            ah1t + half * ((e2z_b - g2z) - (uz(g2n) - g2n)),
            bh1t + half * ((f2z - e2z) - (uz(e2n) - e2n)),
            -half * f2z,
        ),
        "n": (
            none,
            half * ((uz(g2t) - g2t) - (up(g2z) - g2z)),
            bh1n + half * ((uz(e2t) - e2t) - (up(e2z) - e2z)),
            half * ((uz(f2t) - f2t) - (up(f2z) - f2z)),
        ),
        "z": (
            -half * g2t,
            ah1z + half * ((up(g2n) - g2n) - (e2t_b - g2t)),
            bh1z + half * ((up(e2n) - e2n) - (f2t - e2t)),
            half * f2t,
        ),
    }
    d["gb0"], d["gb1"], d["ga"] = (g + pltpu.roll(g, 7, 0) for g in (gb0, gb1, ga))
    return d


def two(first, second, at, count=2):
    if count == 1:
        one, other = first[at : at + 1], second[at : at + 1]
        parts = [one, one, other, other]
    else:
        parts = [first[at : at + 2], second[at : at + 2]]
    parts.append(jnp.zeros((4, first.shape[1]), F32))
    return jnp.concatenate(parts, axis=0)


def seam_inputs(left_hi, my_hi, my_lo, right_lo):
    a = {
        "h0t": two(left_hi, my_hi, HI_H0T),
        "h0z": two(left_hi, my_hi, HI_H0Z),
        "h1t": two(left_hi, my_hi, HI_H1T),
        "h1z": two(left_hi, my_hi, HI_H1Z),
        "wt": two(left_hi, my_hi, HI_WT),
        "wn": two(left_hi, my_hi, HI_WN),
        "wz": two(left_hi, my_hi, HI_WZ),
        "r": two(left_hi, my_hi, HI_R, 1),
    }
    b = {
        "e1t": two(my_lo, right_lo, LO_E1T),
        "e1z": two(my_lo, right_lo, LO_E1Z),
        "e2t": two(my_lo, right_lo, LO_E2T),
        "e2z": two(my_lo, right_lo, LO_E2Z),
        "f0t": two(my_lo, right_lo, LO_F0T),
        "f0z": two(my_lo, right_lo, LO_F0Z),
        "f1t": two(my_lo, right_lo, LO_F1T),
        "f1n": two(my_lo, right_lo, LO_F1N),
        "f1z": two(my_lo, right_lo, LO_F1Z),
        "w1t": two(my_lo, right_lo, LO_W1T),
        "w1z": two(my_lo, right_lo, LO_W1Z),
        "r0": two(my_lo, right_lo, LO_R0, 1),
        "r1": two(my_lo, right_lo, LO_R1, 1),
    }
    return a, b


def even(axis):
    return lax.axis_index(axis) % 2 == 0


def ratio_of(labels, density, eps_ref):
    eps = jnp.full(labels.shape, eps_ref[0], F32)
    for k in range(1, NMAT):
        eps = jnp.where(labels == k, eps_ref[k], eps)
    return courant / (eps + density)


def planes(ref, *lead):
    return [[ref[(*lead, c, z)] for z in range(ref.shape[-3])] for c in range(3)]


def edge_lists(t, nrm, e1, h0, h1, e2, fwd, ratio):
    zs = range(len(e1[0]))
    lo = (
        [(e1[c][z], 0) for c in (t, 2) for z in zs]
        + [(e2[c][z], 0) for c in (t, 2) for z in zs]
        + [(fwd[0][c][z], 0) for c in (t, 2) for z in zs]
        + [(fwd[1][c][z], 0) for c in (t, nrm, 2) for z in zs]
        + [((ratio, fwd[1][c][z]), 1) for c in (t, 2) for z in zs]
        + [(ratio, 0), (ratio, 1)]
    )
    hi = (
        [(h0[c][z], -1) for c in (t, 2) for z in zs]
        + [(h1[c][z], -1) for c in (t, 2) for z in zs]
        + [((ratio, fwd[1][c][z]), -1) for c in (t, nrm, 2) for z in zs]
        + [(ratio, -1)]
    )
    return lo, hi


def pack_columns(grad, lo, hi):
    n, m = grad.shape
    lane = iota((n, 128), 1)
    first, last = grad[:, 0:128], grad[:, m - 128 : m]
    pack = jnp.where(lane < FILT, first, 0.0)
    moved = pltpu.roll(last, LANE_HI + FILT, 1)
    pack = jnp.where((lane >= LANE_HI) & (lane < LANE_HI + FILT), moved, pack)

    def tile(item, at):
        if isinstance(item, tuple):
            return tile(item[0], at) * tile(item[1], at)
        return item[:, m - 128 : m] if at < 0 else item[:, 0:128]

    for group, start in ((lo, FILT), (hi, LANE_HI + FILT)):
        for k, (item, at) in enumerate(group):
            pack = jnp.where(lane == start + k, pltpu.roll(tile(item, at), (start + k - at) % 128, 1), pack)
    return pack


def edge_kernel(e_hbm, h_hbm, f_hbm, lab_hbm, den_hbm, eps_hbm,
                a_ref, b_ref, lo_ref, hi_ref,
                e_ref, h_ref, f_ref, lab_ref, den_ref, tab_ref, sems):
    n, m = lab_hbm.shape
    copies = []

    def fetch(src, dst, lead):
        for at, start in ((0, 0), (EXT, n - EXT)):
            index = (*lead, pl.ds(start, EXT))
            copy = pltpu.make_async_copy(src.at[index], dst.at[(*lead, pl.ds(at, EXT))], sems.at[len(copies) - 1])
            copy.start()
            copies.append(copy)

    every = slice(None)
    table = pltpu.make_async_copy(eps_hbm, tab_ref, sems.at[12])
    table.start()
    copies.append(table)
    fetch(lab_hbm, lab_ref, ())
    fetch(den_hbm, den_ref, ())
    fetch(h_hbm, h_ref, (every, every))
    fetch(e_hbm, e_ref, (every, every))
    for step in range(STEPS):
        fetch(f_hbm, f_ref, (step, every, every))
    for copy in copies[:9]:
        copy.wait()
    ratio = ratio_of(lab_ref[...], den_ref[...], tab_ref)
    h0 = planes(h_ref)

    def saved(step):
        for copy in copies[9 + 2 * step : 11 + 2 * step]:
            copy.wait()
        return planes(f_ref, step)

    e1, h1, e2, grad, fwd = local_solve(planes(e_ref), h0, saved, ratio)
    rows = 2 * EXT

    def line(item, at):
        if isinstance(item, tuple):
            return line(item[0], at) * line(item[1], at)
        at = at % rows
        return item[at : at + 1]

    lo, hi = edge_lists(1, 0, e1, h0, h1, e2, fwd, ratio)
    lo_ref[0:FILT] = grad[0:FILT]
    for k, (item, at) in enumerate(lo):
        lo_ref[FILT + k : FILT + k + 1] = line(item, at)
    hi_ref[0:FILT] = grad[rows - FILT : rows]
    for k, (item, at) in enumerate(hi):
        hi_ref[FILT + k : FILT + k + 1] = line(item, at)
    hi_ref[HI_ROWS - 1 : HI_ROWS] = jnp.zeros((1, m), F32)
    pack = pack_columns(grad, *edge_lists(0, 1, e1, h0, h1, e2, fwd, ratio))

    def corner(part):
        low = jnp.concatenate([part[0:8], part[8:16]], axis=1)
        high = jnp.concatenate([part[16:24], jnp.zeros((8, m - 128), F32)], axis=1)
        return jnp.concatenate([low, high], axis=0)

    lo_all = jnp.concatenate([lo_ref[...], corner(pack[0:EXT])], axis=0)
    hi_all = jnp.concatenate([hi_ref[...], jnp.zeros((LO_ROWS - HI_ROWS, m), F32), corner(pack[EXT:rows])], axis=0)
    first_even = even("gx")
    a_ref[...] = jnp.where(first_even, hi_all, lo_all)
    b_ref[...] = jnp.where(first_even, lo_all, hi_all)


def solve_kernel(e_ref, h_ref, f_ref, lab_ref, den_ref, eps_ref, pack_ref, grad_ref, e2_ref, h1_ref):
    ratio = ratio_of(lab_ref[...], den_ref[...], eps_ref)
    h0 = planes(h_ref)
    e1, h1, e2, grad, fwd = local_solve(planes(e_ref), h0, lambda step: planes(f_ref, step), ratio)
    for c in range(3):
        for z in range(e_ref.shape[1]):
            e2_ref[c, z] = e2[c][z]
            h1_ref[c, z] = h1[c][z]
    grad_ref[...] = grad
    pack_ref[...] = pack_columns(grad, *edge_lists(0, 1, e1, h0, h1, e2, fwd, ratio))


def x_kernel(ra_ref, rb_ref, lo_ref, hi_ref, pack_ref, grad_ref,
             yhi_ref, ylo_ref, ext_ref, dr_ref):
    n, m = grad_ref.shape
    first_even = even("gx")
    right = jnp.where(first_even, ra_ref[...], rb_ref[...])
    left = jnp.where(first_even, rb_ref[...], ra_ref[...])
    a, b = seam_inputs(left, hi_ref[...], lo_ref[...], right)
    col = iota((8, m), 1)
    d = seam(
        -1.0, a, b,
        lambda f: jnp.where(col == m - 1, 0.0, pltpu.roll(f, m - 1, 1)),
        lambda f: jnp.where(col == 0, 0.0, pltpu.roll(f, 1, 1)),
    )
    for f, field in enumerate(("e", "h")):
        for c, name in enumerate(("n", "t", "z")):
            before, end, begin, after = d[field][name]
            for z in range(2):
                p = 4 * (6 * f + 2 * c + z)
                dr_ref[p : p + 1] = before[2 + z : 3 + z]
                dr_ref[p + 1 : p + 2] = end[2 + z : 3 + z]
                dr_ref[p + 2 : p + 3] = begin[z : z + 1]
                dr_ref[p + 3 : p + 4] = after[z : z + 1]
    gb0, gb1, ga = d["gb0"], d["gb1"], d["ga"]
    top = iota((8, m), 0)
    ext_ref[0:n] = grad_ref[...]
    ext_ref[0:8] = grad_ref[0:8] + jnp.where(top == 0, gb0[0:1], jnp.where(top == 1, gb1[0:1], 0.0))
    ext_ref[n - 8 : n] = grad_ref[n - 8 : n] + jnp.where(top == 7, ga[2:3], 0.0)
    ext_ref[n : n + 8] = right[0:8] + jnp.where(top == 0, gb0[2:3], jnp.where(top == 1, gb1[2:3], 0.0))
    ext_ref[n + 8 : n + 16] = right[8:16]
    ext_ref[n + 16 : 2 * n - 16] = jnp.zeros((n - 32, m), F32)
    ext_ref[2 * n - 16 : 2 * n - 8] = left[0:8]
    ext_ref[2 * n - 8 : 2 * n] = left[8:16] + jnp.where(top == 7, ga[0:1], 0.0)

    lane = iota((1, 128), 1)

    def strips(g):
        out = jnp.where(lane < FILT, g[:, 0:128], 0.0)
        moved = pltpu.roll(g[:, m - 128 : m], LANE_HI + FILT, 1)
        return jnp.where((lane >= LANE_HI) & (lane < LANE_HI + FILT), moved, out)

    def put(row_vec, at, value, seam_row, c):
        for z in range(2):
            one = value[seam_row + z : seam_row + z + 1, c : c + 1]
            row_vec = jnp.where(lane == at + z, one, row_vec)
        return row_vec

    hi = LANE_HI
    row0 = strips(gb0[0:1])
    row0 = put(row0, LO_E1Z, d["b_e1z"], 0, 0)
    row0 = put(row0, LO_E2T, d["e"]["n"][2], 0, 0)
    row0 = put(row0, LO_E2Z, d["e"]["z"][2], 0, 0)
    row0 = put(row0, hi + HI_H1T, d["b_h1n"], 0, m - 1)
    row0 = put(row0, hi + HI_H1Z, d["b_h1z"], 0, m - 1)
    row1 = strips(gb1[0:1])
    row1 = put(row1, LO_E2Z, d["e"]["z"][3], 0, 0)
    end = strips(ga[2:3])
    end = put(end, LO_E2T, d["e"]["n"][1], 2, 0)
    end = put(end, LO_E2Z, d["e"]["z"][1], 2, 0)
    end = put(end, hi + HI_H1Z, d["a_h1z"], 2, m - 1)
    out0 = strips(gb0[2:3])
    out0 = put(out0, LO_E1Z, d["b_e1z"], 2, 0)
    out0 = put(out0, hi + HI_H1T, d["b_h1n"], 2, m - 1)
    out0 = put(out0, hi + HI_H1Z, d["b_h1z"], 2, m - 1)
    out1 = strips(gb1[2:3])
    before = strips(ga[0:1])
    before = put(before, hi + HI_H1Z, d["a_h1z"], 0, m - 1)

    sub = iota((8, 128), 0)

    def corner(message):
        return [message[40:48, 0:128], message[40:48, 128:256], message[48:56, 0:128]]

    above, below = corner(right), corner(left)
    above[0] = above[0] + jnp.where(sub == 0, out0, jnp.where(sub == 1, out1, 0.0))
    below[2] = below[2] + jnp.where(sub == 7, before, 0.0)
    head = pack_ref[0:8] + jnp.where(sub == 0, row0, jnp.where(sub == 1, row1, 0.0))
    tail = pack_ref[n - 8 : n] + jnp.where(sub == 7, end, 0.0)
    inner = jnp.concatenate([head, pack_ref[8 : n - 8], tail], axis=0)
    outer = jnp.concatenate(above + [jnp.zeros((n - 2 * EXT, 128), F32)] + below, axis=0)
    packed = jnp.concatenate([inner.T, outer.T], axis=1)
    lo, hi_part = packed[0:LO_ROWS], packed[LANE_HI : LANE_HI + LO_ROWS]
    ylo_ref[...] = lo
    yhi_ref[...] = hi_part


def inner_kernel(ext_ref, e2_ref, h1_ref, out_ref, h2_ref):
    nz = e2_ref.shape[1]
    _, magnetic = updates(*out_ref.shape, nz)
    h2 = magnetic(planes(e2_ref), planes(h1_ref))
    for c in range(3):
        for z in range(nz):
            h2_ref[c, z] = h2[c][z]
    rows, m = ext_ref.shape
    n = out_ref.shape[0]
    d = iota((n, rows), 1) - iota((n, rows), 0)
    d = jnp.where(d > rows // 2, d - rows, jnp.where(d < -(rows // 2), d + rows, d))
    along = jnp.dot(tap(d), ext_ref[...], precision=HIGHEST, preferred_element_type=F32)
    e = iota((m, m), 0) - iota((m, m), 1)
    out_ref[...] = jnp.dot(along, tap(e), precision=HIGHEST, preferred_element_type=F32)


def y_kernel(left_ref, right_ref, lo_ref, hi_ref, dr_ref, e2_ref, h2_ref, inner_ref,
             e_ref, h_ref, out_ref, gt_ref, dc_ref):
    n, m = inner_ref.shape
    right, left = right_ref[...], left_ref[...]
    rows = right.shape[1]
    a, b = seam_inputs(left, hi_ref[...], lo_ref[...], right)
    d = seam(1.0, a, b, lambda f: pltpu.roll(f, rows - 1, 1), lambda f: pltpu.roll(f, 1, 1))

    gb0, gb1, ga = d["gb0"], d["gb1"], d["ga"]
    top = iota((8, rows), 0)
    gt_ref[0:8] = right[0:8] + jnp.where(top == 0, gb0[2:3], jnp.where(top == 1, gb1[2:3], 0.0))
    gt_ref[8:16] = right[8:16]
    gt_ref[16:24] = left[0:8]
    gt_ref[24:32] = left[8:16] + jnp.where(top == 7, ga[0:1], 0.0)
    gt_ref[32:40] = jnp.where(top == 0, gb0[0:1], jnp.where(top == 1, gb1[0:1], jnp.where(top == 2, ga[2:3], 0.0)))

    for f, field in enumerate(("e", "h")):
        for c, name in enumerate(("t", "n", "z")):
            before, end, begin, after = d[field][name]
            for z in range(2):
                p = 4 * (6 * f + 2 * c + z)
                dc_ref[p : p + 1] = before[2 + z : 3 + z, 0:n]
                dc_ref[p + 1 : p + 2] = end[2 + z : 3 + z, 0:n]
                dc_ref[p + 2 : p + 3] = begin[z : z + 1, 0:n]
                dc_ref[p + 3 : p + 4] = after[z : z + 1, 0:n]
    dc_ref[48:128] = jnp.zeros((80, n), F32)
    columns = dc_ref[...].T
    lane = iota((n, 128), 1)
    sub = iota((8, m), 0)
    for f, (src, dst) in enumerate(((e2_ref, e_ref), (h2_ref, h_ref))):
        for c in range(3):
            for z in range(2):
                p = 4 * (6 * f + 2 * c + z)
                moved = pltpu.roll(columns, (126 - p) % 128, 1)
                low = src[c, z, :, 0:128] + jnp.where(lane < 2, moved, 0.0)
                high = src[c, z, :, m - 128 : m] + jnp.where(lane >= 126, moved, 0.0)
                dst[c, z, :, 0:128] = low
                dst[c, z, :, m - 128 : m] = high
                dst[c, z, 0:8] += jnp.where(sub == 0, dr_ref[p + 2 : p + 3], jnp.where(sub == 1, dr_ref[p + 3 : p + 4], 0.0))
                dst[c, z, n - 8 : n] += jnp.where(sub == 6, dr_ref[p : p + 1], jnp.where(sub == 7, dr_ref[p + 1 : p + 2], 0.0))

    d = iota((rows, n), 0) - iota((rows, n), 1)
    d = jnp.where(d > rows // 2, d - rows, jnp.where(d < -(rows // 2), d + rows, d))
    along = jnp.dot(gt_ref[...], tap(d), precision=HIGHEST, preferred_element_type=F32)
    k = iota((40, m), 0)
    place = jnp.where(k < 16, m + k, jnp.where(k < 32, k - 32, jnp.where(k < 34, k - 32, m - 1)))
    spread = jnp.where(k < 35, tap(place - iota((40, m), 1)), 0.0)
    extra = lax.dot_general(along, spread, (((0,), (0,)), ((), ())), precision=HIGHEST, preferred_element_type=F32)
    out_ref[...] = inner_ref[...] + extra


def swap_pairs(count, which):
    if which == 0:
        return [(i, i ^ 1) for i in range(count)]
    return [(i, (i - 1) % count if i % 2 == 0 else (i + 1) % count) for i in range(count)]


def call(kernel, shapes, ins, scratch=(), far=(), sems=0):
    vmem = pl.BlockSpec(memory_space=pltpu.VMEM)
    hbm = pl.BlockSpec(memory_space=pltpu.HBM)
    smem = pl.BlockSpec(memory_space=pltpu.SMEM)
    ins = [pltpu.with_memory_space_constraint(x, pltpu.HBM) if k in far else x for k, x in enumerate(ins)]
    scratches = [s if hasattr(s, "dtype") else pltpu.VMEM(s, F32) for s in scratch]
    if sems:
        scratches.append(pltpu.SemaphoreType.DMA((sems,)))
    return pl.pallas_call(
        kernel,
        out_shape=[jax.ShapeDtypeStruct(s, F32) for s in shapes],
        in_specs=[hbm if k in far else smem if x.shape == (NMAT,) else vmem for k, x in enumerate(ins)],
        out_specs=[vmem] * len(shapes),
        scratch_shapes=scratches,
        compiler_params=pltpu.CompilerParams(vmem_limit_bytes=24 * 1024 * 1024),
    )(*ins)


def body(adj_e, adj_h, fwd_e, labels, eps_table, density):
    n, m = labels.shape
    block = adj_e.shape
    nz = block[1]
    ins = [adj_e, adj_h, fwd_e, labels, density, eps_table]
    message = (LO_ROWS + 16, m)
    strip = (2 * EXT, m)
    xa, xb, lo, hi = call(
        edge_kernel,
        [message, message, (LO_ROWS, m), (HI_ROWS, m)],
        ins,
        [(3, nz, *strip), (3, nz, *strip), (STEPS, 3, nz, *strip), pltpu.VMEM(strip, jnp.int32), strip, pltpu.SMEM((NMAT,), F32)],
        range(6),
        13,
    )
    gx, gy = lax.axis_size("gx"), lax.axis_size("gy")
    got_a = lax.ppermute(xa, "gx", swap_pairs(gx, 0))
    got_b = lax.ppermute(xb, "gx", swap_pairs(gx, 1))
    pack, grad, e2, h1 = call(solve_kernel, [(n, 128), (n, m), block, block], ins)
    column = (LO_ROWS, 2 * n)
    yhi, ylo, ext, dr = call(
        x_kernel,
        [column, column, (2 * n, m), (48, m)],
        [got_a, got_b, lo, hi, pack, grad],
    )
    left = lax.ppermute(yhi, "gy", [(i, (i + 1) % gy) for i in range(gy)])
    right = lax.ppermute(ylo, "gy", [(i, (i - 1) % gy) for i in range(gy)])
    inner, h2 = call(inner_kernel, [(n, m), block], [ext, e2, h1])
    return tuple(
        call(
            y_kernel,
            [block, block, (n, m)],
            [left, right, ylo, yhi, dr, e2, h2, inner],
            [(40, 2 * n), (128, n)],
        )
    )


def solution(mesh):
    return jax.shard_map(
        body,
        mesh=mesh,
        in_specs=(
            P("design", None, "gx", "gy"),
            P("design", None, "gx", "gy"),
            P("design", None, None, "gx", "gy"),
            P(("design", "gx"), "gy"),
            P(),
            P(("design", "gx"), "gy"),
        ),
        out_specs=(
            P("design", None, "gx", "gy"),
            P("design", None, "gx", "gy"),
            P(("design", "gx"), "gy"),
        ),
        check_vma=False,
    )
```

```python
import math

import jax
import jax.numpy as jnp
from jax import lax
from jax.experimental import pallas as pl
from jax.experimental.pallas import tpu as pltpu
from jax.sharding import PartitionSpec as P

STEPS = 2
NMAT = 8
FILT = 16

courant = 0.5
spread_ratio = 0.6

F32 = jnp.float32
HIGHEST = lax.Precision.HIGHEST

LO_G, LO_E1T, LO_E1Z, LO_E2T, LO_E2Z = 0, 16, 18, 20, 22
LO_F0T, LO_F0Z, LO_F1T, LO_F1N, LO_F1Z = 24, 26, 28, 30, 32
LO_W1T, LO_W1Z, LO_R0, LO_R1, LO_ROWS = 34, 36, 38, 39, 40
HI_G, HI_H0T, HI_H0Z, HI_H1T, HI_H1Z = 0, 16, 18, 20, 22
HI_WT, HI_WN, HI_WZ, HI_R, HI_ROWS = 24, 26, 28, 30, 32
EXT, DONE = 24, 16

PACK_F1, PACK_R, PACK_PAIR, PACK_F0, PACK_END = 16, 34, 37, 53, 57
LO_LANES = (
    list(range(FILT))
    + [PACK_PAIR + 2 * j + 1 for j in range(8)]
    + [PACK_F0 + j for j in range(4)]
    + [PACK_F1 + 3 * k + 1 for k in range(6)]
    + [PACK_F1 + 3 * k + 2 for k in (0, 1, 4, 5)]
    + [PACK_R + 1, PACK_R + 2]
)
HI_LANES = (
    list(range(128 - FILT, 128))
    + [PACK_PAIR + 2 * j for j in range(8)]
    + [PACK_F1 + 3 * k for k in range(6)]
    + [PACK_R, PACK_END]
)
CORNER = PACK_END - PACK_F1


def tap(distance):
    spread = spread_ratio * FILT
    norm = math.sqrt(sum(math.exp(-d * d / (spread * spread)) for d in range(-FILT, FILT + 1)))
    far = distance.astype(F32)
    value = jnp.exp(-far * far / (2.0 * spread * spread)) / norm
    return jnp.where(jnp.abs(distance) <= FILT, value, F32(0.0))


def iota(shape, dim):
    return lax.broadcasted_iota(jnp.int32, shape, dim)


def updates(n, m, nz):
    row, col = iota((n, m), 0), iota((n, m), 1)

    def lx(f):
        return jnp.where(row == 0, 0.0, pltpu.roll(f, 1, 0))

    def ux(f):
        return jnp.where(row == n - 1, 0.0, pltpu.roll(f, n - 1, 0))

    def ly(f):
        return jnp.where(col == 0, 0.0, pltpu.roll(f, 1, 1))

    def uy(f):
        return jnp.where(col == m - 1, 0.0, pltpu.roll(f, m - 1, 1))

    def electric(e, h, ratio):
        out = [[None] * nz for _ in range(3)]
        for z in range(nz):
            hx, hy, hz = h[0][z], h[1][z], h[2][z]
            dzx = hx - h[0][z - 1] if z > 0 else hx
            dzy = hy - h[1][z - 1] if z > 0 else hy
            out[0][z] = e[0][z] - ratio * ((hz - ly(hz)) - dzy)
            out[1][z] = e[1][z] - ratio * (dzx - (hz - lx(hz)))
            out[2][z] = e[2][z] - ratio * ((hy - lx(hy)) - (hx - ly(hx)))
        return out

    def magnetic(e, h):
        out = [[None] * nz for _ in range(3)]
        for z in range(nz):
            ex, ey, ez = e[0][z], e[1][z], e[2][z]
            dzx = e[0][z + 1] - ex if z < nz - 1 else -ex
            dzy = e[1][z + 1] - ey if z < nz - 1 else -ey
            out[0][z] = h[0][z] + courant * ((uy(ez) - ez) - dzy)
            out[1][z] = h[1][z] + courant * (dzx - (ux(ez) - ez))
            out[2][z] = h[2][z] + courant * ((ux(ey) - ey) - (uy(ex) - ex))
        return out

    return electric, magnetic


def product(e, f):
    total = None
    for c in range(3):
        for z in range(len(e[c])):
            term = e[c][z] * f[c][z]
            total = term if total is None else total + term
    return total


def local_solve(e0, h0, saved, ratio):
    electric, magnetic = updates(*ratio.shape, len(e0[0]))
    e1 = electric(e0, h0, ratio)
    h1 = magnetic(e1, h0)
    fwd = [saved(0)]
    grad = product(e1, fwd[0])
    e2 = electric(e1, h1, ratio)
    fwd.append(saved(1))
    grad = grad + product(e2, fwd[1])
    return e1, h1, e2, grad, fwd


def seam(sgn, a, b, up, down):
    odd = iota(a["h0t"].shape, 0) % 2 == 1
    half = sgn * courant

    def uz(f):
        return jnp.where(odd, 0.0, pltpu.roll(f, 7, 0))

    def lz(f):
        return jnp.where(odd, pltpu.roll(f, 1, 0), 0.0)

    rb, rb1, ra = sgn * b["r0"], sgn * b["r1"], sgn * a["r"]
    d = {}
    e1t = rb * a["h0z"]
    e1z = -rb * a["h0t"]
    e1t_b = b["e1t"] + e1t
    e1z_b = b["e1z"] + e1z
    ah1t = half * e1z_b
    ah1z = -half * e1t_b
    h1t_a = a["h1t"] + ah1t
    h1z_a = a["h1z"] + ah1z
    bh1t = -half * e1z
    bh1n = half * ((uz(e1t) - e1t) - (up(e1z) - e1z))
    bh1z = half * e1t
    e2t = e1t - rb * ((bh1z - h1z_a) - (bh1n - lz(bh1n)))
    e2n = -rb * ((bh1t - lz(bh1t)) - (bh1z - down(bh1z)))
    e2z = e1z - rb * ((bh1n - down(bh1n)) - (bh1t - h1t_a))
    f2t = rb1 * bh1z
    f2z = -rb1 * bh1t
    at = ah1z
    an = (ah1t - lz(ah1t)) - (ah1z - down(ah1z))
    az = -ah1t
    g2t, g2n, g2z = -ra * at, -ra * an, -ra * az
    gb0 = b["f0t"] * e1t + b["f0z"] * e1z + b["f1t"] * e2t + b["f1n"] * e2n + b["f1z"] * e2z
    gb1 = sgn * (b["w1t"] * bh1z - b["w1z"] * bh1t)
    ga = -sgn * (a["wt"] * at + a["wn"] * an + a["wz"] * az)
    e2t_b = b["e2t"] + e2t
    e2z_b = b["e2z"] + e2z
    d["b_e1z"], d["b_h1n"], d["b_h1z"], d["a_h1z"] = e1z, bh1n, bh1z, ah1z
    none = jnp.zeros_like(e1t)
    d["e"] = {"t": (none, g2t, e2t, f2t), "n": (none, g2n, e2n, none), "z": (none, g2z, e2z, f2z)}
    d["h"] = {
        "t": (
            half * g2z,
            ah1t + half * ((e2z_b - g2z) - (uz(g2n) - g2n)),
            bh1t + half * ((f2z - e2z) - (uz(e2n) - e2n)),
            -half * f2z,
        ),
        "n": (
            none,
            half * ((uz(g2t) - g2t) - (up(g2z) - g2z)),
            bh1n + half * ((uz(e2t) - e2t) - (up(e2z) - e2z)),
            half * ((uz(f2t) - f2t) - (up(f2z) - f2z)),
        ),
        "z": (
            -half * g2t,
            ah1z + half * ((up(g2n) - g2n) - (e2t_b - g2t)),
            bh1z + half * ((up(e2n) - e2n) - (f2t - e2t)),
            half * f2t,
        ),
    }
    d["gb0"], d["gb1"], d["ga"] = (g + pltpu.roll(g, 7, 0) for g in (gb0, gb1, ga))
    return d


def two(first, second, at, count=2):
    if count == 1:
        one, other = first[at : at + 1], second[at : at + 1]
        parts = [one, one, other, other]
    else:
        parts = [first[at : at + 2], second[at : at + 2]]
    parts.append(jnp.zeros((4, first.shape[1]), F32))
    return jnp.concatenate(parts, axis=0)


def seam_inputs(left_hi, my_hi, my_lo, right_lo):
    a = {
        "h0t": two(left_hi, my_hi, HI_H0T),
        "h0z": two(left_hi, my_hi, HI_H0Z),
        "h1t": two(left_hi, my_hi, HI_H1T),
        "h1z": two(left_hi, my_hi, HI_H1Z),
        "wt": two(left_hi, my_hi, HI_WT),
        "wn": two(left_hi, my_hi, HI_WN),
        "wz": two(left_hi, my_hi, HI_WZ),
        "r": two(left_hi, my_hi, HI_R, 1),
    }
    b = {
        "e1t": two(my_lo, right_lo, LO_E1T),
        "e1z": two(my_lo, right_lo, LO_E1Z),
        "e2t": two(my_lo, right_lo, LO_E2T),
        "e2z": two(my_lo, right_lo, LO_E2Z),
        "f0t": two(my_lo, right_lo, LO_F0T),
        "f0z": two(my_lo, right_lo, LO_F0Z),
        "f1t": two(my_lo, right_lo, LO_F1T),
        "f1n": two(my_lo, right_lo, LO_F1N),
        "f1z": two(my_lo, right_lo, LO_F1Z),
        "w1t": two(my_lo, right_lo, LO_W1T),
        "w1z": two(my_lo, right_lo, LO_W1Z),
        "r0": two(my_lo, right_lo, LO_R0, 1),
        "r1": two(my_lo, right_lo, LO_R1, 1),
    }
    return a, b


def even(axis):
    return lax.axis_index(axis) % 2 == 0


def ratio_of(labels, density, eps_ref):
    eps = jnp.full(labels.shape, eps_ref[0], F32)
    for k in range(1, NMAT):
        eps = jnp.where(labels == k, eps_ref[k], eps)
    return courant / (eps + density)


def planes(ref, *lead):
    return [[ref[(*lead, c, z)] for z in range(ref.shape[-3])] for c in range(3)]


def edge_lists(t, nrm, e1, h0, h1, e2, fwd, ratio):
    zs = range(len(e1[0]))
    lo = (
        [(e1[c][z], 0) for c in (t, 2) for z in zs]
        + [(e2[c][z], 0) for c in (t, 2) for z in zs]
        + [(fwd[0][c][z], 0) for c in (t, 2) for z in zs]
        + [(fwd[1][c][z], 0) for c in (t, nrm, 2) for z in zs]
        + [((ratio, fwd[1][c][z]), 1) for c in (t, 2) for z in zs]
        + [(ratio, 0), (ratio, 1)]
    )
    hi = (
        [(h0[c][z], -1) for c in (t, 2) for z in zs]
        + [(h1[c][z], -1) for c in (t, 2) for z in zs]
        + [((ratio, fwd[1][c][z]), -1) for c in (t, nrm, 2) for z in zs]
        + [(ratio, -1)]
    )
    return lo, hi


def fold(first, last):
    m = first.shape[1]
    lane = iota((first.shape[0], 128), 1)
    return jnp.where(lane < 64, first[:, 0:128], last[:, m - 128 : m])


def strips(grad):
    lane = iota((grad.shape[0], 128), 1)
    return jnp.where((lane < FILT) | (lane >= 128 - FILT), fold(grad, grad), 0.0)


def place(pack, values, base, count=3):
    lane = iota(pack.shape, 1)
    return jnp.where((lane >= base) & (lane < base + count), pltpu.roll(values, base + 1, 1), pack)


def pack_fields(pack, ratio, e1, h0, h1, e2):
    pack = place(pack, fold(ratio, ratio), PACK_R)
    for k, (first, last) in enumerate(((e1, h0), (e2, h1))):
        for j, (c, z) in enumerate((c, z) for c in (0, 2) for z in range(2)):
            pack = place(pack, fold(first[c][z], last[c][z]), PACK_PAIR + 8 * k + 2 * j, 2)
    return pack


def pack_saved(pack, ratio, fwd):
    lane = iota(pack.shape, 1)
    for j, (c, z) in enumerate((c, z) for c in (0, 2) for z in range(2)):
        pack = jnp.where(lane == PACK_F0 + j, pltpu.roll(fwd[0][c][z][:, 0:128], PACK_F0 + j, 1), pack)
    scale = jnp.where(lane == 0, 1.0, fold(ratio, ratio))
    for k, (c, z) in enumerate((c, z) for c in range(3) for z in range(2)):
        pack = place(pack, fold(fwd[1][c][z], fwd[1][c][z]) * scale, PACK_F1 + 3 * k)
    return pack


def unpack_rows(packed, lanes, ref, at=0):
    ref[0:FILT, at : at + 128] = packed[lanes[0] : lanes[0] + FILT]
    for k in range(FILT, len(lanes)):
        ref[k : k + 1, at : at + 128] = packed[lanes[k] : lanes[k] + 1]


def edge_kernel(e_hbm, h_hbm, f_hbm, lab_hbm, den_hbm, eps_hbm,
                a_ref, b_ref, lo_ref, hi_ref, e2_ref, h1_ref, grad_ref, pack_ref,
                e_ref, h_ref, f_ref, lab_ref, den_ref, tab_ref, sems):
    n, m = lab_hbm.shape
    copies = []

    def fetch(src, dst, lead):
        for at, start in ((0, 0), (EXT, n - EXT)):
            index = (*lead, pl.ds(start, EXT))
            copy = pltpu.make_async_copy(src.at[index], dst.at[(*lead, pl.ds(at, EXT))], sems.at[len(copies) - 1])
            copy.start()
            copies.append(copy)

    every = slice(None)
    table = pltpu.make_async_copy(eps_hbm, tab_ref, sems.at[12])
    table.start()
    copies.append(table)
    fetch(lab_hbm, lab_ref, ())
    fetch(den_hbm, den_ref, ())
    fetch(h_hbm, h_ref, (every, every))
    fetch(e_hbm, e_ref, (every, every))
    for step in range(STEPS):
        fetch(f_hbm, f_ref, (step, every, every))
    for copy in copies[:9]:
        copy.wait()
    ratio = ratio_of(lab_ref[...], den_ref[...], tab_ref)
    h0 = planes(h_ref)

    electric, magnetic = updates(2 * EXT, m, e_hbm.shape[1])
    e1 = electric(planes(e_ref), h0, ratio)
    h1 = magnetic(e1, h0)
    e2 = electric(e1, h1, ratio)
    pack = pack_fields(jnp.zeros((2 * EXT, 128), F32), ratio, e1, h0, h1, e2)
    for copy in copies[9:11]:
        copy.wait()
    fwd = [planes(f_ref, 0)]
    grad = product(e1, fwd[0])
    for copy in copies[11:13]:
        copy.wait()
    fwd.append(planes(f_ref, 1))
    grad = grad + product(e2, fwd[1])
    pack = pack_saved(pack, ratio, fwd)
    rows = 2 * EXT

    def line(item, at):
        if isinstance(item, tuple):
            return line(item[0], at) * line(item[1], at)
        at = at % rows
        return item[at : at + 1]

    lo, hi = edge_lists(1, 0, e1, h0, h1, e2, fwd, ratio)
    for ref, group, strip in ((hi_ref, hi, grad[rows - FILT : rows]), (lo_ref, lo, grad[0:FILT])):
        ref[0:FILT] = strip
        for k, (item, at) in enumerate(group):
            ref[FILT + k : FILT + k + 1] = line(item, at)
    hi_ref[HI_ROWS - 1 : HI_ROWS] = jnp.zeros((1, m), F32)
    lane = iota((8, 128), 1)

    def corner(part):
        out = pltpu.roll(part[0:8], 128 - PACK_F1, 1)
        for k in range(1, 3):
            out = jnp.where(lane < CORNER * k, out, pltpu.roll(part[8 * k : 8 * k + 8], CORNER * k - PACK_F1, 1))
        return out

    first_even = even("gx")
    lo_corner, hi_corner = corner(pack[0:EXT]), corner(pack[EXT:rows])
    for half in range(2):
        at, cols = half * LO_ROWS, slice(128 * half, 128 * half + 128)
        low, high = lo_ref[:, cols], hi_ref[:, cols]
        high = jnp.concatenate([high, jnp.zeros((LO_ROWS - HI_ROWS, 128), F32)], axis=0)
        a_ref[at : at + LO_ROWS] = jnp.where(first_even, high, low)
        b_ref[at : at + LO_ROWS] = jnp.where(first_even, low, high)
    a_ref[2 * LO_ROWS :] = jnp.where(first_even, hi_corner, lo_corner)
    b_ref[2 * LO_ROWS :] = jnp.where(first_even, lo_corner, hi_corner)
    pack = jnp.where((iota(pack.shape, 1) < FILT) | (iota(pack.shape, 1) >= 128 - FILT), strips(grad), pack)
    for to, at in ((0, 0), (DONE, rows - DONE)):
        for c in range(3):
            for z in range(e_hbm.shape[1]):
                e2_ref[c, z, to : to + DONE] = e2[c][z][at : at + DONE]
                h1_ref[c, z, to : to + DONE] = h1[c][z][at : at + DONE]
        grad_ref[to : to + DONE] = grad[at : at + DONE]
        pack_ref[to : to + DONE] = pack[at : at + DONE]


def solve_kernel(e_ref, h_ref, f_ref, lab_ref, den_ref, eps_ref, e2_edge, h1_edge, grad_edge, pack_edge,
                 lo_ref, hi_ref, grad_ref, e2_ref, h1_ref):
    n, m = lab_ref.shape
    nz = e_ref.shape[1]
    rows = pl.ds(DONE - 8, n - 2 * DONE + 16)

    def inner(ref, *lead):
        return [[ref[(*lead, c, z, rows)] for z in range(nz)] for c in range(3)]

    ratio = ratio_of(lab_ref[rows], den_ref[rows], eps_ref)
    h0 = inner(h_ref)
    e1, h1, e2, grad, fwd = local_solve(inner(e_ref), h0, lambda step: inner(f_ref, step), ratio)
    last = n - DONE
    for c in range(3):
        for z in range(nz):
            for ref, edge, value in ((e2_ref, e2_edge, e2), (h1_ref, h1_edge, h1)):
                ref[c, z, 0:DONE] = edge[c, z, 0:DONE]
                ref[c, z, DONE:last] = value[c][z][8 : last - DONE + 8]
                ref[c, z, last:n] = edge[c, z, DONE : 2 * DONE]
    grad_ref[0:DONE] = grad_edge[0:DONE]
    grad_ref[DONE:last] = grad[8 : last - DONE + 8]
    grad_ref[last:n] = grad_edge[DONE : 2 * DONE]
    pack = pack_saved(pack_fields(strips(grad), ratio, e1, h0, h1, e2), ratio, fwd)
    packed = jnp.concatenate([pack_edge[0:DONE], pack[8 : last - DONE + 8], pack_edge[DONE : 2 * DONE]], axis=0).T
    unpack_rows(packed, LO_LANES, lo_ref)
    unpack_rows(packed, HI_LANES, hi_ref)


def x_kernel(ra_ref, rb_ref, lo_ref, hi_ref, plo_ref, phi_ref, grad_ref,
             yhi_ref, ylo_ref, ext_ref, dr_ref):
    n, m = grad_ref.shape
    first_even = even("gx")
    got_right = jnp.where(first_even, ra_ref[...], rb_ref[...])
    got_left = jnp.where(first_even, rb_ref[...], ra_ref[...])
    right, left = (jnp.concatenate([got[0:LO_ROWS], got[LO_ROWS : 2 * LO_ROWS]], axis=1) for got in (got_right, got_left))
    a, b = seam_inputs(left, hi_ref[...], lo_ref[...], right)
    col = iota((8, m), 1)
    d = seam(
        -1.0, a, b,
        lambda f: jnp.where(col == m - 1, 0.0, pltpu.roll(f, m - 1, 1)),
        lambda f: jnp.where(col == 0, 0.0, pltpu.roll(f, 1, 1)),
    )
    for f, field in enumerate(("e", "h")):
        for c, name in enumerate(("n", "t", "z")):
            before, end, begin, after = d[field][name]
            for z in range(2):
                p = 4 * (6 * f + 2 * c + z)
                dr_ref[p : p + 1] = before[2 + z : 3 + z]
                dr_ref[p + 1 : p + 2] = end[2 + z : 3 + z]
                dr_ref[p + 2 : p + 3] = begin[z : z + 1]
                dr_ref[p + 3 : p + 4] = after[z : z + 1]
    gb0, gb1, ga = d["gb0"], d["gb1"], d["ga"]
    top = iota((8, m), 0)
    ext_ref[0:n] = grad_ref[...]
    ext_ref[0:8] = grad_ref[0:8] + jnp.where(top == 0, gb0[0:1], jnp.where(top == 1, gb1[0:1], 0.0))
    ext_ref[n - 8 : n] = grad_ref[n - 8 : n] + jnp.where(top == 7, ga[2:3], 0.0)
    ext_ref[n : n + 8] = right[0:8] + jnp.where(top == 0, gb0[2:3], jnp.where(top == 1, gb1[2:3], 0.0))
    ext_ref[n + 8 : n + 16] = right[8:16]
    ext_ref[n + 16 : 2 * n - 16] = jnp.zeros((n - 32, m), F32)
    ext_ref[2 * n - 16 : 2 * n - 8] = left[0:8]
    ext_ref[2 * n - 8 : 2 * n] = left[8:16] + jnp.where(top == 7, ga[0:1], 0.0)

    lane = iota((1, 128), 1)

    def put(row_vec, lanes, at, value, seam_row, c):
        for z in range(2):
            one = value[seam_row + z : seam_row + z + 1, c : c + 1]
            row_vec = jnp.where(lane == lanes[at + z], one, row_vec)
        return row_vec

    row0 = put(strips(gb0[0:1]), LO_LANES, LO_E1Z, d["b_e1z"], 0, 0)
    row0 = put(row0, LO_LANES, LO_E2T, d["e"]["n"][2], 0, 0)
    row0 = put(row0, LO_LANES, LO_E2Z, d["e"]["z"][2], 0, 0)
    row0 = put(row0, HI_LANES, HI_H1T, d["b_h1n"], 0, m - 1)
    row0 = put(row0, HI_LANES, HI_H1Z, d["b_h1z"], 0, m - 1)
    row1 = put(strips(gb1[0:1]), LO_LANES, LO_E2Z, d["e"]["z"][3], 0, 0)
    end = put(strips(ga[2:3]), LO_LANES, LO_E2T, d["e"]["n"][1], 2, 0)
    end = put(end, LO_LANES, LO_E2Z, d["e"]["z"][1], 2, 0)
    end = put(end, HI_LANES, HI_H1Z, d["a_h1z"], 2, m - 1)
    none = jnp.zeros((1, 128), F32)
    out0 = put(none, LO_LANES, LO_E1Z, d["b_e1z"], 2, 0)
    out0 = put(out0, HI_LANES, HI_H1T, d["b_h1n"], 2, m - 1)
    out0 = put(out0, HI_LANES, HI_H1Z, d["b_h1z"], 2, m - 1)
    before = put(none, HI_LANES, HI_H1Z, d["a_h1z"], 0, m - 1)

    sub = iota((8, 128), 0)
    wide = iota((8, 128), 1)

    def corner(message, first_row):
        tile = message[2 * LO_ROWS : 2 * LO_ROWS + 8]
        out = []
        for k in range(3):
            moved = pltpu.roll(tile, (PACK_F1 - CORNER * k) % 128, 1)
            part = jnp.where((wide >= PACK_F1) & (wide < PACK_END), moved, 0.0)
            at = first_row + 8 * k
            if n <= at < n + FILT or at >= 2 * n - FILT:
                part = part + strips(ext_ref[at : at + 8])
            out.append(part)
        return out

    above, below = corner(got_right, n), corner(got_left, 2 * n - EXT)
    above[0] = above[0] + jnp.where(sub == 0, out0, 0.0)
    below[2] = below[2] + jnp.where(sub == 7, before, 0.0)
    own = jnp.where(sub == 0, end, jnp.where(sub == 1, row0, jnp.where(sub == 2, row1, 0.0)))
    filler = jnp.zeros((8, 128), F32)
    used = EXT // 8
    tiles = above + [own] + [filler] * (n // 8 - 2 * used - 1) + below
    packed = jnp.concatenate(tiles, axis=0).T
    for ref, mine, lanes in ((ylo_ref, plo_ref, LO_LANES), (yhi_ref, phi_ref, HI_LANES)):
        count = len(lanes)
        unpack_rows(packed, lanes, ref, n)
        at = iota((count, n), 1)
        moved = pltpu.roll(ref[0:count, n : 2 * n], (n - EXT - 1) % n, 1)
        ref[0:count, 0:n] = mine[...] + jnp.where((at < 2) | (at == n - 1), moved, 0.0)
    yhi_ref[HI_ROWS:LO_ROWS] = jnp.zeros((LO_ROWS - HI_ROWS, 2 * n), F32)


def inner_kernel(ext_ref, e2_ref, h1_ref, out_ref, h2_ref):
    nz = e2_ref.shape[1]
    _, magnetic = updates(*out_ref.shape, nz)
    h2 = magnetic(planes(e2_ref), planes(h1_ref))
    for c in range(3):
        for z in range(nz):
            h2_ref[c, z] = h2[c][z]
    rows, m = ext_ref.shape
    n = out_ref.shape[0]
    d = iota((n, rows), 1) - iota((n, rows), 0)
    d = jnp.where(d > rows // 2, d - rows, jnp.where(d < -(rows // 2), d + rows, d))
    along = jnp.dot(tap(d), ext_ref[...], precision=HIGHEST, preferred_element_type=F32)
    e = iota((m, m), 0) - iota((m, m), 1)
    out_ref[...] = jnp.dot(along, tap(e), precision=HIGHEST, preferred_element_type=F32)


def y_kernel(left_ref, right_ref, lo_ref, hi_ref, dr_ref, e2_ref, h2_ref, inner_ref,
             e_ref, h_ref, out_ref, gt_ref, dc_ref):
    n, m = inner_ref.shape
    right, left = right_ref[...], left_ref[...]
    rows = right.shape[1]
    a, b = seam_inputs(left, hi_ref[...], lo_ref[...], right)
    d = seam(1.0, a, b, lambda f: pltpu.roll(f, rows - 1, 1), lambda f: pltpu.roll(f, 1, 1))

    gb0, gb1, ga = d["gb0"], d["gb1"], d["ga"]
    top = iota((8, rows), 0)
    gt_ref[0:8] = right[0:8] + jnp.where(top == 0, gb0[2:3], jnp.where(top == 1, gb1[2:3], 0.0))
    gt_ref[8:16] = right[8:16]
    gt_ref[16:24] = left[0:8]
    gt_ref[24:32] = left[8:16] + jnp.where(top == 7, ga[0:1], 0.0)
    gt_ref[32:40] = jnp.where(top == 0, gb0[0:1], jnp.where(top == 1, gb1[0:1], jnp.where(top == 2, ga[2:3], 0.0)))

    for f, field in enumerate(("e", "h")):
        for c, name in enumerate(("t", "n", "z")):
            before, end, begin, after = d[field][name]
            for z in range(2):
                p = 4 * (6 * f + 2 * c + z)
                dc_ref[p : p + 1] = before[2 + z : 3 + z, 0:n]
                dc_ref[p + 1 : p + 2] = end[2 + z : 3 + z, 0:n]
                dc_ref[p + 2 : p + 3] = begin[z : z + 1, 0:n]
                dc_ref[p + 3 : p + 4] = after[z : z + 1, 0:n]
    dc_ref[48:128] = jnp.zeros((80, n), F32)
    columns = dc_ref[...].T
    lane = iota((n, 128), 1)
    sub = iota((8, m), 0)
    for f, (src, dst) in enumerate(((e2_ref, e_ref), (h2_ref, h_ref))):
        for c in range(3):
            for z in range(2):
                p = 4 * (6 * f + 2 * c + z)
                moved = pltpu.roll(columns, (126 - p) % 128, 1)
                low = src[c, z, :, 0:128] + jnp.where(lane < 2, moved, 0.0)
                high = src[c, z, :, m - 128 : m] + jnp.where(lane >= 126, moved, 0.0)
                dst[c, z, :, 0:128] = low
                dst[c, z, :, m - 128 : m] = high
                dst[c, z, 0:8] += jnp.where(sub == 0, dr_ref[p + 2 : p + 3], jnp.where(sub == 1, dr_ref[p + 3 : p + 4], 0.0))
                dst[c, z, n - 8 : n] += jnp.where(sub == 6, dr_ref[p : p + 1], jnp.where(sub == 7, dr_ref[p + 1 : p + 2], 0.0))

    d = iota((rows, n), 0) - iota((rows, n), 1)
    d = jnp.where(d > rows // 2, d - rows, jnp.where(d < -(rows // 2), d + rows, d))
    along = jnp.dot(gt_ref[...], tap(d), precision=HIGHEST, preferred_element_type=F32)
    k = iota((40, m), 0)
    place = jnp.where(k < 16, m + k, jnp.where(k < 32, k - 32, jnp.where(k < 34, k - 32, m - 1)))
    spread = jnp.where(k < 35, tap(place - iota((40, m), 1)), 0.0)
    extra = lax.dot_general(along, spread, (((0,), (0,)), ((), ())), precision=HIGHEST, preferred_element_type=F32)
    out_ref[...] = inner_ref[...] + extra


def swap_pairs(count, which):
    if which == 0:
        return [(i, i ^ 1) for i in range(count)]
    return [(i, (i - 1) % count if i % 2 == 0 else (i + 1) % count) for i in range(count)]


def call(kernel, shapes, ins, scratch=(), far=(), sems=0):
    vmem = pl.BlockSpec(memory_space=pltpu.VMEM)
    hbm = pl.BlockSpec(memory_space=pltpu.HBM)
    smem = pl.BlockSpec(memory_space=pltpu.SMEM)
    ins = [pltpu.with_memory_space_constraint(x, pltpu.HBM) if k in far else x for k, x in enumerate(ins)]
    scratches = [s if hasattr(s, "dtype") else pltpu.VMEM(s, F32) for s in scratch]
    if sems:
        scratches.append(pltpu.SemaphoreType.DMA((sems,)))
    return pl.pallas_call(
        kernel,
        out_shape=[jax.ShapeDtypeStruct(s, F32) for s in shapes],
        in_specs=[hbm if k in far else smem if x.shape == (NMAT,) else vmem for k, x in enumerate(ins)],
        out_specs=[vmem] * len(shapes),
        scratch_shapes=scratches,
        compiler_params=pltpu.CompilerParams(vmem_limit_bytes=24 * 1024 * 1024),
    )(*ins)


def body(adj_e, adj_h, fwd_e, labels, eps_table, density):
    n, m = labels.shape
    block = adj_e.shape
    nz = block[1]
    ins = [adj_e, adj_h, fwd_e, labels, density, eps_table]
    message = (2 * LO_ROWS + 8, 128)
    strip = (2 * EXT, m)
    edges = (3, nz, 2 * DONE, m)
    xa, xb, lo, hi, *solved = call(
        edge_kernel,
        [message, message, (LO_ROWS, m), (HI_ROWS, m), edges, edges, (2 * DONE, m), (2 * DONE, 128)],
        ins,
        [(3, nz, *strip), (3, nz, *strip), (STEPS, 3, nz, *strip), pltpu.VMEM(strip, jnp.int32), strip, pltpu.SMEM((NMAT,), F32)],
        range(6),
        13,
    )
    gx, gy = lax.axis_size("gx"), lax.axis_size("gy")
    got_a = lax.ppermute(xa, "gx", swap_pairs(gx, 0))
    got_b = lax.ppermute(xb, "gx", swap_pairs(gx, 1))
    plo, phi, grad, e2, h1 = call(
        solve_kernel, [(LO_ROWS, n), (HI_ROWS, n), (n, m), block, block], ins + solved
    )
    column = (LO_ROWS, 2 * n)
    yhi, ylo, ext, dr = call(
        x_kernel,
        [column, column, (2 * n, m), (48, m)],
        [got_a, got_b, lo, hi, plo, phi, grad],
    )
    left = lax.ppermute(yhi, "gy", [(i, (i + 1) % gy) for i in range(gy)])
    right = lax.ppermute(ylo, "gy", [(i, (i - 1) % gy) for i in range(gy)])
    inner, h2 = call(inner_kernel, [(n, m), block], [ext, e2, h1])
    return tuple(
        call(
            y_kernel,
            [block, block, (n, m)],
            [left, right, ylo, yhi, dr, e2, h2, inner],
            [(40, 2 * n), (128, n)],
        )
    )


def solution(mesh):
    return jax.shard_map(
        body,
        mesh=mesh,
        in_specs=(
            P("design", None, "gx", "gy"),
            P("design", None, "gx", "gy"),
            P("design", None, None, "gx", "gy"),
            P(("design", "gx"), "gy"),
            P(),
            P(("design", "gx"), "gy"),
        ),
        out_specs=(
            P("design", None, "gx", "gy"),
            P("design", None, "gx", "gy"),
            P(("design", "gx"), "gy"),
        ),
        check_vma=False,
    )
```

```python
import math

import jax
import jax.numpy as jnp
from jax import lax
from jax.experimental import pallas as pl
from jax.experimental.pallas import tpu as pltpu
from jax.sharding import PartitionSpec as P

STEPS = 2
NMAT = 8
FILT = 16

courant = 0.5
spread_ratio = 0.6

F32 = jnp.float32
HIGHEST = lax.Precision.HIGHEST

LO_G, LO_E1T, LO_E1Z, LO_E2T, LO_E2Z = 0, 16, 18, 20, 22
LO_F0T, LO_F0Z, LO_F1T, LO_F1N, LO_F1Z = 24, 26, 28, 30, 32
LO_W1T, LO_W1Z, LO_R0, LO_R1, LO_ROWS = 34, 36, 38, 39, 40
HI_G, HI_H0T, HI_H0Z, HI_H1T, HI_H1Z = 0, 16, 18, 20, 22
HI_WT, HI_WN, HI_WZ, HI_R, HI_ROWS = 24, 26, 28, 30, 32
EXT = 24

PACK_F1, PACK_R, PACK_PAIR, PACK_F0, PACK_END = 16, 34, 37, 53, 57
LO_LANES = (
    list(range(FILT))
    + [PACK_PAIR + 2 * j + 1 for j in range(8)]
    + [PACK_F0 + j for j in range(4)]
    + [PACK_F1 + 3 * k + 1 for k in range(6)]
    + [PACK_F1 + 3 * k + 2 for k in (0, 1, 4, 5)]
    + [PACK_R + 1, PACK_R + 2]
)
HI_LANES = (
    list(range(128 - FILT, 128))
    + [PACK_PAIR + 2 * j for j in range(8)]
    + [PACK_F1 + 3 * k for k in range(6)]
    + [PACK_R, PACK_END]
)
CORNER = PACK_END - PACK_F1


def tap(distance):
    spread = spread_ratio * FILT
    norm = math.sqrt(sum(math.exp(-d * d / (spread * spread)) for d in range(-FILT, FILT + 1)))
    far = distance.astype(F32)
    value = jnp.exp(-far * far / (2.0 * spread * spread)) / norm
    return jnp.where(jnp.abs(distance) <= FILT, value, F32(0.0))


def iota(shape, dim):
    return lax.broadcasted_iota(jnp.int32, shape, dim)


def updates(n, m, nz):
    row, col = iota((n, m), 0), iota((n, m), 1)

    def lx(f):
        return jnp.where(row == 0, 0.0, pltpu.roll(f, 1, 0))

    def ux(f):
        return jnp.where(row == n - 1, 0.0, pltpu.roll(f, n - 1, 0))

    def ly(f):
        return jnp.where(col == 0, 0.0, pltpu.roll(f, 1, 1))

    def uy(f):
        return jnp.where(col == m - 1, 0.0, pltpu.roll(f, m - 1, 1))

    def turn(h, ratio):
        out = [[None] * nz for _ in range(3)]
        for z in range(nz):
            hx, hy, hz = h[0][z], h[1][z], h[2][z]
            dzx = hx - h[0][z - 1] if z > 0 else hx
            dzy = hy - h[1][z - 1] if z > 0 else hy
            out[0][z] = ratio * ((hz - ly(hz)) - dzy)
            out[1][z] = ratio * (dzx - (hz - lx(hz)))
            out[2][z] = ratio * ((hy - lx(hy)) - (hx - ly(hx)))
        return out

    def magnetic(e, h):
        out = [[None] * nz for _ in range(3)]
        for z in range(nz):
            ex, ey, ez = e[0][z], e[1][z], e[2][z]
            dzx = e[0][z + 1] - ex if z < nz - 1 else -ex
            dzy = e[1][z + 1] - ey if z < nz - 1 else -ey
            out[0][z] = h[0][z] + courant * ((uy(ez) - ez) - dzy)
            out[1][z] = h[1][z] + courant * (dzx - (ux(ez) - ez))
            out[2][z] = h[2][z] + courant * ((ux(ey) - ey) - (uy(ex) - ex))
        return out

    return turn, magnetic


def less(e, change):
    return [[a - b for a, b in zip(one, other, strict=True)] for one, other in zip(e, change, strict=True)]


def product(e, f):
    total = None
    for c in range(3):
        for z in range(len(e[c])):
            term = e[c][z] * f[c][z]
            total = term if total is None else total + term
    return total


def local_solve(e0, h0, saved, ratio):
    turn, magnetic = updates(*ratio.shape, len(e0[0]))
    e1 = less(e0, turn(h0, ratio))
    h1 = magnetic(e1, h0)
    fwd = [saved(0)]
    grad = product(e1, fwd[0])
    e2 = less(e1, turn(h1, ratio))
    fwd.append(saved(1))
    grad = grad + product(e2, fwd[1])
    return e1, h1, e2, grad, fwd


def seam(sgn, a, b, up, down):
    odd = iota(a["h0t"].shape, 0) % 2 == 1
    half = sgn * courant

    def uz(f):
        return jnp.where(odd, 0.0, pltpu.roll(f, 7, 0))

    def lz(f):
        return jnp.where(odd, pltpu.roll(f, 1, 0), 0.0)

    rb, rb1, ra = sgn * b["r0"], sgn * b["r1"], sgn * a["r"]
    d = {}
    e1t = rb * a["h0z"]
    e1z = -rb * a["h0t"]
    e1t_b = b["e1t"] + e1t
    e1z_b = b["e1z"] + e1z
    ah1t = half * e1z_b
    ah1z = -half * e1t_b
    h1t_a = a["h1t"] + ah1t
    h1z_a = a["h1z"] + ah1z
    bh1t = -half * e1z
    bh1n = half * ((uz(e1t) - e1t) - (up(e1z) - e1z))
    bh1z = half * e1t
    e2t = e1t - rb * ((bh1z - h1z_a) - (bh1n - lz(bh1n)))
    e2n = -rb * ((bh1t - lz(bh1t)) - (bh1z - down(bh1z)))
    e2z = e1z - rb * ((bh1n - down(bh1n)) - (bh1t - h1t_a))
    f2t = rb1 * bh1z
    f2z = -rb1 * bh1t
    at = ah1z
    an = (ah1t - lz(ah1t)) - (ah1z - down(ah1z))
    az = -ah1t
    g2t, g2n, g2z = -ra * at, -ra * an, -ra * az
    gb0 = b["f0t"] * e1t + b["f0z"] * e1z + b["f1t"] * e2t + b["f1n"] * e2n + b["f1z"] * e2z
    gb1 = sgn * (b["w1t"] * bh1z - b["w1z"] * bh1t)
    ga = -sgn * (a["wt"] * at + a["wn"] * an + a["wz"] * az)
    e2t_b = b["e2t"] + e2t
    e2z_b = b["e2z"] + e2z
    d["b_e1z"], d["b_h1n"], d["b_h1z"], d["a_h1z"] = e1z, bh1n, bh1z, ah1z
    none = jnp.zeros_like(e1t)
    d["e"] = {"t": (none, g2t, e2t, f2t), "n": (none, g2n, e2n, none), "z": (none, g2z, e2z, f2z)}
    d["h"] = {
        "t": (
            half * g2z,
            ah1t + half * ((e2z_b - g2z) - (uz(g2n) - g2n)),
            bh1t + half * ((f2z - e2z) - (uz(e2n) - e2n)),
            -half * f2z,
        ),
        "n": (
            none,
            half * ((uz(g2t) - g2t) - (up(g2z) - g2z)),
            bh1n + half * ((uz(e2t) - e2t) - (up(e2z) - e2z)),
            half * ((uz(f2t) - f2t) - (up(f2z) - f2z)),
        ),
        "z": (
            -half * g2t,
            ah1z + half * ((up(g2n) - g2n) - (e2t_b - g2t)),
            bh1z + half * ((up(e2n) - e2n) - (f2t - e2t)),
            half * f2t,
        ),
    }
    d["gb0"], d["gb1"], d["ga"] = (g + pltpu.roll(g, 7, 0) for g in (gb0, gb1, ga))
    return d


def two(first, second, at, count=2):
    if count == 1:
        one, other = first[at : at + 1], second[at : at + 1]
        parts = [one, one, other, other]
    else:
        parts = [first[at : at + 2], second[at : at + 2]]
    parts.append(jnp.zeros((4, first.shape[1]), F32))
    return jnp.concatenate(parts, axis=0)


def seam_inputs(left_hi, my_hi, my_lo, right_lo):
    a = {
        "h0t": two(left_hi, my_hi, HI_H0T),
        "h0z": two(left_hi, my_hi, HI_H0Z),
        "h1t": two(left_hi, my_hi, HI_H1T),
        "h1z": two(left_hi, my_hi, HI_H1Z),
        "wt": two(left_hi, my_hi, HI_WT),
        "wn": two(left_hi, my_hi, HI_WN),
        "wz": two(left_hi, my_hi, HI_WZ),
        "r": two(left_hi, my_hi, HI_R, 1),
    }
    b = {
        "e1t": two(my_lo, right_lo, LO_E1T),
        "e1z": two(my_lo, right_lo, LO_E1Z),
        "e2t": two(my_lo, right_lo, LO_E2T),
        "e2z": two(my_lo, right_lo, LO_E2Z),
        "f0t": two(my_lo, right_lo, LO_F0T),
        "f0z": two(my_lo, right_lo, LO_F0Z),
        "f1t": two(my_lo, right_lo, LO_F1T),
        "f1n": two(my_lo, right_lo, LO_F1N),
        "f1z": two(my_lo, right_lo, LO_F1Z),
        "w1t": two(my_lo, right_lo, LO_W1T),
        "w1z": two(my_lo, right_lo, LO_W1Z),
        "r0": two(my_lo, right_lo, LO_R0, 1),
        "r1": two(my_lo, right_lo, LO_R1, 1),
    }
    return a, b


def even(axis):
    return lax.axis_index(axis) % 2 == 0


def ratio_of(labels, density, table):
    eps = jnp.broadcast_to(table[0], labels.shape)
    for k in range(1, NMAT):
        eps = jnp.where(labels == k, table[k], eps)
    return courant / (eps + density)


def planes(ref, *lead):
    return [[ref[(*lead, c, z)] for z in range(ref.shape[-3])] for c in range(3)]


def edge_lists(t, nrm, e1, h0, h1, e2, fwd, ratio):
    zs = range(len(e1[0]))
    lo = (
        [(e1[c][z], 0) for c in (t, 2) for z in zs]
        + [(e2[c][z], 0) for c in (t, 2) for z in zs]
        + [(fwd[0][c][z], 0) for c in (t, 2) for z in zs]
        + [(fwd[1][c][z], 0) for c in (t, nrm, 2) for z in zs]
        + [((ratio, fwd[1][c][z]), 1) for c in (t, 2) for z in zs]
        + [(ratio, 0), (ratio, 1)]
    )
    hi = (
        [(h0[c][z], -1) for c in (t, 2) for z in zs]
        + [(h1[c][z], -1) for c in (t, 2) for z in zs]
        + [((ratio, fwd[1][c][z]), -1) for c in (t, nrm, 2) for z in zs]
        + [(ratio, -1)]
    )
    return lo, hi


def fold(first, last):
    m = first.shape[1]
    lane = iota((first.shape[0], 128), 1)
    return jnp.where(lane < 64, first[:, 0:128], last[:, m - 128 : m])


def strips(grad):
    lane = iota((grad.shape[0], 128), 1)
    return jnp.where((lane < FILT) | (lane >= 128 - FILT), fold(grad, grad), 0.0)


def place(pack, values, base, count=3):
    lane = iota(pack.shape, 1)
    return jnp.where((lane >= base) & (lane < base + count), pltpu.roll(values, base + 1, 1), pack)


def pack_fields(pack, ratio, e1, h0, h1, e2):
    pack = place(pack, fold(ratio, ratio), PACK_R)
    for k, (first, last) in enumerate(((e1, h0), (e2, h1))):
        for j, (c, z) in enumerate((c, z) for c in (0, 2) for z in range(2)):
            pack = place(pack, fold(first[c][z], last[c][z]), PACK_PAIR + 8 * k + 2 * j, 2)
    return pack


def pack_saved(pack, ratio, fwd):
    lane = iota(pack.shape, 1)
    for j, (c, z) in enumerate((c, z) for c in (0, 2) for z in range(2)):
        pack = jnp.where(lane == PACK_F0 + j, pltpu.roll(fwd[0][c][z][:, 0:128], PACK_F0 + j, 1), pack)
    scale = jnp.where(lane == 0, 1.0, fold(ratio, ratio))
    for k, (c, z) in enumerate((c, z) for c in range(3) for z in range(2)):
        pack = place(pack, fold(fwd[1][c][z], fwd[1][c][z]) * scale, PACK_F1 + 3 * k)
    return pack


def unpack_rows(packed, lanes, ref, at=0):
    ref[0:FILT, at : at + 128] = packed[lanes[0] : lanes[0] + FILT]
    for k in range(FILT, len(lanes)):
        ref[k : k + 1, at : at + 128] = packed[lanes[k] : lanes[k] + 1]


def edge_kernel(e_hbm, h_hbm, f_hbm, lab_hbm, den_hbm, eps_hbm,
                a_ref, b_ref, lo_ref, hi_ref, table_ref,
                e_ref, h_ref, f_ref, lab_ref, den_ref, tab_ref, sems):
    n, m = lab_hbm.shape
    nz = e_hbm.shape[1]
    copies = []

    def fetch(src, dst, *lead):
        for to, at in ((0, 0), (EXT, n - EXT)):
            copy = pltpu.make_async_copy(src.at[(*lead, pl.ds(at, EXT))], dst.at[(*lead, pl.ds(to, EXT))], sems.at[len(copies)])
            copy.start()
            copies.append(copy)

    every = slice(None)
    fetch(h_hbm, h_ref, every, every)
    fetch(lab_hbm, lab_ref)
    fetch(den_hbm, den_ref)
    copies.append(pltpu.make_async_copy(eps_hbm, tab_ref, sems.at[len(copies)]))
    copies[-1].start()
    fetch(e_hbm, e_ref, every, every)
    for step in range(STEPS):
        fetch(f_hbm, f_ref, step, every, every)

    def wait(first, last):
        for copy in copies[first:last]:
            copy.wait()

    turn, magnetic = updates(2 * EXT, m, nz)
    wait(2, 7)
    ratio = ratio_of(lab_ref[...], den_ref[...], tab_ref)
    wait(0, 2)
    h0 = planes(h_ref)
    change = turn(h0, ratio)
    wait(7, 9)
    e1 = less(planes(e_ref), change)
    h1 = magnetic(e1, h0)
    e2 = less(e1, turn(h1, ratio))
    pack = pack_fields(jnp.zeros((2 * EXT, 128), F32), ratio, e1, h0, h1, e2)
    wait(9, 11)
    fwd = [planes(f_ref, 0)]
    grad = product(e1, fwd[0])
    wait(11, 13)
    fwd.append(planes(f_ref, 1))
    grad = grad + product(e2, fwd[1])
    pack = pack_saved(pack, ratio, fwd)
    rows = 2 * EXT

    def line(item, at):
        if isinstance(item, tuple):
            return line(item[0], at) * line(item[1], at)
        at = at % rows
        return item[at : at + 1]

    lo, hi = edge_lists(1, 0, e1, h0, h1, e2, fwd, ratio)
    for ref, group, strip in ((hi_ref, hi, grad[rows - FILT : rows]), (lo_ref, lo, grad[0:FILT])):
        ref[0:FILT] = strip
        for k, (item, at) in enumerate(group):
            ref[FILT + k : FILT + k + 1] = line(item, at)
    hi_ref[HI_ROWS - 1 : HI_ROWS] = jnp.zeros((1, m), F32)
    lane = iota((8, 128), 1)

    def corner(part):
        out = pltpu.roll(part[0:8], 128 - PACK_F1, 1)
        for k in range(1, 3):
            out = jnp.where(lane < CORNER * k, out, pltpu.roll(part[8 * k : 8 * k + 8], CORNER * k - PACK_F1, 1))
        return out

    first_even = even("gx")
    lo_corner, hi_corner = corner(pack[0:EXT]), corner(pack[EXT:rows])
    for half in range(2):
        at, cols = half * LO_ROWS, slice(128 * half, 128 * half + 128)
        low, high = lo_ref[:, cols], hi_ref[:, cols]
        high = jnp.concatenate([high, jnp.zeros((LO_ROWS - HI_ROWS, 128), F32)], axis=0)
        a_ref[at : at + LO_ROWS] = jnp.where(first_even, high, low)
        b_ref[at : at + LO_ROWS] = jnp.where(first_even, low, high)
    a_ref[2 * LO_ROWS :] = jnp.where(first_even, hi_corner, lo_corner)
    b_ref[2 * LO_ROWS :] = jnp.where(first_even, lo_corner, hi_corner)
    for k in range(NMAT):
        table_ref[k : k + 1] = jnp.full((1, m), tab_ref[k], F32)


def solve_kernel(e_ref, h_ref, f_ref, lab_ref, den_ref, table_ref, lo_ref, hi_ref, grad_ref, e2_ref, h1_ref):
    ratio = ratio_of(lab_ref[...], den_ref[...], [table_ref[k : k + 1] for k in range(NMAT)])
    h0 = planes(h_ref)
    e1, h1, e2, grad, fwd = local_solve(planes(e_ref), h0, lambda step: planes(f_ref, step), ratio)
    for c in range(3):
        for z in range(e_ref.shape[1]):
            e2_ref[c, z] = e2[c][z]
            h1_ref[c, z] = h1[c][z]
    grad_ref[...] = grad
    packed = pack_saved(pack_fields(strips(grad), ratio, e1, h0, h1, e2), ratio, fwd).T
    unpack_rows(packed, LO_LANES, lo_ref)
    unpack_rows(packed, HI_LANES, hi_ref)


def x_kernel(ra_ref, rb_ref, lo_ref, hi_ref, plo_ref, phi_ref, grad_ref,
             yhi_ref, ylo_ref, ext_ref, dr_ref):
    n, m = grad_ref.shape
    first_even = even("gx")
    got_right = jnp.where(first_even, ra_ref[...], rb_ref[...])
    got_left = jnp.where(first_even, rb_ref[...], ra_ref[...])
    right, left = (jnp.concatenate([got[0:LO_ROWS], got[LO_ROWS : 2 * LO_ROWS]], axis=1) for got in (got_right, got_left))
    a, b = seam_inputs(left, hi_ref[...], lo_ref[...], right)
    col = iota((8, m), 1)
    d = seam(
        -1.0, a, b,
        lambda f: jnp.where(col == m - 1, 0.0, pltpu.roll(f, m - 1, 1)),
        lambda f: jnp.where(col == 0, 0.0, pltpu.roll(f, 1, 1)),
    )
    for f, field in enumerate(("e", "h")):
        for c, name in enumerate(("n", "t", "z")):
            before, end, begin, after = d[field][name]
            for z in range(2):
                p = 4 * (6 * f + 2 * c + z)
                dr_ref[p : p + 1] = before[2 + z : 3 + z]
                dr_ref[p + 1 : p + 2] = end[2 + z : 3 + z]
                dr_ref[p + 2 : p + 3] = begin[z : z + 1]
                dr_ref[p + 3 : p + 4] = after[z : z + 1]
    gb0, gb1, ga = d["gb0"], d["gb1"], d["ga"]
    top = iota((8, m), 0)
    ext_ref[0:n] = grad_ref[...]
    ext_ref[0:8] = grad_ref[0:8] + jnp.where(top == 0, gb0[0:1], jnp.where(top == 1, gb1[0:1], 0.0))
    ext_ref[n - 8 : n] = grad_ref[n - 8 : n] + jnp.where(top == 7, ga[2:3], 0.0)
    ext_ref[n : n + 8] = right[0:8] + jnp.where(top == 0, gb0[2:3], jnp.where(top == 1, gb1[2:3], 0.0))
    ext_ref[n + 8 : n + 16] = right[8:16]
    ext_ref[n + 16 : 2 * n - 16] = jnp.zeros((n - 32, m), F32)
    ext_ref[2 * n - 16 : 2 * n - 8] = left[0:8]
    ext_ref[2 * n - 8 : 2 * n] = left[8:16] + jnp.where(top == 7, ga[0:1], 0.0)

    lane = iota((1, 128), 1)

    def put(row_vec, lanes, at, value, seam_row, c):
        for z in range(2):
            one = value[seam_row + z : seam_row + z + 1, c : c + 1]
            row_vec = jnp.where(lane == lanes[at + z], one, row_vec)
        return row_vec

    row0 = put(strips(gb0[0:1]), LO_LANES, LO_E1Z, d["b_e1z"], 0, 0)
    row0 = put(row0, LO_LANES, LO_E2T, d["e"]["n"][2], 0, 0)
    row0 = put(row0, LO_LANES, LO_E2Z, d["e"]["z"][2], 0, 0)
    row0 = put(row0, HI_LANES, HI_H1T, d["b_h1n"], 0, m - 1)
    row0 = put(row0, HI_LANES, HI_H1Z, d["b_h1z"], 0, m - 1)
    row1 = put(strips(gb1[0:1]), LO_LANES, LO_E2Z, d["e"]["z"][3], 0, 0)
    end = put(strips(ga[2:3]), LO_LANES, LO_E2T, d["e"]["n"][1], 2, 0)
    end = put(end, LO_LANES, LO_E2Z, d["e"]["z"][1], 2, 0)
    end = put(end, HI_LANES, HI_H1Z, d["a_h1z"], 2, m - 1)
    none = jnp.zeros((1, 128), F32)
    out0 = put(none, LO_LANES, LO_E1Z, d["b_e1z"], 2, 0)
    out0 = put(out0, HI_LANES, HI_H1T, d["b_h1n"], 2, m - 1)
    out0 = put(out0, HI_LANES, HI_H1Z, d["b_h1z"], 2, m - 1)
    before = put(none, HI_LANES, HI_H1Z, d["a_h1z"], 0, m - 1)

    sub = iota((8, 128), 0)
    wide = iota((8, 128), 1)

    def corner(message, first_row):
        tile = message[2 * LO_ROWS : 2 * LO_ROWS + 8]
        out = []
        for k in range(3):
            moved = pltpu.roll(tile, (PACK_F1 - CORNER * k) % 128, 1)
            part = jnp.where((wide >= PACK_F1) & (wide < PACK_END), moved, 0.0)
            at = first_row + 8 * k
            if n <= at < n + FILT or at >= 2 * n - FILT:
                part = part + strips(ext_ref[at : at + 8])
            out.append(part)
        return out

    above, below = corner(got_right, n), corner(got_left, 2 * n - EXT)
    above[0] = above[0] + jnp.where(sub == 0, out0, 0.0)
    below[2] = below[2] + jnp.where(sub == 7, before, 0.0)
    own = jnp.where(sub == 0, end, jnp.where(sub == 1, row0, jnp.where(sub == 2, row1, 0.0)))
    filler = jnp.zeros((8, 128), F32)
    used = EXT // 8
    tiles = above + [own] + [filler] * (n // 8 - 2 * used - 1) + below
    packed = jnp.concatenate(tiles, axis=0).T
    for ref, mine, lanes in ((ylo_ref, plo_ref, LO_LANES), (yhi_ref, phi_ref, HI_LANES)):
        count = len(lanes)
        unpack_rows(packed, lanes, ref, n)
        at = iota((count, n), 1)
        moved = pltpu.roll(ref[0:count, n : 2 * n], (n - EXT - 1) % n, 1)
        ref[0:count, 0:n] = mine[...] + jnp.where((at < 2) | (at == n - 1), moved, 0.0)
    yhi_ref[HI_ROWS:LO_ROWS] = jnp.zeros((LO_ROWS - HI_ROWS, 2 * n), F32)


def cyclic(d, count):
    return jnp.where(d > count // 2, d - count, jnp.where(d < -(count // 2), d + count, d))


def inner_kernel(ext_ref, e2_ref, h1_ref, out_ref, h2_ref, band_ref, spread_ref):
    rows, m = ext_ref.shape
    n = out_ref.shape[0]
    nz = e2_ref.shape[1]
    _, magnetic = updates(n, m, nz)
    h2 = magnetic(planes(e2_ref), planes(h1_ref))
    for c in range(3):
        for z in range(nz):
            h2_ref[c, z] = h2[c][z]
    band = tap(cyclic(iota((n, rows), 1) - iota((n, rows), 0), rows))
    along = jnp.dot(band, ext_ref[...], precision=HIGHEST, preferred_element_type=F32)
    out_ref[...] = jnp.dot(along, tap(iota((m, m), 0) - iota((m, m), 1)), precision=HIGHEST, preferred_element_type=F32)
    band_ref[...] = tap(cyclic(iota((rows, n), 0) - iota((rows, n), 1), rows))
    k = iota(spread_ref.shape, 0)
    column = jnp.where(k < FILT, m + k, jnp.where(k < 2 * FILT + 2, k - 2 * FILT, m - 1))
    spread_ref[...] = jnp.where(k < 2 * FILT + 3, tap(column - iota(spread_ref.shape, 1)), 0.0)


def y_kernel(left_ref, right_ref, lo_ref, hi_ref, dr_ref, e2_ref, h2_ref, inner_ref, band_ref, spread_ref,
             e_hbm, h_hbm, out_hbm, gt_ref, dc_ref, out_ref, e_ref, h_ref, sems):
    n, m = inner_ref.shape
    right, left = right_ref[...], left_ref[...]
    rows = right.shape[1]
    a, b = seam_inputs(left, hi_ref[...], lo_ref[...], right)
    d = seam(1.0, a, b, lambda f: pltpu.roll(f, rows - 1, 1), lambda f: pltpu.roll(f, 1, 1))

    for f, field in enumerate(("e", "h")):
        for c, name in enumerate(("t", "n", "z")):
            before, end, begin, after = d[field][name]
            for z in range(2):
                p = 4 * (6 * f + 2 * c + z)
                dc_ref[p : p + 1] = before[2 + z : 3 + z, 0:n]
                dc_ref[p + 1 : p + 2] = end[2 + z : 3 + z, 0:n]
                dc_ref[p + 2 : p + 3] = begin[z : z + 1, 0:n]
                dc_ref[p + 3 : p + 4] = after[z : z + 1, 0:n]
    dc_ref[48:128] = jnp.zeros((80, n), F32)
    columns = dc_ref[...].T
    lane = iota((n, 128), 1)
    sub = iota((8, m), 0)
    copies = []
    for f, (src, ref, dst) in enumerate(((e2_ref, e_ref, e_hbm), (h2_ref, h_ref, h_hbm))):
        for c in range(3):
            for z in range(2):
                p = 4 * (6 * f + 2 * c + z)
                moved = pltpu.roll(columns, (126 - p) % 128, 1)
                ref[c, z, :, 0:128] = src[c, z, :, 0:128] + jnp.where(lane < 2, moved, 0.0)
                ref[c, z, :, m - 128 : m] = src[c, z, :, m - 128 : m] + jnp.where(lane >= 126, moved, 0.0)
                ref[c, z, 0:8] += jnp.where(sub == 0, dr_ref[p + 2 : p + 3], jnp.where(sub == 1, dr_ref[p + 3 : p + 4], 0.0))
                ref[c, z, n - 8 : n] += jnp.where(sub == 6, dr_ref[p : p + 1], jnp.where(sub == 7, dr_ref[p + 1 : p + 2], 0.0))
            copies.append(pltpu.make_async_copy(ref.at[c], dst.at[c], sems.at[len(copies)]))
            copies[-1].start()

    gb0, gb1, ga = d["gb0"], d["gb1"], d["ga"]
    top = iota((8, rows), 0)
    gt_ref[0:8] = right[0:8] + jnp.where(top == 0, gb0[2:3], jnp.where(top == 1, gb1[2:3], 0.0))
    gt_ref[8:16] = right[8:16]
    gt_ref[16:24] = left[0:8]
    gt_ref[24:32] = left[8:16] + jnp.where(top == 7, ga[0:1], 0.0)
    gt_ref[32:40] = jnp.where(top == 0, gb0[0:1], jnp.where(top == 1, gb1[0:1], jnp.where(top == 2, ga[2:3], 0.0)))
    along = jnp.dot(gt_ref[...], band_ref[...], precision=HIGHEST, preferred_element_type=F32)
    extra = lax.dot_general(along, spread_ref[...], (((0,), (0,)), ((), ())), precision=HIGHEST, preferred_element_type=F32)
    out_ref[...] = inner_ref[...] + extra
    copies.append(pltpu.make_async_copy(out_ref, out_hbm, sems.at[len(copies)]))
    copies[-1].start()
    for copy in copies:
        copy.wait()


def swap_pairs(count, which):
    if which == 0:
        return [(i, i ^ 1) for i in range(count)]
    return [(i, (i - 1) % count if i % 2 == 0 else (i + 1) % count) for i in range(count)]


def call(kernel, shapes, ins, scratch=(), far=(), sems=0, far_out=False):
    vmem = pl.BlockSpec(memory_space=pltpu.VMEM)
    hbm = pl.BlockSpec(memory_space=pltpu.HBM)
    smem = pl.BlockSpec(memory_space=pltpu.SMEM)
    ins = [pltpu.with_memory_space_constraint(x, pltpu.HBM) if k in far else x for k, x in enumerate(ins)]
    scratches = [s if hasattr(s, "dtype") else pltpu.VMEM(s, F32) for s in scratch]
    if sems:
        scratches.append(pltpu.SemaphoreType.DMA((sems,)))
    return pl.pallas_call(
        kernel,
        out_shape=[s if hasattr(s, "dtype") else jax.ShapeDtypeStruct(s, F32) for s in shapes],
        in_specs=[hbm if k in far else smem if x.shape == (NMAT,) else vmem for k, x in enumerate(ins)],
        out_specs=[hbm if far_out else vmem] * len(shapes),
        scratch_shapes=scratches,
        compiler_params=pltpu.CompilerParams(vmem_limit_bytes=24 * 1024 * 1024),
    )(*ins)


def body(adj_e, adj_h, fwd_e, labels, eps_table, density):
    n, m = labels.shape
    block = adj_e.shape
    ins = [adj_e, adj_h, fwd_e, labels, density, eps_table]
    message = (2 * LO_ROWS + 8, 128)
    nz = block[1]
    strip = (2 * EXT, m)
    xa, xb, lo, hi, table = call(
        edge_kernel,
        [message, message, (LO_ROWS, m), (HI_ROWS, m), (NMAT, m)],
        ins,
        [(3, nz, *strip), (3, nz, *strip), (STEPS, 3, nz, *strip), pltpu.VMEM(strip, jnp.int32), strip, pltpu.SMEM((NMAT,), F32)],
        range(6),
        13,
    )
    gx, gy = lax.axis_size("gx"), lax.axis_size("gy")
    got_a = lax.ppermute(xa, "gx", swap_pairs(gx, 0))
    got_b = lax.ppermute(xb, "gx", swap_pairs(gx, 1))
    plo, phi, grad, e2, h1 = call(
        solve_kernel, [(LO_ROWS, n), (HI_ROWS, n), (n, m), block, block], ins[:-1] + [table]
    )
    column = (LO_ROWS, 2 * n)
    yhi, ylo, ext, dr = call(
        x_kernel,
        [column, column, (2 * n, m), (48, m)],
        [got_a, got_b, lo, hi, plo, phi, grad],
    )
    left = lax.ppermute(yhi, "gy", [(i, (i + 1) % gy) for i in range(gy)])
    right = lax.ppermute(ylo, "gy", [(i, (i - 1) % gy) for i in range(gy)])
    inner, h2, band, spread = call(inner_kernel, [(n, m), block, (2 * n, n), (40, m)], [ext, e2, h1])
    return tuple(
        call(
            y_kernel,
            [block, block, (n, m)],
            [left, right, ylo, yhi, dr, e2, h2, inner, band, spread],
            [(40, 2 * n), (128, n), (n, m), block, block],
            sems=7,
            far_out=True,
        )
    )


def solution(mesh):
    return jax.shard_map(
        body,
        mesh=mesh,
        in_specs=(
            P("design", None, "gx", "gy"),
            P("design", None, "gx", "gy"),
            P("design", None, None, "gx", "gy"),
            P(("design", "gx"), "gy"),
            P(),
            P(("design", "gx"), "gy"),
        ),
        out_specs=(
            P("design", None, "gx", "gy"),
            P("design", None, "gx", "gy"),
            P(("design", "gx"), "gy"),
        ),
        check_vma=False,
    )
```

```python
import math

import jax
import jax.numpy as jnp
from jax import lax
from jax.experimental import pallas as pl
from jax.experimental.pallas import tpu as pltpu
from jax.sharding import PartitionSpec as P

STEPS = 2
NMAT = 8
FILT = 16

courant = 0.5
spread_ratio = 0.6

F32 = jnp.float32
HIGHEST = lax.Precision.HIGHEST

LO_G, LO_E1T, LO_E1Z, LO_E2T, LO_E2Z = 0, 16, 18, 20, 22
LO_F0T, LO_F0Z, LO_F1T, LO_F1N, LO_F1Z = 24, 26, 28, 30, 32
LO_W1T, LO_W1Z, LO_R0, LO_R1, LO_ROWS = 34, 36, 38, 39, 40
HI_G, HI_H0T, HI_H0Z, HI_H1T, HI_H1Z = 0, 16, 18, 20, 22
HI_WT, HI_WN, HI_WZ, HI_R, HI_ROWS = 24, 26, 28, 30, 32
EXT = 24

PACK_F1, PACK_R, PACK_PAIR, PACK_F0, PACK_END = 16, 34, 37, 53, 57
LO_LANES = (
    list(range(FILT))
    + [PACK_PAIR + 2 * j + 1 for j in range(8)]
    + [PACK_F0 + j for j in range(4)]
    + [PACK_F1 + 3 * k + 1 for k in range(6)]
    + [PACK_F1 + 3 * k + 2 for k in (0, 1, 4, 5)]
    + [PACK_R + 1, PACK_R + 2]
)
HI_LANES = (
    list(range(128 - FILT, 128))
    + [PACK_PAIR + 2 * j for j in range(8)]
    + [PACK_F1 + 3 * k for k in range(6)]
    + [PACK_R, PACK_END]
)
CORNER = PACK_END - PACK_F1
REACH = FILT + 2


def tap(distance):
    spread = spread_ratio * FILT
    norm = math.sqrt(sum(math.exp(-d * d / (spread * spread)) for d in range(-FILT, FILT + 1)))
    far = distance.astype(F32)
    value = jnp.exp(-far * far / (2.0 * spread * spread)) / norm
    return jnp.where(jnp.abs(distance) <= FILT, value, F32(0.0))


def iota(shape, dim):
    return lax.broadcasted_iota(jnp.int32, shape, dim)


def updates(n, m, nz):
    row, col = iota((n, m), 0), iota((n, m), 1)

    def lx(f):
        return jnp.where(row == 0, 0.0, pltpu.roll(f, 1, 0))

    def ux(f):
        return jnp.where(row == n - 1, 0.0, pltpu.roll(f, n - 1, 0))

    def ly(f):
        return jnp.where(col == 0, 0.0, pltpu.roll(f, 1, 1))

    def uy(f):
        return jnp.where(col == m - 1, 0.0, pltpu.roll(f, m - 1, 1))

    def turn(h, ratio):
        out = [[None] * nz for _ in range(3)]
        for z in range(nz):
            hx, hy, hz = h[0][z], h[1][z], h[2][z]
            dzx = hx - h[0][z - 1] if z > 0 else hx
            dzy = hy - h[1][z - 1] if z > 0 else hy
            out[0][z] = ratio * ((hz - ly(hz)) - dzy)
            out[1][z] = ratio * (dzx - (hz - lx(hz)))
            out[2][z] = ratio * ((hy - lx(hy)) - (hx - ly(hx)))
        return out

    def magnetic(e, h):
        out = [[None] * nz for _ in range(3)]
        for z in range(nz):
            ex, ey, ez = e[0][z], e[1][z], e[2][z]
            dzx = e[0][z + 1] - ex if z < nz - 1 else -ex
            dzy = e[1][z + 1] - ey if z < nz - 1 else -ey
            out[0][z] = h[0][z] + courant * ((uy(ez) - ez) - dzy)
            out[1][z] = h[1][z] + courant * (dzx - (ux(ez) - ez))
            out[2][z] = h[2][z] + courant * ((ux(ey) - ey) - (uy(ex) - ex))
        return out

    return turn, magnetic


def less(e, change):
    return [[a - b for a, b in zip(one, other, strict=True)] for one, other in zip(e, change, strict=True)]


def product(e, f):
    total = None
    for c in range(3):
        for z in range(len(e[c])):
            term = e[c][z] * f[c][z]
            total = term if total is None else total + term
    return total


def local_solve(e0, h0, saved, ratio):
    turn, magnetic = updates(*ratio.shape, len(e0[0]))
    e1 = less(e0, turn(h0, ratio))
    h1 = magnetic(e1, h0)
    fwd = [saved(0)]
    grad = product(e1, fwd[0])
    e2 = less(e1, turn(h1, ratio))
    fwd.append(saved(1))
    grad = grad + product(e2, fwd[1])
    return e1, h1, e2, grad, fwd


def seam(sgn, a, b, up, down):
    odd = iota(a["h0t"].shape, 0) % 2 == 1
    half = sgn * courant

    def uz(f):
        return jnp.where(odd, 0.0, pltpu.roll(f, 7, 0))

    def lz(f):
        return jnp.where(odd, pltpu.roll(f, 1, 0), 0.0)

    rb, rb1, ra = sgn * b["r0"], sgn * b["r1"], sgn * a["r"]
    d = {}
    e1t = rb * a["h0z"]
    e1z = -rb * a["h0t"]
    e1t_b = b["e1t"] + e1t
    e1z_b = b["e1z"] + e1z
    ah1t = half * e1z_b
    ah1z = -half * e1t_b
    h1t_a = a["h1t"] + ah1t
    h1z_a = a["h1z"] + ah1z
    bh1t = -half * e1z
    bh1n = half * ((uz(e1t) - e1t) - (up(e1z) - e1z))
    bh1z = half * e1t
    e2t = e1t - rb * ((bh1z - h1z_a) - (bh1n - lz(bh1n)))
    e2n = -rb * ((bh1t - lz(bh1t)) - (bh1z - down(bh1z)))
    e2z = e1z - rb * ((bh1n - down(bh1n)) - (bh1t - h1t_a))
    f2t = rb1 * bh1z
    f2z = -rb1 * bh1t
    at = ah1z
    an = (ah1t - lz(ah1t)) - (ah1z - down(ah1z))
    az = -ah1t
    g2t, g2n, g2z = -ra * at, -ra * an, -ra * az
    gb0 = b["f0t"] * e1t + b["f0z"] * e1z + b["f1t"] * e2t + b["f1n"] * e2n + b["f1z"] * e2z
    gb1 = sgn * (b["w1t"] * bh1z - b["w1z"] * bh1t)
    ga = -sgn * (a["wt"] * at + a["wn"] * an + a["wz"] * az)
    e2t_b = b["e2t"] + e2t
    e2z_b = b["e2z"] + e2z
    d["b_e1z"], d["b_h1n"], d["b_h1z"], d["a_h1z"] = e1z, bh1n, bh1z, ah1z
    none = jnp.zeros_like(e1t)
    d["e"] = {"t": (none, g2t, e2t, f2t), "n": (none, g2n, e2n, none), "z": (none, g2z, e2z, f2z)}
    d["h"] = {
        "t": (
            half * g2z,
            ah1t + half * ((e2z_b - g2z) - (uz(g2n) - g2n)),
            bh1t + half * ((f2z - e2z) - (uz(e2n) - e2n)),
            -half * f2z,
        ),
        "n": (
            none,
            half * ((uz(g2t) - g2t) - (up(g2z) - g2z)),
            bh1n + half * ((uz(e2t) - e2t) - (up(e2z) - e2z)),
            half * ((uz(f2t) - f2t) - (up(f2z) - f2z)),
        ),
        "z": (
            -half * g2t,
            ah1z + half * ((up(g2n) - g2n) - (e2t_b - g2t)),
            bh1z + half * ((up(e2n) - e2n) - (f2t - e2t)),
            half * f2t,
        ),
    }
    d["gb0"], d["gb1"], d["ga"] = (g + pltpu.roll(g, 7, 0) for g in (gb0, gb1, ga))
    return d


def two(first, second, at, count=2):
    if count == 1:
        one, other = first[at : at + 1], second[at : at + 1]
        parts = [one, one, other, other]
    else:
        parts = [first[at : at + 2], second[at : at + 2]]
    parts.append(jnp.zeros((4, first.shape[1]), F32))
    return jnp.concatenate(parts, axis=0)


def seam_inputs(left_hi, my_hi, my_lo, right_lo):
    a = {
        "h0t": two(left_hi, my_hi, HI_H0T),
        "h0z": two(left_hi, my_hi, HI_H0Z),
        "h1t": two(left_hi, my_hi, HI_H1T),
        "h1z": two(left_hi, my_hi, HI_H1Z),
        "wt": two(left_hi, my_hi, HI_WT),
        "wn": two(left_hi, my_hi, HI_WN),
        "wz": two(left_hi, my_hi, HI_WZ),
        "r": two(left_hi, my_hi, HI_R, 1),
    }
    b = {
        "e1t": two(my_lo, right_lo, LO_E1T),
        "e1z": two(my_lo, right_lo, LO_E1Z),
        "e2t": two(my_lo, right_lo, LO_E2T),
        "e2z": two(my_lo, right_lo, LO_E2Z),
        "f0t": two(my_lo, right_lo, LO_F0T),
        "f0z": two(my_lo, right_lo, LO_F0Z),
        "f1t": two(my_lo, right_lo, LO_F1T),
        "f1n": two(my_lo, right_lo, LO_F1N),
        "f1z": two(my_lo, right_lo, LO_F1Z),
        "w1t": two(my_lo, right_lo, LO_W1T),
        "w1z": two(my_lo, right_lo, LO_W1Z),
        "r0": two(my_lo, right_lo, LO_R0, 1),
        "r1": two(my_lo, right_lo, LO_R1, 1),
    }
    return a, b


def even(axis):
    return lax.axis_index(axis) % 2 == 0


def ratio_of(labels, density, table):
    eps = jnp.broadcast_to(table[0], labels.shape)
    for k in range(1, NMAT):
        eps = jnp.where(labels == k, table[k], eps)
    return courant / (eps + density)


def planes(ref, *lead):
    return [[ref[(*lead, c, z)] for z in range(ref.shape[-3])] for c in range(3)]


def edge_lists(t, nrm, e1, h0, h1, e2, fwd, ratio):
    zs = range(len(e1[0]))
    lo = (
        [(e1[c][z], 0) for c in (t, 2) for z in zs]
        + [(e2[c][z], 0) for c in (t, 2) for z in zs]
        + [(fwd[0][c][z], 0) for c in (t, 2) for z in zs]
        + [(fwd[1][c][z], 0) for c in (t, nrm, 2) for z in zs]
        + [((ratio, fwd[1][c][z]), 1) for c in (t, 2) for z in zs]
        + [(ratio, 0), (ratio, 1)]
    )
    hi = (
        [(h0[c][z], -1) for c in (t, 2) for z in zs]
        + [(h1[c][z], -1) for c in (t, 2) for z in zs]
        + [((ratio, fwd[1][c][z]), -1) for c in (t, nrm, 2) for z in zs]
        + [(ratio, -1)]
    )
    return lo, hi


def fold(first, last):
    m = first.shape[1]
    lane = iota((first.shape[0], 128), 1)
    return jnp.where(lane < 64, first[:, 0:128], last[:, m - 128 : m])


def strips(grad):
    lane = iota((grad.shape[0], 128), 1)
    return jnp.where((lane < FILT) | (lane >= 128 - FILT), fold(grad, grad), 0.0)


def place(pack, values, base, count=3):
    lane = iota(pack.shape, 1)
    return jnp.where((lane >= base) & (lane < base + count), pltpu.roll(values, base + 1, 1), pack)


def pack_fields(pack, ratio, e1, h0, h1, e2):
    pack = place(pack, fold(ratio, ratio), PACK_R)
    for k, (first, last) in enumerate(((e1, h0), (e2, h1))):
        for j, (c, z) in enumerate((c, z) for c in (0, 2) for z in range(2)):
            pack = place(pack, fold(first[c][z], last[c][z]), PACK_PAIR + 8 * k + 2 * j, 2)
    return pack


def saved_scale(ratio):
    return jnp.where(iota((ratio.shape[0], 128), 1) == 0, 1.0, fold(ratio, ratio))


def pack_saved(pack, ratio, fwd):
    lane = iota(pack.shape, 1)
    for j, (c, z) in enumerate((c, z) for c in (0, 2) for z in range(2)):
        pack = jnp.where(lane == PACK_F0 + j, pltpu.roll(fwd[0][c][z][:, 0:128], PACK_F0 + j, 1), pack)
    scale = saved_scale(ratio)
    for k, (c, z) in enumerate((c, z) for c in range(3) for z in range(2)):
        pack = place(pack, fold(fwd[1][c][z], fwd[1][c][z]) * scale, PACK_F1 + 3 * k)
    return pack


def unpack_rows(packed, lanes, ref, at=0):
    ref[0:FILT, at : at + 128] = packed[lanes[0] : lanes[0] + FILT]
    for k in range(FILT, len(lanes)):
        ref[k : k + 1, at : at + 128] = packed[lanes[k] : lanes[k] + 1]


def edge_kernel(e_hbm, h_hbm, f_hbm, lab_hbm, den_hbm, eps_hbm,
                a_ref, b_ref, lo_ref, hi_ref, table_ref,
                e_ref, h_ref, f_ref, lab_ref, den_ref, tab_ref, sems):
    n, m = lab_hbm.shape
    nz = e_hbm.shape[1]
    copies = []

    def fetch(src, dst, *lead):
        for to, at in ((0, 0), (EXT, n - EXT)):
            copy = pltpu.make_async_copy(src.at[(*lead, pl.ds(at, EXT))], dst.at[(*lead, pl.ds(to, EXT))], sems.at[len(copies)])
            copy.start()
            copies.append(copy)

    every = slice(None)
    fetch(h_hbm, h_ref, every, every)
    fetch(lab_hbm, lab_ref)
    fetch(den_hbm, den_ref)
    copies.append(pltpu.make_async_copy(eps_hbm, tab_ref, sems.at[len(copies)]))
    copies[-1].start()
    fetch(e_hbm, e_ref, every, every)
    for step in range(STEPS):
        fetch(f_hbm, f_ref, step, every, every)

    def wait(first, last):
        for copy in copies[first:last]:
            copy.wait()

    turn, magnetic = updates(2 * EXT, m, nz)
    wait(2, 7)
    ratio = ratio_of(lab_ref[...], den_ref[...], tab_ref)
    wait(0, 2)
    h0 = planes(h_ref)
    change = turn(h0, ratio)
    wait(7, 9)
    e1 = less(planes(e_ref), change)
    h1 = magnetic(e1, h0)
    e2 = less(e1, turn(h1, ratio))
    lane = iota((8, 128), 1)
    corners = [[jnp.zeros((8, 128), F32) for _ in range(3)] for _ in range(2)]

    def put_corner(values, base, first=0, count=3):
        for end in range(2):
            for k in range(3):
                at = CORNER * k + base - PACK_F1
                tile = values[EXT * end + 8 * k : EXT * end + 8 * k + 8]
                moved = pltpu.roll(tile, (at + 1) % 128, 1)
                corners[end][k] = jnp.where((lane >= at + first) & (lane < at + count), moved, corners[end][k])

    sides = [(c, z) for c in (0, 2) for z in range(nz)]
    put_corner(fold(ratio, ratio), PACK_R)
    for j, (c, z) in enumerate(sides):
        put_corner(fold(e1[c][z], h0[c][z]), PACK_PAIR + 2 * j, 0, 2)
        put_corner(h1[c][z][:, m - 128 : m], PACK_PAIR + 8 + 2 * j, 0, 1)
    wait(9, 11)
    fwd = [planes(f_ref, 0)]
    grad = product(e1, fwd[0])
    for j, (c, z) in enumerate(sides):
        put_corner(fwd[0][c][z][:, 0:128], PACK_F0 + j - 1, 1, 2)
    wait(11, 13)
    fwd.append(planes(f_ref, 1))
    grad = grad + product(e2, fwd[1])
    scale = saved_scale(ratio)
    for k, (c, z) in enumerate((c, z) for c in range(3) for z in range(nz)):
        put_corner(fold(fwd[1][c][z], fwd[1][c][z]) * scale, PACK_F1 + 3 * k)
    rows = 2 * EXT

    def line(item, at):
        if isinstance(item, tuple):
            return line(item[0], at) * line(item[1], at)
        at = at % rows
        return item[at : at + 1]

    lo, hi = edge_lists(1, 0, e1, h0, h1, e2, fwd, ratio)
    for ref, group, strip in ((hi_ref, hi, grad[rows - FILT : rows]), (lo_ref, lo, grad[0:FILT])):
        ref[0:FILT] = strip
        for k, (item, at) in enumerate(group):
            ref[FILT + k : FILT + k + 1] = line(item, at)
    hi_ref[HI_ROWS - 1 : HI_ROWS] = jnp.zeros((1, m), F32)
    first_even = even("gx")
    lo_corner, hi_corner = (
        jnp.where(lane < CORNER, part[0], jnp.where(lane < 2 * CORNER, part[1], part[2])) for part in corners
    )
    for half in range(2):
        at, cols = half * LO_ROWS, slice(128 * half, 128 * half + 128)
        low, high = lo_ref[:, cols], hi_ref[:, cols]
        high = jnp.concatenate([high, jnp.zeros((LO_ROWS - HI_ROWS, 128), F32)], axis=0)
        a_ref[at : at + LO_ROWS] = jnp.where(first_even, high, low)
        b_ref[at : at + LO_ROWS] = jnp.where(first_even, low, high)
    a_ref[2 * LO_ROWS :] = jnp.where(first_even, hi_corner, lo_corner)
    b_ref[2 * LO_ROWS :] = jnp.where(first_even, lo_corner, hi_corner)
    for k in range(NMAT):
        table_ref[k : k + 1] = jnp.full((1, m), tab_ref[k], F32)


def solve_kernel(e_ref, h_ref, f_ref, lab_ref, den_ref, table_ref, lo_ref, hi_ref, grad_ref, e2_ref, h1_ref):
    ratio = ratio_of(lab_ref[...], den_ref[...], [table_ref[k : k + 1] for k in range(NMAT)])
    h0 = planes(h_ref)
    e1, h1, e2, grad, fwd = local_solve(planes(e_ref), h0, lambda step: planes(f_ref, step), ratio)
    for c in range(3):
        for z in range(e_ref.shape[1]):
            e2_ref[c, z] = e2[c][z]
            h1_ref[c, z] = h1[c][z]
    grad_ref[...] = grad
    packed = pack_saved(pack_fields(strips(grad), ratio, e1, h0, h1, e2), ratio, fwd).T
    unpack_rows(packed, LO_LANES, lo_ref)
    unpack_rows(packed, HI_LANES, hi_ref)


def x_kernel(ra_ref, rb_ref, lo_ref, hi_ref, plo_ref, phi_ref, grad_ref,
             yhi_ref, down_ref, ylo_ref, ext_ref, dr_ref):
    n, m = grad_ref.shape
    first_even = even("gx")
    got_right = jnp.where(first_even, ra_ref[...], rb_ref[...])
    got_left = jnp.where(first_even, rb_ref[...], ra_ref[...])
    right, left = (jnp.concatenate([got[0:LO_ROWS], got[LO_ROWS : 2 * LO_ROWS]], axis=1) for got in (got_right, got_left))
    a, b = seam_inputs(left, hi_ref[...], lo_ref[...], right)
    col = iota((8, m), 1)
    d = seam(
        -1.0, a, b,
        lambda f: jnp.where(col == m - 1, 0.0, pltpu.roll(f, m - 1, 1)),
        lambda f: jnp.where(col == 0, 0.0, pltpu.roll(f, 1, 1)),
    )
    for f, field in enumerate(("e", "h")):
        for c, name in enumerate(("n", "t", "z")):
            before, end, begin, after = d[field][name]
            for z in range(2):
                p = 4 * (6 * f + 2 * c + z)
                dr_ref[p : p + 1] = before[2 + z : 3 + z]
                dr_ref[p + 1 : p + 2] = end[2 + z : 3 + z]
                dr_ref[p + 2 : p + 3] = begin[z : z + 1]
                dr_ref[p + 3 : p + 4] = after[z : z + 1]
    gb0, gb1, ga = d["gb0"], d["gb1"], d["ga"]
    top = iota((8, m), 0)
    ext_ref[0:n] = grad_ref[...]
    ext_ref[0:8] = grad_ref[0:8] + jnp.where(top == 0, gb0[0:1], jnp.where(top == 1, gb1[0:1], 0.0))
    ext_ref[n - 8 : n] = grad_ref[n - 8 : n] + jnp.where(top == 7, ga[2:3], 0.0)
    ext_ref[n : n + 8] = right[0:8] + jnp.where(top == 0, gb0[2:3], jnp.where(top == 1, gb1[2:3], 0.0))
    ext_ref[n + 8 : n + 16] = right[8:16]
    ext_ref[n + 16 : 2 * n - 16] = jnp.zeros((n - 32, m), F32)
    ext_ref[2 * n - 16 : 2 * n - 8] = left[0:8]
    ext_ref[2 * n - 8 : 2 * n] = left[8:16] + jnp.where(top == 7, ga[0:1], 0.0)

    lane = iota((1, 128), 1)

    def put(row_vec, lanes, at, value, seam_row, c):
        for z in range(2):
            one = value[seam_row + z : seam_row + z + 1, c : c + 1]
            row_vec = jnp.where(lane == lanes[at + z], one, row_vec)
        return row_vec

    row0 = put(strips(gb0[0:1]), LO_LANES, LO_E1Z, d["b_e1z"], 0, 0)
    row0 = put(row0, LO_LANES, LO_E2T, d["e"]["n"][2], 0, 0)
    row0 = put(row0, LO_LANES, LO_E2Z, d["e"]["z"][2], 0, 0)
    row0 = put(row0, HI_LANES, HI_H1T, d["b_h1n"], 0, m - 1)
    row0 = put(row0, HI_LANES, HI_H1Z, d["b_h1z"], 0, m - 1)
    row1 = put(strips(gb1[0:1]), LO_LANES, LO_E2Z, d["e"]["z"][3], 0, 0)
    end = put(strips(ga[2:3]), LO_LANES, LO_E2T, d["e"]["n"][1], 2, 0)
    end = put(end, LO_LANES, LO_E2Z, d["e"]["z"][1], 2, 0)
    end = put(end, HI_LANES, HI_H1Z, d["a_h1z"], 2, m - 1)
    none = jnp.zeros((1, 128), F32)
    out0 = put(none, LO_LANES, LO_E1Z, d["b_e1z"], 2, 0)
    out0 = put(out0, HI_LANES, HI_H1T, d["b_h1n"], 2, m - 1)
    out0 = put(out0, HI_LANES, HI_H1Z, d["b_h1z"], 2, m - 1)
    before = put(none, HI_LANES, HI_H1Z, d["a_h1z"], 0, m - 1)

    sub = iota((8, 128), 0)
    wide = iota((8, 128), 1)

    def corner(message, first_row):
        tile = message[2 * LO_ROWS : 2 * LO_ROWS + 8]
        out = []
        for k in range(3):
            moved = pltpu.roll(tile, (PACK_F1 - CORNER * k) % 128, 1)
            part = jnp.where((wide >= PACK_F1) & (wide < PACK_END), moved, 0.0)
            at = first_row + 8 * k
            if n <= at < n + FILT or at >= 2 * n - FILT:
                part = part + strips(ext_ref[at : at + 8])
            out.append(part)
        return out

    above, below = corner(got_right, n), corner(got_left, 2 * n - EXT)
    above[0] = above[0] + jnp.where(sub == 0, out0, 0.0)
    below[2] = below[2] + jnp.where(sub == 7, before, 0.0)
    own = jnp.where(sub == 0, end, jnp.where(sub == 1, row0, jnp.where(sub == 2, row1, 0.0)))
    filler = jnp.zeros((8, 128), F32)
    used = EXT // 8
    tiles = above + [own] + [filler] * (n // 8 - 2 * used - 1) + below
    packed = jnp.concatenate(tiles, axis=0).T
    for ref, mine, lanes in ((ylo_ref, plo_ref, LO_LANES), (yhi_ref, phi_ref, HI_LANES)):
        count = len(lanes)
        unpack_rows(packed, lanes, ref, n)
        at = iota((count, n), 1)
        moved = pltpu.roll(ref[0:count, n : 2 * n], (n - EXT - 1) % n, 1)
        ref[0:count, 0:n] = mine[...] + jnp.where((at < 2) | (at == n - 1), moved, 0.0)
    down_ref[0:LO_ROWS] = ylo_ref[:, 0:n]
    for k in range(LO_ROWS // 8):
        moved = pltpu.roll(ylo_ref[8 * k : 8 * k + 8, n : 2 * n], REACH + 2 * REACH * (k % 3), 1)
        at = LO_ROWS + 8 * (k // 3)
        down_ref[at : at + 8] = moved if k % 3 == 0 else jnp.where(wide < 2 * REACH * (k % 3), down_ref[at : at + 8], moved)


def cyclic(d, count):
    return jnp.where(d > count // 2, d - count, jnp.where(d < -(count // 2), d + count, d))


def inner_kernel(ext_ref, e2_ref, h1_ref, out_ref, h2_ref, band_ref, spread_ref):
    rows, m = ext_ref.shape
    n = out_ref.shape[0]
    nz = e2_ref.shape[1]
    _, magnetic = updates(n, m, nz)
    h2 = magnetic(planes(e2_ref), planes(h1_ref))
    for c in range(3):
        for z in range(nz):
            h2_ref[c, z] = h2[c][z]
    band = tap(cyclic(iota((n, rows), 1) - iota((n, rows), 0), rows))
    along = jnp.dot(band, ext_ref[...], precision=HIGHEST, preferred_element_type=F32)
    out_ref[...] = jnp.dot(along, tap(iota((m, m), 0) - iota((m, m), 1)), precision=HIGHEST, preferred_element_type=F32)
    band_ref[...] = tap(cyclic(iota((rows, n), 0) - iota((rows, n), 1), rows))
    k = iota(spread_ref.shape, 0)
    column = jnp.where(k < FILT, m + k, jnp.where(k < 2 * FILT + 2, k - 2 * FILT, m - 1))
    spread_ref[...] = jnp.where(k < 2 * FILT + 3, tap(column - iota(spread_ref.shape, 1)), 0.0)


def y_kernel(left_ref, right_ref, lo_ref, hi_ref, dr_ref, e2_ref, h2_ref, inner_ref, band_ref, spread_ref,
             e_hbm, h_hbm, out_hbm, gt_ref, dc_ref, out_ref, e_ref, h_ref, sems):
    n, m = inner_ref.shape
    left = left_ref[...]
    rows = left.shape[1]
    tile_lane = iota((8, 128), 1)
    outer = []
    for k in range(LO_ROWS // 8):
        at = LO_ROWS + 8 * (k // 3)
        moved = pltpu.roll(right_ref[at : at + 8], 128 - REACH - 2 * REACH * (k % 3), 1)
        outer.append(jnp.where((tile_lane < REACH) | (tile_lane >= 128 - REACH), moved, 0.0))
    right = jnp.concatenate([right_ref[0:LO_ROWS], jnp.concatenate(outer, axis=0)], axis=1)
    a, b = seam_inputs(left, hi_ref[...], lo_ref[...], right)
    d = seam(1.0, a, b, lambda f: pltpu.roll(f, rows - 1, 1), lambda f: pltpu.roll(f, 1, 1))

    for f, field in enumerate(("e", "h")):
        for c, name in enumerate(("t", "n", "z")):
            before, end, begin, after = d[field][name]
            for z in range(2):
                p = 4 * (6 * f + 2 * c + z)
                dc_ref[p : p + 1] = before[2 + z : 3 + z, 0:n]
                dc_ref[p + 1 : p + 2] = end[2 + z : 3 + z, 0:n]
                dc_ref[p + 2 : p + 3] = begin[z : z + 1, 0:n]
                dc_ref[p + 3 : p + 4] = after[z : z + 1, 0:n]
    dc_ref[48:128] = jnp.zeros((80, n), F32)
    columns = dc_ref[...].T
    lane = iota((n, 128), 1)
    sub = iota((8, m), 0)
    copies = []
    for f, (src, ref, dst) in enumerate(((e2_ref, e_ref, e_hbm), (h2_ref, h_ref, h_hbm))):
        for c in range(3):
            for z in range(2):
                p = 4 * (6 * f + 2 * c + z)
                moved = pltpu.roll(columns, (126 - p) % 128, 1)
                ref[c, z, :, 0:128] = src[c, z, :, 0:128] + jnp.where(lane < 2, moved, 0.0)
                ref[c, z, :, m - 128 : m] = src[c, z, :, m - 128 : m] + jnp.where(lane >= 126, moved, 0.0)
                ref[c, z, 0:8] += jnp.where(sub == 0, dr_ref[p + 2 : p + 3], jnp.where(sub == 1, dr_ref[p + 3 : p + 4], 0.0))
                ref[c, z, n - 8 : n] += jnp.where(sub == 6, dr_ref[p : p + 1], jnp.where(sub == 7, dr_ref[p + 1 : p + 2], 0.0))
                copies.append(pltpu.make_async_copy(ref.at[c, z], dst.at[c, z], sems.at[len(copies)]))
                copies[-1].start()

    gb0, gb1, ga = d["gb0"], d["gb1"], d["ga"]
    top = iota((8, rows), 0)
    gt_ref[0:8] = right[0:8] + jnp.where(top == 0, gb0[2:3], jnp.where(top == 1, gb1[2:3], 0.0))
    gt_ref[8:16] = right[8:16]
    gt_ref[16:24] = left[0:8]
    gt_ref[24:32] = left[8:16] + jnp.where(top == 7, ga[0:1], 0.0)
    gt_ref[32:40] = jnp.where(top == 0, gb0[0:1], jnp.where(top == 1, gb1[0:1], jnp.where(top == 2, ga[2:3], 0.0)))
    along = jnp.dot(gt_ref[...], band_ref[...], precision=HIGHEST, preferred_element_type=F32)
    extra = lax.dot_general(along, spread_ref[...], (((0,), (0,)), ((), ())), precision=HIGHEST, preferred_element_type=F32)
    out_ref[...] = inner_ref[...] + extra
    copies.append(pltpu.make_async_copy(out_ref, out_hbm, sems.at[len(copies)]))
    copies[-1].start()
    for copy in copies:
        copy.wait()


def swap_pairs(count, which):
    if which == 0:
        return [(i, i ^ 1) for i in range(count)]
    return [(i, (i - 1) % count if i % 2 == 0 else (i + 1) % count) for i in range(count)]


def call(kernel, shapes, ins, scratch=(), far=(), sems=0, far_out=False):
    vmem = pl.BlockSpec(memory_space=pltpu.VMEM)
    hbm = pl.BlockSpec(memory_space=pltpu.HBM)
    smem = pl.BlockSpec(memory_space=pltpu.SMEM)
    ins = [pltpu.with_memory_space_constraint(x, pltpu.HBM) if k in far else x for k, x in enumerate(ins)]
    scratches = [s if hasattr(s, "dtype") else pltpu.VMEM(s, F32) for s in scratch]
    if sems:
        scratches.append(pltpu.SemaphoreType.DMA((sems,)))
    return pl.pallas_call(
        kernel,
        out_shape=[s if hasattr(s, "dtype") else jax.ShapeDtypeStruct(s, F32) for s in shapes],
        in_specs=[hbm if k in far else smem if x.shape == (NMAT,) else vmem for k, x in enumerate(ins)],
        out_specs=[hbm if far_out else vmem] * len(shapes),
        scratch_shapes=scratches,
        compiler_params=pltpu.CompilerParams(vmem_limit_bytes=24 * 1024 * 1024),
    )(*ins)


def body(adj_e, adj_h, fwd_e, labels, eps_table, density):
    n, m = labels.shape
    block = adj_e.shape
    ins = [adj_e, adj_h, fwd_e, labels, density, eps_table]
    message = (2 * LO_ROWS + 8, 128)
    nz = block[1]
    strip = (2 * EXT, m)
    xa, xb, lo, hi, table = call(
        edge_kernel,
        [message, message, (LO_ROWS, m), (HI_ROWS, m), (NMAT, m)],
        ins,
        [(3, nz, *strip), (3, nz, *strip), (STEPS, 3, nz, *strip), pltpu.VMEM(strip, jnp.int32), strip, pltpu.SMEM((NMAT,), F32)],
        range(6),
        13,
    )
    gx, gy = lax.axis_size("gx"), lax.axis_size("gy")
    got_a = lax.ppermute(xa, "gx", swap_pairs(gx, 0))
    got_b = lax.ppermute(xb, "gx", swap_pairs(gx, 1))
    plo, phi, grad, e2, h1 = call(
        solve_kernel, [(LO_ROWS, n), (HI_ROWS, n), (n, m), block, block], ins[:-1] + [table]
    )
    yhi, down, ylo, ext, dr = call(
        x_kernel,
        [(HI_ROWS, 2 * n), (LO_ROWS + 16, n), (LO_ROWS, 2 * n), (2 * n, m), (48, m)],
        [got_a, got_b, lo, hi, plo, phi, grad],
    )
    left = lax.ppermute(yhi, "gy", [(i, (i + 1) % gy) for i in range(gy)])
    right = lax.ppermute(down, "gy", [(i, (i - 1) % gy) for i in range(gy)])
    inner, h2, band, spread = call(inner_kernel, [(n, m), block, (2 * n, n), (40, m)], [ext, e2, h1])
    return tuple(
        call(
            y_kernel,
            [block, block, (n, m)],
            [left, right, ylo, yhi, dr, e2, h2, inner, band, spread],
            [(40, 2 * n), (128, n), (n, m), block, block],
            sems=13,
            far_out=True,
        )
    )


def solution(mesh):
    return jax.shard_map(
        body,
        mesh=mesh,
        in_specs=(
            P("design", None, "gx", "gy"),
            P("design", None, "gx", "gy"),
            P("design", None, None, "gx", "gy"),
            P(("design", "gx"), "gy"),
            P(),
            P(("design", "gx"), "gy"),
        ),
        out_specs=(
            P("design", None, "gx", "gy"),
            P("design", None, "gx", "gy"),
            P(("design", "gx"), "gy"),
        ),
        check_vma=False,
    )
```

```python
import math

import jax
import jax.numpy as jnp
from jax import lax
from jax.experimental import pallas as pl
from jax.experimental.pallas import tpu as pltpu
from jax.sharding import PartitionSpec as P

STEPS = 2
NMAT = 8
FILT = 16

courant = 0.5
spread_ratio = 0.6

F32 = jnp.float32

LO_G, LO_E1T, LO_E1Z, LO_E2T, LO_E2Z = 0, 16, 18, 20, 22
LO_F0T, LO_F0Z, LO_F1T, LO_F1N, LO_F1Z = 24, 26, 28, 30, 32
LO_W1T, LO_W1Z, LO_R0, LO_R1, LO_ROWS = 34, 36, 38, 39, 40
HI_G, HI_H0T, HI_H0Z, HI_H1T, HI_H1Z = 0, 16, 18, 20, 22
HI_WT, HI_WN, HI_WZ, HI_R, HI_ROWS = 24, 26, 28, 30, 32
PACK_F1, PACK_R, PACK_PAIR, PACK_F0, PACK_END = 16, 34, 37, 53, 57
LO_LANES = (
    list(range(FILT))
    + [PACK_PAIR + 2 * j + 1 for j in range(8)]
    + [PACK_F0 + j for j in range(4)]
    + [PACK_F1 + 3 * k + 1 for k in range(6)]
    + [PACK_F1 + 3 * k + 2 for k in (0, 1, 4, 5)]
    + [PACK_R + 1, PACK_R + 2]
)
HI_LANES = (
    list(range(128 - FILT, 128))
    + [PACK_PAIR + 2 * j for j in range(8)]
    + [PACK_F1 + 3 * k for k in range(6)]
    + [PACK_R, PACK_END]
)
REACH = FILT + 2
GROUP = 24
EDGE = 24
LO_REST, HI_REST = LO_ROWS - FILT, HI_ROWS - FILT - 1

TURN_G, TURN_OWN, TURN_X = 48, 80, 88


def filter_taps():
    spread = spread_ratio * FILT
    norm = math.sqrt(sum(math.exp(-d * d / (spread * spread)) for d in range(-FILT, FILT + 1)))
    return [math.exp(-d * d / (2.0 * spread * spread)) / norm for d in range(FILT + 1)]


def tap(distance):
    spread = spread_ratio * FILT
    norm = math.sqrt(sum(math.exp(-d * d / (spread * spread)) for d in range(-FILT, FILT + 1)))
    far = distance.astype(F32)
    value = jnp.exp(-far * far / (2.0 * spread * spread)) / norm
    return jnp.where(jnp.abs(distance) <= FILT, value, F32(0.0))


def halves(x):
    high = x.astype(jnp.bfloat16)
    return high, (x - high.astype(F32)).astype(jnp.bfloat16)


def dot3(a, b):
    terms = [jnp.dot(x, y, preferred_element_type=F32) for x, y in ((a[0], b[1]), (a[1], b[0]), (a[0], b[0]))]
    return terms[0] + terms[1] + terms[2]


def iota(shape, dim):
    return lax.broadcasted_iota(jnp.int32, shape, dim)


def updates(n, m, nz):
    row, col = iota((n, m), 0), iota((n, m), 1)

    def lx(f):
        return jnp.where(row == 0, 0.0, pltpu.roll(f, 1, 0))

    def ux(f):
        return jnp.where(row == n - 1, 0.0, pltpu.roll(f, n - 1, 0))

    def ly(f):
        return jnp.where(col == 0, 0.0, pltpu.roll(f, 1, 1))

    def uy(f):
        return jnp.where(col == m - 1, 0.0, pltpu.roll(f, m - 1, 1))

    def turn(h, ratio):
        out = [[None] * nz for _ in range(3)]
        for z in range(nz):
            hx, hy, hz = h[0][z], h[1][z], h[2][z]
            dzx = hx - h[0][z - 1] if z > 0 else hx
            dzy = hy - h[1][z - 1] if z > 0 else hy
            out[0][z] = ratio * ((hz - ly(hz)) - dzy)
            out[1][z] = ratio * (dzx - (hz - lx(hz)))
            out[2][z] = ratio * ((hy - lx(hy)) - (hx - ly(hx)))
        return out

    def magnetic(e, h):
        out = [[None] * nz for _ in range(3)]
        for z in range(nz):
            ex, ey, ez = e[0][z], e[1][z], e[2][z]
            dzx = e[0][z + 1] - ex if z < nz - 1 else -ex
            dzy = e[1][z + 1] - ey if z < nz - 1 else -ey
            out[0][z] = h[0][z] + courant * ((uy(ez) - ez) - dzy)
            out[1][z] = h[1][z] + courant * (dzx - (ux(ez) - ez))
            out[2][z] = h[2][z] + courant * ((ux(ey) - ey) - (uy(ex) - ex))
        return out

    return turn, magnetic


def less(e, change):
    return [[a - b for a, b in zip(one, other, strict=True)] for one, other in zip(e, change, strict=True)]


def product(e, f):
    total = None
    for c in range(3):
        for z in range(len(e[c])):
            term = e[c][z] * f[c][z]
            total = term if total is None else total + term
    return total


def local_solve(e0, h0, saved, ratio):
    turn, magnetic = updates(*ratio.shape, len(e0[0]))
    e1 = less(e0, turn(h0, ratio))
    h1 = magnetic(e1, h0)
    fwd = [saved(0)]
    grad = product(e1, fwd[0])
    e2 = less(e1, turn(h1, ratio))
    fwd.append(saved(1))
    grad = grad + product(e2, fwd[1])
    return e1, h1, e2, grad, fwd


def seam(sgn, a, b, up, down):
    odd = iota(a["h0t"].shape, 0) % 2 == 1
    half = sgn * courant

    def uz(f):
        return jnp.where(odd, 0.0, pltpu.roll(f, 7, 0))

    def lz(f):
        return jnp.where(odd, pltpu.roll(f, 1, 0), 0.0)

    rb, rb1, ra = sgn * b["r0"], sgn * b["r1"], sgn * a["r"]
    d = {}
    e1t = rb * a["h0z"]
    e1z = -rb * a["h0t"]
    e1t_b = b["e1t"] + e1t
    e1z_b = b["e1z"] + e1z
    ah1t = half * e1z_b
    ah1z = -half * e1t_b
    h1t_a = a["h1t"] + ah1t
    h1z_a = a["h1z"] + ah1z
    bh1t = -half * e1z
    bh1n = half * ((uz(e1t) - e1t) - (up(e1z) - e1z))
    bh1z = half * e1t
    e2t = e1t - rb * ((bh1z - h1z_a) - (bh1n - lz(bh1n)))
    e2n = -rb * ((bh1t - lz(bh1t)) - (bh1z - down(bh1z)))
    e2z = e1z - rb * ((bh1n - down(bh1n)) - (bh1t - h1t_a))
    f2t = rb1 * bh1z
    f2z = -rb1 * bh1t
    at = ah1z
    an = (ah1t - lz(ah1t)) - (ah1z - down(ah1z))
    az = -ah1t
    g2t, g2n, g2z = -ra * at, -ra * an, -ra * az
    gb0 = b["f0t"] * e1t + b["f0z"] * e1z + b["f1t"] * e2t + b["f1n"] * e2n + b["f1z"] * e2z
    gb1 = sgn * (b["w1t"] * bh1z - b["w1z"] * bh1t)
    ga = -sgn * (a["wt"] * at + a["wn"] * an + a["wz"] * az)
    e2t_b = b["e2t"] + e2t
    e2z_b = b["e2z"] + e2z
    d["b_e1z"], d["b_h1n"], d["b_h1z"], d["a_h1z"] = e1z, bh1n, bh1z, ah1z
    none = jnp.zeros_like(e1t)
    d["e"] = {"t": (none, g2t, e2t, f2t), "n": (none, g2n, e2n, none), "z": (none, g2z, e2z, f2z)}
    d["h"] = {
        "t": (
            half * g2z,
            ah1t + half * ((e2z_b - g2z) - (uz(g2n) - g2n)),
            bh1t + half * ((f2z - e2z) - (uz(e2n) - e2n)),
            -half * f2z,
        ),
        "n": (
            none,
            half * ((uz(g2t) - g2t) - (up(g2z) - g2z)),
            bh1n + half * ((uz(e2t) - e2t) - (up(e2z) - e2z)),
            half * ((uz(f2t) - f2t) - (up(f2z) - f2z)),
        ),
        "z": (
            -half * g2t,
            ah1z + half * ((up(g2n) - g2n) - (e2t_b - g2t)),
            bh1z + half * ((up(e2n) - e2n) - (f2t - e2t)),
            half * f2t,
        ),
    }
    d["gb0"], d["gb1"], d["ga"] = (g + pltpu.roll(g, 7, 0) for g in (gb0, gb1, ga))
    return d


def two(first, second, at, count=2):
    if count == 1:
        one, other = first[at : at + 1], second[at : at + 1]
        parts = [one, one, other, other]
    else:
        parts = [first[at : at + 2], second[at : at + 2]]
    parts.append(jnp.zeros((4, first.shape[1]), F32))
    return jnp.concatenate(parts, axis=0)


def seam_inputs(left_hi, my_hi, my_lo, right_lo):
    a = {
        "h0t": two(left_hi, my_hi, HI_H0T),
        "h0z": two(left_hi, my_hi, HI_H0Z),
        "h1t": two(left_hi, my_hi, HI_H1T),
        "h1z": two(left_hi, my_hi, HI_H1Z),
        "wt": two(left_hi, my_hi, HI_WT),
        "wn": two(left_hi, my_hi, HI_WN),
        "wz": two(left_hi, my_hi, HI_WZ),
        "r": two(left_hi, my_hi, HI_R, 1),
    }
    b = {
        "e1t": two(my_lo, right_lo, LO_E1T),
        "e1z": two(my_lo, right_lo, LO_E1Z),
        "e2t": two(my_lo, right_lo, LO_E2T),
        "e2z": two(my_lo, right_lo, LO_E2Z),
        "f0t": two(my_lo, right_lo, LO_F0T),
        "f0z": two(my_lo, right_lo, LO_F0Z),
        "f1t": two(my_lo, right_lo, LO_F1T),
        "f1n": two(my_lo, right_lo, LO_F1N),
        "f1z": two(my_lo, right_lo, LO_F1Z),
        "w1t": two(my_lo, right_lo, LO_W1T),
        "w1z": two(my_lo, right_lo, LO_W1Z),
        "r0": two(my_lo, right_lo, LO_R0, 1),
        "r1": two(my_lo, right_lo, LO_R1, 1),
    }
    return a, b


def even(axis):
    return lax.axis_index(axis) % 2 == 0


def ratio_of(labels, density, table):
    eps = jnp.broadcast_to(table[0], labels.shape)
    for k in range(1, NMAT):
        eps = jnp.where(labels == k, table[k], eps)
    return courant / (eps + density)


def planes(ref, *lead):
    return [[ref[(*lead, c, z)] for z in range(ref.shape[-3])] for c in range(3)]


def edge_lists(t, nrm, e1, h0, h1, e2, fwd, ratio):
    zs = range(len(e1[0]))
    lo = (
        [(e1[c][z], 0) for c in (t, 2) for z in zs]
        + [(e2[c][z], 0) for c in (t, 2) for z in zs]
        + [(fwd[0][c][z], 0) for c in (t, 2) for z in zs]
        + [(fwd[1][c][z], 0) for c in (t, nrm, 2) for z in zs]
        + [((ratio, fwd[1][c][z]), 1) for c in (t, 2) for z in zs]
        + [(ratio, 0), (ratio, 1)]
    )
    hi = (
        [(h0[c][z], -1) for c in (t, 2) for z in zs]
        + [(h1[c][z], -1) for c in (t, 2) for z in zs]
        + [((ratio, fwd[1][c][z]), -1) for c in (t, nrm, 2) for z in zs]
        + [(ratio, -1)]
    )
    return lo, hi


def fold(plane):
    m = plane.shape[1]
    lane = iota((plane.shape[0], 128), 1)
    return jnp.where(lane < 64, plane[:, 0:128], plane[:, m - 128 : m])


def place(pack, values, base, count=3):
    lane = iota(pack.shape, 1)
    return jnp.where((lane >= base) & (lane < base + count), pltpu.roll(values, base + 1, 1), pack)


def unpack_rows(packed, lanes, ref):
    ref[0:FILT] = packed[lanes[0] : lanes[0] + FILT]
    for k in range(FILT, len(lanes)):
        ref[k : k + 1] = packed[lanes[k] : lanes[k] + 1]


def line(item, at):
    if isinstance(item, tuple):
        return line(item[0], at) * line(item[1], at)
    at = at % item.shape[0]
    return item[at : at + 1]


def side_by_side(tiles, width, first):
    lane = iota((8, 128), 1)
    out = None
    for k, tile in enumerate(tiles):
        moved = pltpu.roll(tile, (width * k - first) % 128, 1)
        out = moved if out is None else jnp.where(lane < width * k, out, moved)
    return out


def first_kernel(e_hbm, h_hbm, f_hbm, lab_hbm, den_hbm, eps_hbm,
                 up_ref, down_ref, lo_ref, hi_ref, e_ref, h_ref, f_ref, lab_ref, den_ref, table_ref,
                 tab_ref, sems):
    n, m = lab_hbm.shape
    nz = e_hbm.shape[1]
    copies = []
    for src, dst in ((h_hbm, h_ref), (lab_hbm, lab_ref), (den_hbm, den_ref), (eps_hbm, tab_ref), (e_hbm, e_ref),
                     (f_hbm.at[0], f_ref.at[0]), (f_hbm.at[1], f_ref.at[1])):
        copies.append(pltpu.make_async_copy(src, dst, sems.at[len(copies)]))
        copies[-1].start()

    def folded(ref, *lead):
        return [[fold(plane) for plane in comp] for comp in planes(ref, *lead)]

    turn, magnetic = updates(n, 128, nz)
    sides = [(c, z) for c in (0, 2) for z in range(nz)]
    lane = iota((n, 128), 1)
    for copy in copies[1:4]:
        copy.wait()
    ratio = ratio_of(fold(lab_ref[...]), fold(den_ref[...]), tab_ref)
    copies[0].wait()
    h0 = folded(h_ref)
    change = turn(h0, ratio)
    copies[4].wait()
    e1 = less(folded(e_ref), change)
    h1 = magnetic(e1, h0)
    e2 = less(e1, turn(h1, ratio))
    pack = place(jnp.zeros((n, 128), F32), ratio, PACK_R)
    for k, (first, last) in enumerate(((e1, h0), (e2, h1))):
        for j, (c, z) in enumerate(sides):
            pack = place(pack, jnp.where(lane < 64, first[c][z], last[c][z]), PACK_PAIR + 8 * k + 2 * j, 2)
    copies[5].wait()
    fwd = [folded(f_ref, 0)]
    grad = product(e1, fwd[0])
    for j, (c, z) in enumerate(sides):
        pack = jnp.where(lane == PACK_F0 + j, pltpu.roll(fwd[0][c][z], PACK_F0 + j, 1), pack)
    copies[6].wait()
    fwd.append(folded(f_ref, 1))
    grad = grad + product(e2, fwd[1])
    pack = jnp.where((lane < FILT) | (lane >= 128 - FILT), grad, pack)
    scale = jnp.where(lane == 0, 1.0, ratio)
    for k, (c, z) in enumerate((c, z) for c in range(3) for z in range(nz)):
        pack = place(pack, fwd[1][c][z] * scale, PACK_F1 + 3 * k)
    packed = pack.T
    unpack_rows(packed, LO_LANES, lo_ref)
    unpack_rows(packed, HI_LANES, hi_ref)
    lo, hi = edge_lists(1, 0, e1, h0, h1, e2, fwd, ratio)
    rest = [line(*entry) for entry in lo + hi]
    rest = jnp.concatenate(rest + [jnp.zeros((1, 128), F32)], axis=0)
    tiles = [rest[8 * k : 8 * k + 8] for k in range(rest.shape[0] // 8)]
    down_ref[0:LO_ROWS] = lo_ref[...]
    down_ref[LO_ROWS : LO_ROWS + 8] = side_by_side(tiles, GROUP, 0)
    up_ref[0:HI_ROWS] = hi_ref[...]
    up_ref[HI_ROWS:LO_ROWS] = jnp.zeros((LO_ROWS - HI_ROWS, n), F32)
    up_ref[LO_ROWS : LO_ROWS + 8] = side_by_side(tiles, GROUP, 128 - REACH)
    for k in range(NMAT):
        table_ref[k : k + 1] = jnp.full((1, m), tab_ref[k], F32)


def solve_kernel(e_ref, h_ref, f_ref, lab_ref, den_ref, table_ref,
                 lo_ref, hi_ref, grad_ref, e2_ref, h2_ref, across_high, across_low, along_ref, around_ref, near_ref):
    n, m = lab_ref.shape
    nz = e_ref.shape[1]
    ratio = ratio_of(lab_ref[...], den_ref[...], [table_ref[k : k + 1] for k in range(NMAT)])
    h0 = planes(h_ref)
    e1, h1, e2, grad, fwd = local_solve(planes(e_ref), h0, lambda step: planes(f_ref, step), ratio)
    grad_ref[...] = grad
    lo, hi = edge_lists(1, 0, e1, h0, h1, e2, fwd, ratio)
    for ref, group, strip in ((hi_ref, hi, grad[n - FILT : n]), (lo_ref, lo, grad[0:FILT])):
        ref[0:FILT] = strip
        for k, (item, at) in enumerate(group):
            ref[FILT + k : FILT + k + 1] = line(item, at)
    hi_ref[HI_ROWS - 1 : HI_ROWS] = jnp.zeros((1, m), F32)
    _, magnetic = updates(n, m, nz)
    h2 = magnetic(e2, h1)
    for c in range(3):
        for z in range(nz):
            e2_ref[c, z] = e2[c][z]
            h2_ref[c, z] = h2[c][z]
    wide = across_high.shape[0]
    across_high[...], across_low[...] = halves(tap(cyclic(iota((wide, m), 0) - iota((wide, m), 1), wide)))
    around_ref[...] = tap(iota((n, n), 0) - iota((n, n), 1))
    k, r = iota(along_ref.shape, 1), iota(along_ref.shape, 0)
    same = (k < FILT) == (r < FILT)
    along_ref[...] = jnp.where(same, tap(k - r + jnp.where(r < FILT, -FILT, FILT)), 0.0)
    r = iota((EDGE, m), 0)
    for k in range(3):
        near_ref[k] = tap(r - (k - 1))
        near_ref[3 + k] = tap(r - EDGE - (k - 1))


def y_kernel(left_ref, right_ref, lo_ref, hi_ref, xlo_ref, xhi_ref, grad_ref,
             a_ref, b_ref, lo_ext, hi_ext, grad_ext, cols_ref, turned_ref):
    n, m = grad_ref.shape
    right, left = right_ref[0:LO_ROWS], left_ref[0:HI_ROWS]
    a, b = seam_inputs(left, hi_ref[...], lo_ref[...], right)
    lane = iota((8, n), 1)
    d = seam(
        1.0, a, b,
        lambda f: jnp.where(lane == n - 1, 0.0, pltpu.roll(f, n - 1, 1)),
        lambda f: jnp.where(lane == 0, 0.0, pltpu.roll(f, 1, 1)),
    )
    for f, field in enumerate(("e", "h")):
        for c, name in enumerate(("t", "n", "z")):
            before, end, begin, after = d[field][name]
            for z in range(2):
                p = 4 * (6 * f + 2 * c + z)
                turned_ref[p : p + 1] = before[2 + z : 3 + z]
                turned_ref[p + 1 : p + 2] = end[2 + z : 3 + z]
                turned_ref[p + 2 : p + 3] = begin[z : z + 1]
                turned_ref[p + 3 : p + 4] = after[z : z + 1]
    gb0, gb1, ga = d["gb0"], d["gb1"], d["ga"]
    top = iota((8, n), 0)
    at = TURN_G
    turned_ref[at : at + 8] = right[0:8] + jnp.where(top == 0, gb0[2:3], jnp.where(top == 1, gb1[2:3], 0.0))
    turned_ref[at + 8 : at + 16] = right[8:16]
    turned_ref[at + 16 : at + 24] = left[0:8]
    turned_ref[at + 24 : at + 32] = left[8:16] + jnp.where(top == 7, ga[0:1], 0.0)
    turned_ref[TURN_OWN : TURN_OWN + 8] = jnp.where(
        top == 0, ga[2:3], jnp.where(top == 1, gb0[0:1], jnp.where(top == 2, gb1[0:1], 0.0))
    )
    none = jnp.zeros((8, n), F32)
    for k, (last, first) in enumerate(((none, d["b_e1z"]), (none, d["b_h1n"]), (d["a_h1z"], d["b_h1z"]))):
        for z in range(2):
            p = TURN_X + 4 * (2 * k + z)
            turned_ref[p : p + 1] = last[2 + z : 3 + z]
            turned_ref[p + 1 : p + 2] = first[z : z + 1]
            turned_ref[p + 2 : p + 3] = last[z : z + 1]
            turned_ref[p + 3 : p + 4] = first[2 + z : 3 + z]
    turned_ref[TURN_X + 24 : 128] = jnp.zeros((128 - TURN_X - 24, n), F32)
    columns = turned_ref[...].T
    cols_ref[...] = columns

    wide = iota((n, 128), 1)
    own = pltpu.roll(columns, 128 - TURN_OWN - 1, 1)
    grad_ext[:, 0:128] = grad_ref[:, 0:128] + jnp.where(wide < 2, own, 0.0)
    grad_ext[:, m - 128 : m] = grad_ref[:, m - 128 : m] + jnp.where(wide == 127, own, 0.0)
    outside = jnp.where(wide < FILT, pltpu.roll(columns, 128 - TURN_G, 1), 0.0)
    grad_ext[:, m : m + 128] = jnp.where(wide >= 128 - FILT, pltpu.roll(columns, 128 - TURN_G - 2 * FILT, 1), outside)

    lane = iota((8, 128), 1)
    right_tile, left_tile = right_ref[LO_ROWS : LO_ROWS + 8], left_ref[LO_ROWS : LO_ROWS + 8]
    rest = []
    for k in range(LO_ROWS // 8):
        part = jnp.where(lane < REACH, pltpu.roll(right_tile, (128 - GROUP * k) % 128, 1), 0.0)
        rest.append(jnp.where(lane >= 128 - REACH, pltpu.roll(left_tile, (128 - REACH - GROUP * k) % 128, 1), part))
    rest = jnp.concatenate(rest, axis=0)
    for ref, mine, strip, halo in (
        (lo_ext, xlo_ref, slice(0, FILT), rest[0:LO_REST]),
        (hi_ext, xhi_ref, slice(n - FILT, n), rest[LO_REST : LO_REST + HI_REST]),
    ):
        count = mine.shape[0]
        ref[0:FILT] = grad_ext[strip]
        ref[FILT:count, 0:m] = mine[FILT:count]
        ref[FILT : FILT + halo.shape[0], m : m + 128] = halo
    hi_ext[HI_ROWS - 1 : HI_ROWS, m : m + 128] = jnp.zeros((1, 128), F32)
    one = iota((1, 128), 1)
    first, last = columns[0:1], columns[n - 1 : n]

    def add(ref, k, row, at, halo=True):
        inner = pltpu.roll(row, (127 - at) % 128, 1)
        ref[k : k + 1, 0:128] += jnp.where(one < (1 if halo else 2), inner, 0.0)
        ref[k : k + 1, m - 128 : m] += jnp.where(one == 127, inner, 0.0)
        if halo:
            outer = pltpu.roll(row, (125 - at) % 128, 1)
            ref[k : k + 1, m : m + 128] += jnp.where((one == 127) | (one == 0), outer, 0.0)

    for z in range(2):
        add(lo_ext, LO_E1Z + z, first, TURN_X + 4 * z)
        add(hi_ext, HI_H1T + z, last, TURN_X + 8 + 4 * z)
        add(hi_ext, HI_H1Z + z, last, TURN_X + 16 + 4 * z)
        add(lo_ext, LO_E2T + z, first, 4 * (2 + z) + 1, False)
        add(lo_ext, LO_E2Z + z, first, 4 * (4 + z) + 1, False)

    first_even = even("gx")
    low = lo_ext[...]
    high = jnp.concatenate([hi_ext[...], jnp.zeros((LO_ROWS - HI_ROWS, m + 128), F32)], axis=0)
    for ref, part in ((a_ref, jnp.where(first_even, high, low)), (b_ref, jnp.where(first_even, low, high))):
        ref[0:LO_ROWS] = part[:, 0:128]
        ref[LO_ROWS : 2 * LO_ROWS] = part[:, 128:256]
        tiles = [part[8 * k : 8 * k + 8, m : m + 128] for k in range(LO_ROWS // 8)]
        ref[2 * LO_ROWS : 2 * LO_ROWS + 8] = side_by_side(tiles[:3], 2 * REACH, 128 - REACH)
        ref[2 * LO_ROWS + 8 : 2 * LO_ROWS + 16] = side_by_side(tiles[3:], 2 * REACH, 128 - REACH)


def cyclic(d, count):
    return jnp.where(d > count // 2, d - count, jnp.where(d < -(count // 2), d + count, d))


def patch_kernel(cols_ref, e2_ref, h2_ref, grad_ext, across_high, across_low, around_ref,
                 e_hbm, h_hbm, out_hbm, e_rows, h_rows, inner_ref,
                 e_ref, h_ref, sems):
    n, wide = grad_ext.shape
    m = inner_ref.shape[1]
    lane = iota((n, 128), 1)
    columns = cols_ref[...]
    copies = []
    for f, (src, ref, dst, rows) in enumerate(((e2_ref, e_ref, e_hbm, e_rows), (h2_ref, h_ref, h_hbm, h_rows))):
        for c in range(3):
            for z in range(2):
                p = 4 * (6 * f + 2 * c + z)
                moved = pltpu.roll(columns, (126 - p) % 128, 1)
                ref[c, z, :, 0:128] = src[c, z, :, 0:128] + jnp.where(lane < 2, moved, 0.0)
                ref[c, z, :, m - 128 : m] = src[c, z, :, m - 128 : m] + jnp.where(lane >= 126, moved, 0.0)
                rows[c, z, 0:8] = ref[c, z, 0:8]
                rows[c, z, 8:16] = ref[c, z, n - 8 : n]
                copies.append(pltpu.make_async_copy(ref.at[c, z], dst.at[c, z], sems.at[len(copies)]))
                copies[-1].start()
    part = dot3(halves(grad_ext[...]), (across_high[...], across_low[...]))
    inner_ref[...] = dot3(halves(around_ref[...]), halves(part))
    rows = pl.ds(EDGE, n - 2 * EDGE)
    copies.append(pltpu.make_async_copy(inner_ref.at[rows], out_hbm.at[rows], sems.at[len(copies)]))
    copies[-1].start()
    for copy in copies:
        copy.wait()


def x_kernel(ra_ref, rb_ref, lo_ref, hi_ref, e_rows, h_rows, inner_ref, across_high, across_low, along_ref, near_ref,
             e_in, h_in, out_in, e_hbm, h_hbm, out_hbm, ends_ref, out_ref, sems):
    n, m = inner_ref.shape
    wide = lo_ref.shape[1]
    first_even = even("gx")
    tile_lane = iota((8, 128), 1)

    def unfold(message):
        outer = []
        for k in range(LO_ROWS // 8):
            at = 2 * LO_ROWS + 8 * (k // 3)
            moved = pltpu.roll(message[at : at + 8], 128 - REACH - 2 * REACH * (k % 3), 1)
            outer.append(jnp.where((tile_lane < REACH) | (tile_lane >= 128 - REACH), moved, 0.0))
        return jnp.concatenate([message[0:LO_ROWS], message[LO_ROWS : 2 * LO_ROWS], jnp.concatenate(outer, axis=0)], axis=1)

    right = unfold(jnp.where(first_even, ra_ref[...], rb_ref[...]))
    left = unfold(jnp.where(first_even, rb_ref[...], ra_ref[...]))
    a, b = seam_inputs(left, hi_ref[...], lo_ref[...], right)
    raw = jnp.concatenate([left[0:FILT], right[0:FILT]], axis=0)
    part = dot3(halves(raw), (across_high[...], across_low[...]))
    far = dot3(halves(along_ref[...]), halves(part))
    d = seam(-1.0, a, b, lambda f: pltpu.roll(f, wide - 1, 1), lambda f: pltpu.roll(f, 1, 1))
    gb0, gb1, ga = d["gb0"], d["gb1"], d["ga"]
    top = iota((8, wide), 0)
    change = jnp.zeros((8, wide), F32)
    for k, row in enumerate((ga[0:1], gb0[0:1], gb1[0:1], ga[2:3], gb0[2:3], gb1[2:3])):
        change = jnp.where(top == k, row, change)
    taps = filter_taps()
    moved = change[:, 0:m] * taps[0]
    for k in range(1, FILT + 1):
        moved = moved + taps[k] * (pltpu.roll(change, k, 1)[:, 0:m] + pltpu.roll(change, wide - k, 1)[:, 0:m])
    for side, at in ((0, 0), (1, n - EDGE)):
        rows = inner_ref[at : at + EDGE]
        for k in range(3 * side, 3 * side + 3):
            rows = rows + near_ref[k] * moved[k : k + 1]
        out_ref[side] = rows
    out_ref[0, 0:FILT] += far[0:FILT]
    out_ref[1, EDGE - FILT : EDGE] += far[FILT : 2 * FILT]
    copies = []
    for side, at in ((0, 0), (1, n - EDGE)):
        copies.append(pltpu.make_async_copy(out_ref.at[side], out_hbm.at[pl.ds(at, EDGE)], sems.at[side]))
        copies[-1].start()
    sub = iota((8, m), 0)
    for f, (field, rows, dst) in enumerate((("e", e_rows, e_hbm), ("h", h_rows, h_hbm))):
        for c, name in enumerate(("n", "t", "z")):
            before, end, begin, after = (value[:, 0:m] for value in d[field][name])
            for z in range(2):
                ends_ref[0, f, c, z] = rows[c, z, 0:8] + jnp.where(
                    sub == 0, begin[z : z + 1], jnp.where(sub == 1, after[z : z + 1], 0.0)
                )
                ends_ref[1, f, c, z] = rows[c, z, 8:16] + jnp.where(
                    sub == 6, before[2 + z : 3 + z], jnp.where(sub == 7, end[2 + z : 3 + z], 0.0)
                )
        for side, at in ((0, 0), (1, n - 8)):
            dst_rows = dst.at[:, :, pl.ds(at, 8)]
            copies.append(pltpu.make_async_copy(ends_ref.at[side, f], dst_rows, sems.at[len(copies)]))
            copies[-1].start()
    for copy in copies:
        copy.wait()


def swap_pairs(count, which):
    if which == 0:
        return [(i, i ^ 1) for i in range(count)]
    return [(i, (i - 1) % count if i % 2 == 0 else (i + 1) % count) for i in range(count)]


def call(kernel, shapes, ins, scratch=(), far=(), sems=0, far_out=(), aliases=None):
    vmem = pl.BlockSpec(memory_space=pltpu.VMEM)
    hbm = pl.BlockSpec(memory_space=pltpu.HBM)
    ins = [pltpu.with_memory_space_constraint(x, pltpu.HBM) if k in far else x for k, x in enumerate(ins)]
    scratches = [s if hasattr(s, "dtype") else pltpu.VMEM(s, F32) for s in scratch]
    if sems:
        scratches.append(pltpu.SemaphoreType.DMA((sems,)))
    return pl.pallas_call(
        kernel,
        out_shape=[s if hasattr(s, "dtype") else jax.ShapeDtypeStruct(s, F32) for s in shapes],
        in_specs=[hbm if k in far else vmem for k in range(len(ins))],
        out_specs=[hbm if k in far_out else vmem for k in range(len(shapes))],
        scratch_shapes=scratches,
        input_output_aliases=aliases or {},
        compiler_params=pltpu.CompilerParams(vmem_limit_bytes=24 * 1024 * 1024),
    )(*ins)


def body(adj_e, adj_h, fwd_e, labels, eps_table, density):
    n, m = labels.shape
    block = adj_e.shape
    nz = block[1]
    gx, gy = lax.axis_size("gx"), lax.axis_size("gy")
    message = (LO_ROWS + 8, n)
    labels_in = jax.ShapeDtypeStruct((n, m), jnp.int32)
    up, down, ylo, yhi, *fetched = call(
        first_kernel,
        [message, message, (LO_ROWS, n), (HI_ROWS, n), block, block, fwd_e.shape, labels_in, (n, m), (NMAT, m)],
        [adj_e, adj_h, fwd_e, labels, density, eps_table],
        [pltpu.SMEM((NMAT,), F32)],
        range(6),
        7,
    )
    left = lax.ppermute(up, "gy", [(i, (i + 1) % gy) for i in range(gy)])
    right = lax.ppermute(down, "gy", [(i, (i - 1) % gy) for i in range(gy)])
    wide = m + 128
    bands = jax.ShapeDtypeStruct((wide, m), jnp.bfloat16)
    xlo, xhi, grad, e2, h2, across_high, across_low, along, around, near = call(
        solve_kernel,
        [(LO_ROWS, m), (HI_ROWS, m), (n, m), block, block, bands, bands, (2 * FILT, 2 * FILT), (n, n), (6, EDGE, m)],
        fetched,
    )
    message = (2 * LO_ROWS + 16, 128)
    xa, xb, lo_ext, hi_ext, grad_ext, cols = call(
        y_kernel,
        [message, message, (LO_ROWS, wide), (HI_ROWS, wide), (n, wide), (n, 128)],
        [left, right, ylo, yhi, xlo, xhi, grad],
        [(128, n)],
    )
    got_a = lax.ppermute(xa, "gx", swap_pairs(gx, 0))
    got_b = lax.ppermute(xb, "gx", swap_pairs(gx, 1))
    ends = (3, nz, 16, m)
    electric, magnetic, filtered, e_rows, h_rows, inner = call(
        patch_kernel,
        [block, block, (n, m), ends, ends, (n, m)],
        [cols, e2, h2, grad_ext, across_high, across_low, around],
        [block, block],
        sems=13,
        far_out=(0, 1, 2),
    )
    return tuple(
        call(
            x_kernel,
            [block, block, (n, m)],
            [got_a, got_b, lo_ext, hi_ext, e_rows, h_rows, inner, across_high, across_low, along, near]
            + [electric, magnetic, filtered],
            [(2, 2, 3, nz, 8, m), (2, EDGE, m)],
            (11, 12, 13),
            6,
            (0, 1, 2),
            {11: 0, 12: 1, 13: 2},
        )
    )


def solution(mesh):
    return jax.shard_map(
        body,
        mesh=mesh,
        in_specs=(
            P("design", None, "gx", "gy"),
            P("design", None, "gx", "gy"),
            P("design", None, None, "gx", "gy"),
            P(("design", "gx"), "gy"),
            P(),
            P(("design", "gx"), "gy"),
        ),
        out_specs=(
            P("design", None, "gx", "gy"),
            P("design", None, "gx", "gy"),
            P(("design", "gx"), "gy"),
        ),
        check_vma=False,
    )
```

```python
import math

import jax
import jax.numpy as jnp
from jax import lax
from jax.experimental import pallas as pl
from jax.experimental.pallas import tpu as pltpu
from jax.sharding import PartitionSpec as P

STEPS = 2
NMAT = 8
FILT = 16

courant = 0.5
spread_ratio = 0.6

F32 = jnp.float32

LO_G, LO_E1T, LO_E1Z, LO_E2T, LO_E2Z = 0, 16, 18, 20, 22
LO_F0T, LO_F0Z, LO_F1T, LO_F1N, LO_F1Z = 24, 26, 28, 30, 32
LO_W1T, LO_W1Z, LO_R0, LO_R1, LO_ROWS = 34, 36, 38, 39, 40
HI_G, HI_H0T, HI_H0Z, HI_H1T, HI_H1Z = 0, 16, 18, 20, 22
HI_WT, HI_WN, HI_WZ, HI_R, HI_ROWS = 24, 26, 28, 30, 32
PACK_F1, PACK_R, PACK_PAIR, PACK_F0, PACK_END = 16, 34, 37, 53, 57
LO_LANES = (
    list(range(FILT))
    + [PACK_PAIR + 2 * j + 1 for j in range(8)]
    + [PACK_F0 + j for j in range(4)]
    + [PACK_F1 + 3 * k + 1 for k in range(6)]
    + [PACK_F1 + 3 * k + 2 for k in (0, 1, 4, 5)]
    + [PACK_R + 1, PACK_R + 2]
)
HI_LANES = (
    list(range(128 - FILT, 128))
    + [PACK_PAIR + 2 * j for j in range(8)]
    + [PACK_F1 + 3 * k for k in range(6)]
    + [PACK_R, PACK_END]
)
REACH = FILT + 2
GROUP = 24
EDGE = 24
LO_REST, HI_REST = LO_ROWS - FILT, HI_ROWS - FILT - 1

TURN_G, TURN_OWN, TURN_X = 48, 80, 88


def filter_taps():
    spread = spread_ratio * FILT
    norm = math.sqrt(sum(math.exp(-d * d / (spread * spread)) for d in range(-FILT, FILT + 1)))
    return [math.exp(-d * d / (2.0 * spread * spread)) / norm for d in range(FILT + 1)]


def tap(distance):
    spread = spread_ratio * FILT
    norm = math.sqrt(sum(math.exp(-d * d / (spread * spread)) for d in range(-FILT, FILT + 1)))
    far = distance.astype(F32)
    value = jnp.exp(-far * far / (2.0 * spread * spread)) / norm
    return jnp.where(jnp.abs(distance) <= FILT, value, F32(0.0))


def halves(x):
    high = x.astype(jnp.bfloat16)
    return high, (x - high.astype(F32)).astype(jnp.bfloat16)


def dot3(a, b):
    terms = [jnp.dot(x, y, preferred_element_type=F32) for x, y in ((a[0], b[1]), (a[1], b[0]), (a[0], b[0]))]
    return terms[0] + terms[1] + terms[2]


def iota(shape, dim):
    return lax.broadcasted_iota(jnp.int32, shape, dim)


def updates(n, m, nz):
    row, col = iota((n, m), 0), iota((n, m), 1)

    def lx(f):
        return jnp.where(row == 0, 0.0, pltpu.roll(f, 1, 0))

    def ux(f):
        return jnp.where(row == n - 1, 0.0, pltpu.roll(f, n - 1, 0))

    def ly(f):
        return jnp.where(col == 0, 0.0, pltpu.roll(f, 1, 1))

    def uy(f):
        return jnp.where(col == m - 1, 0.0, pltpu.roll(f, m - 1, 1))

    def turn(h, ratio):
        out = [[None] * nz for _ in range(3)]
        for z in range(nz):
            hx, hy, hz = h[0][z], h[1][z], h[2][z]
            dzx = hx - h[0][z - 1] if z > 0 else hx
            dzy = hy - h[1][z - 1] if z > 0 else hy
            out[0][z] = ratio * ((hz - ly(hz)) - dzy)
            out[1][z] = ratio * (dzx - (hz - lx(hz)))
            out[2][z] = ratio * ((hy - lx(hy)) - (hx - ly(hx)))
        return out

    def magnetic(e, h):
        out = [[None] * nz for _ in range(3)]
        for z in range(nz):
            ex, ey, ez = e[0][z], e[1][z], e[2][z]
            dzx = e[0][z + 1] - ex if z < nz - 1 else -ex
            dzy = e[1][z + 1] - ey if z < nz - 1 else -ey
            out[0][z] = h[0][z] + courant * ((uy(ez) - ez) - dzy)
            out[1][z] = h[1][z] + courant * (dzx - (ux(ez) - ez))
            out[2][z] = h[2][z] + courant * ((ux(ey) - ey) - (uy(ex) - ex))
        return out

    return turn, magnetic


def less(e, change):
    return [[a - b for a, b in zip(one, other, strict=True)] for one, other in zip(e, change, strict=True)]


def product(e, f):
    total = None
    for c in range(3):
        for z in range(len(e[c])):
            term = e[c][z] * f[c][z]
            total = term if total is None else total + term
    return total


def local_solve(e0, h0, saved, ratio):
    turn, magnetic = updates(*ratio.shape, len(e0[0]))
    e1 = less(e0, turn(h0, ratio))
    h1 = magnetic(e1, h0)
    fwd = [saved(0)]
    grad = product(e1, fwd[0])
    e2 = less(e1, turn(h1, ratio))
    fwd.append(saved(1))
    grad = grad + product(e2, fwd[1])
    return e1, h1, e2, grad, fwd


def depth_shifts(shape):
    odd = iota(shape, 0) % 2 == 1
    return (
        lambda f: jnp.where(odd, 0.0, pltpu.roll(f, 7, 0)),
        lambda f: jnp.where(odd, pltpu.roll(f, 1, 0), 0.0),
    )


def seam_magnetic(sgn, v, up):
    half = sgn * courant
    uz, _ = depth_shifts(v[0].shape)
    e2t, e2n, e2z, f2t, f2z, g2t, g2n, g2z, ah1t, ah1z, bh1t, bh1n, bh1z, e2t_b, e2z_b = v
    none = jnp.zeros_like(e2t)
    return {
        "t": (
            half * g2z,
            ah1t + half * ((e2z_b - g2z) - (uz(g2n) - g2n)),
            bh1t + half * ((f2z - e2z) - (uz(e2n) - e2n)),
            -half * f2z,
        ),
        "n": (
            none,
            half * ((uz(g2t) - g2t) - (up(g2z) - g2z)),
            bh1n + half * ((uz(e2t) - e2t) - (up(e2z) - e2z)),
            half * ((uz(f2t) - f2t) - (up(f2z) - f2z)),
        ),
        "z": (
            -half * g2t,
            ah1z + half * ((up(g2n) - g2n) - (e2t_b - g2t)),
            bh1z + half * ((up(e2n) - e2n) - (f2t - e2t)),
            half * f2t,
        ),
    }


def seam(sgn, a, b, up, down):
    odd = iota(a["h0t"].shape, 0) % 2 == 1
    half = sgn * courant
    uz, lz = depth_shifts(a["h0t"].shape)
    rb, rb1, ra = sgn * b["r0"], sgn * b["r1"], sgn * a["r"]
    d = {}
    e1t = rb * a["h0z"]
    e1z = -rb * a["h0t"]
    e1t_b = b["e1t"] + e1t
    e1z_b = b["e1z"] + e1z
    ah1t = half * e1z_b
    ah1z = -half * e1t_b
    h1t_a = a["h1t"] + ah1t
    h1z_a = a["h1z"] + ah1z
    bh1t = -half * e1z
    bh1n = half * ((uz(e1t) - e1t) - (up(e1z) - e1z))
    bh1z = half * e1t
    e2t = e1t - rb * ((bh1z - h1z_a) - (bh1n - lz(bh1n)))
    e2n = -rb * ((bh1t - lz(bh1t)) - (bh1z - down(bh1z)))
    e2z = e1z - rb * ((bh1n - down(bh1n)) - (bh1t - h1t_a))
    f2t = rb1 * bh1z
    f2z = -rb1 * bh1t
    at = ah1z
    an = (ah1t - lz(ah1t)) - (ah1z - down(ah1z))
    az = -ah1t
    g2t, g2n, g2z = -ra * at, -ra * an, -ra * az
    gb0 = b["f0t"] * e1t + b["f0z"] * e1z + b["f1t"] * e2t + b["f1n"] * e2n + b["f1z"] * e2z
    gb1 = sgn * (b["w1t"] * bh1z - b["w1z"] * bh1t)
    ga = -sgn * (a["wt"] * at + a["wn"] * an + a["wz"] * az)
    e2t_b = b["e2t"] + e2t
    e2z_b = b["e2z"] + e2z
    d["b_e1z"], d["b_h1n"], d["b_h1z"], d["a_h1z"] = e1z, bh1n, bh1z, ah1z
    none = jnp.zeros_like(e1t)
    d["e"] = {"t": (none, g2t, e2t, f2t), "n": (none, g2n, e2n, none), "z": (none, g2z, e2z, f2z)}
    d["v"] = (e2t, e2n, e2z, f2t, f2z, g2t, g2n, g2z, ah1t, ah1z, bh1t, bh1n, bh1z, e2t_b, e2z_b)
    d["gb0"], d["gb1"], d["ga"] = (g + pltpu.roll(g, 7, 0) for g in (gb0, gb1, ga))
    return d


def two(first, second, at, count=2):
    if count == 1:
        one, other = first[at : at + 1], second[at : at + 1]
        parts = [one, one, other, other]
    else:
        parts = [first[at : at + 2], second[at : at + 2]]
    parts.append(jnp.zeros((4, first.shape[1]), F32))
    return jnp.concatenate(parts, axis=0)


def seam_inputs(left_hi, my_hi, my_lo, right_lo):
    a = {
        "h0t": two(left_hi, my_hi, HI_H0T),
        "h0z": two(left_hi, my_hi, HI_H0Z),
        "h1t": two(left_hi, my_hi, HI_H1T),
        "h1z": two(left_hi, my_hi, HI_H1Z),
        "wt": two(left_hi, my_hi, HI_WT),
        "wn": two(left_hi, my_hi, HI_WN),
        "wz": two(left_hi, my_hi, HI_WZ),
        "r": two(left_hi, my_hi, HI_R, 1),
    }
    b = {
        "e1t": two(my_lo, right_lo, LO_E1T),
        "e1z": two(my_lo, right_lo, LO_E1Z),
        "e2t": two(my_lo, right_lo, LO_E2T),
        "e2z": two(my_lo, right_lo, LO_E2Z),
        "f0t": two(my_lo, right_lo, LO_F0T),
        "f0z": two(my_lo, right_lo, LO_F0Z),
        "f1t": two(my_lo, right_lo, LO_F1T),
        "f1n": two(my_lo, right_lo, LO_F1N),
        "f1z": two(my_lo, right_lo, LO_F1Z),
        "w1t": two(my_lo, right_lo, LO_W1T),
        "w1z": two(my_lo, right_lo, LO_W1Z),
        "r0": two(my_lo, right_lo, LO_R0, 1),
        "r1": two(my_lo, right_lo, LO_R1, 1),
    }
    return a, b


def even(axis):
    return lax.axis_index(axis) % 2 == 0


def ratio_of(labels, density, table):
    eps = jnp.broadcast_to(table[0], labels.shape)
    for k in range(1, NMAT):
        eps = jnp.where(labels == k, table[k], eps)
    return courant / (eps + density)


def planes(ref, *lead):
    return [[ref[(*lead, c, z)] for z in range(ref.shape[-3])] for c in range(3)]


def edge_lists(t, nrm, e1, h0, h1, e2, fwd, ratio):
    zs = range(len(e1[0]))
    lo = (
        [(e1[c][z], 0) for c in (t, 2) for z in zs]
        + [(e2[c][z], 0) for c in (t, 2) for z in zs]
        + [(fwd[0][c][z], 0) for c in (t, 2) for z in zs]
        + [(fwd[1][c][z], 0) for c in (t, nrm, 2) for z in zs]
        + [((ratio, fwd[1][c][z]), 1) for c in (t, 2) for z in zs]
        + [(ratio, 0), (ratio, 1)]
    )
    hi = (
        [(h0[c][z], -1) for c in (t, 2) for z in zs]
        + [(h1[c][z], -1) for c in (t, 2) for z in zs]
        + [((ratio, fwd[1][c][z]), -1) for c in (t, nrm, 2) for z in zs]
        + [(ratio, -1)]
    )
    return lo, hi


def fold(plane):
    m = plane.shape[1]
    lane = iota((plane.shape[0], 128), 1)
    return jnp.where(lane < 64, plane[:, 0:128], plane[:, m - 128 : m])


def place(pack, values, base, count=3):
    lane = iota(pack.shape, 1)
    return jnp.where((lane >= base) & (lane < base + count), pltpu.roll(values, base + 1, 1), pack)


def unpack_rows(packed, lanes, ref):
    ref[0:FILT] = packed[lanes[0] : lanes[0] + FILT]
    for k in range(FILT, len(lanes)):
        ref[k : k + 1] = packed[lanes[k] : lanes[k] + 1]


def line(item, at):
    if isinstance(item, tuple):
        return line(item[0], at) * line(item[1], at)
    at = at % item.shape[0]
    return item[at : at + 1]


def side_by_side(tiles, width, first):
    lane = iota((8, 128), 1)
    out = None
    for k, tile in enumerate(tiles):
        moved = pltpu.roll(tile, (width * k - first) % 128, 1)
        out = moved if out is None else jnp.where(lane < width * k, out, moved)
    return out


def first_kernel(e_hbm, h_hbm, f_hbm, lab_hbm, den_hbm, eps_hbm,
                 up_ref, down_ref, lo_ref, hi_ref, e_ref, h_ref, f_ref, lab_ref, den_ref, table_ref,
                 tab_ref, sems):
    n, m = lab_hbm.shape
    nz = e_hbm.shape[1]
    copies = []
    for src, dst in ((h_hbm, h_ref), (lab_hbm, lab_ref), (den_hbm, den_ref), (eps_hbm, tab_ref), (e_hbm, e_ref),
                     (f_hbm.at[0], f_ref.at[0]), (f_hbm.at[1], f_ref.at[1])):
        copies.append(pltpu.make_async_copy(src, dst, sems.at[len(copies)]))
        copies[-1].start()

    def folded(ref, *lead):
        return [[fold(plane) for plane in comp] for comp in planes(ref, *lead)]

    turn, magnetic = updates(n, 128, nz)
    sides = [(c, z) for c in (0, 2) for z in range(nz)]
    lane = iota((n, 128), 1)
    for copy in copies[1:4]:
        copy.wait()
    ratio = ratio_of(fold(lab_ref[...]), fold(den_ref[...]), tab_ref)
    copies[0].wait()
    h0 = folded(h_ref)
    change = turn(h0, ratio)
    copies[4].wait()
    e1 = less(folded(e_ref), change)
    h1 = magnetic(e1, h0)
    e2 = less(e1, turn(h1, ratio))
    pack = place(jnp.zeros((n, 128), F32), ratio, PACK_R)
    for k, (first, last) in enumerate(((e1, h0), (e2, h1))):
        for j, (c, z) in enumerate(sides):
            pack = place(pack, jnp.where(lane < 64, first[c][z], last[c][z]), PACK_PAIR + 8 * k + 2 * j, 2)
    copies[5].wait()
    fwd = [folded(f_ref, 0)]
    grad = product(e1, fwd[0])
    for j, (c, z) in enumerate(sides):
        pack = jnp.where(lane == PACK_F0 + j, pltpu.roll(fwd[0][c][z], PACK_F0 + j, 1), pack)
    copies[6].wait()
    fwd.append(folded(f_ref, 1))
    grad = grad + product(e2, fwd[1])
    pack = jnp.where((lane < FILT) | (lane >= 128 - FILT), grad, pack)
    scale = jnp.where(lane == 0, 1.0, ratio)
    for k, (c, z) in enumerate((c, z) for c in range(3) for z in range(nz)):
        pack = place(pack, fwd[1][c][z] * scale, PACK_F1 + 3 * k)
    packed = pack.T
    unpack_rows(packed, LO_LANES, lo_ref)
    unpack_rows(packed, HI_LANES, hi_ref)
    lo, hi = edge_lists(1, 0, e1, h0, h1, e2, fwd, ratio)
    rest = [line(*entry) for entry in lo + hi]
    rest = jnp.concatenate(rest + [jnp.zeros((1, 128), F32)], axis=0)
    tiles = [rest[8 * k : 8 * k + 8] for k in range(rest.shape[0] // 8)]
    down_ref[0:LO_ROWS] = lo_ref[...]
    down_ref[LO_ROWS : LO_ROWS + 8] = side_by_side(tiles, GROUP, 0)
    up_ref[0:HI_ROWS] = hi_ref[...]
    up_ref[HI_ROWS:LO_ROWS] = jnp.zeros((LO_ROWS - HI_ROWS, n), F32)
    up_ref[LO_ROWS : LO_ROWS + 8] = side_by_side(tiles, GROUP, 128 - REACH)
    for k in range(NMAT):
        table_ref[k : k + 1] = jnp.full((1, m), tab_ref[k], F32)


def solve_kernel(e_ref, h_ref, f_ref, lab_ref, den_ref, table_ref,
                 lo_ref, hi_ref, grad_ref, e2_ref, h2_ref, across_high, across_low, along_ref, around_ref, near_ref):
    n, m = lab_ref.shape
    nz = e_ref.shape[1]
    ratio = ratio_of(lab_ref[...], den_ref[...], [table_ref[k : k + 1] for k in range(NMAT)])
    h0 = planes(h_ref)
    e1, h1, e2, grad, fwd = local_solve(planes(e_ref), h0, lambda step: planes(f_ref, step), ratio)
    grad_ref[...] = grad
    lo, hi = edge_lists(1, 0, e1, h0, h1, e2, fwd, ratio)
    for ref, group, strip in ((hi_ref, hi, grad[n - FILT : n]), (lo_ref, lo, grad[0:FILT])):
        ref[0:FILT] = strip
        for k, (item, at) in enumerate(group):
            ref[FILT + k : FILT + k + 1] = line(item, at)
    hi_ref[HI_ROWS - 1 : HI_ROWS] = jnp.zeros((1, m), F32)
    _, magnetic = updates(n, m, nz)
    h2 = magnetic(e2, h1)
    for c in range(3):
        for z in range(nz):
            e2_ref[c, z] = e2[c][z]
            h2_ref[c, z] = h2[c][z]
    wide = across_high.shape[0]
    across_high[...], across_low[...] = halves(tap(cyclic(iota((wide, m), 0) - iota((wide, m), 1), wide)))
    around_ref[...] = tap(iota((n, n), 0) - iota((n, n), 1))
    k, r = iota(along_ref.shape, 1), iota(along_ref.shape, 0)
    same = (k < FILT) == (r < FILT)
    along_ref[...] = jnp.where(same, tap(k - r + jnp.where(r < FILT, -FILT, FILT)), 0.0)
    r = iota((EDGE, m), 0)
    for k in range(3):
        near_ref[k] = tap(r - (k - 1))
        near_ref[3 + k] = tap(r - EDGE - (k - 1))


def put_lines(ref, lines):
    for c, name in enumerate(("t", "n", "z")):
        before, end, begin, after = lines[name]
        for z in range(2):
            p = 4 * (2 * c + z)
            ref[p : p + 1] = before[2 + z : 3 + z]
            ref[p + 1 : p + 2] = end[2 + z : 3 + z]
            ref[p + 2 : p + 3] = begin[z : z + 1]
            ref[p + 3 : p + 4] = after[z : z + 1]


def extended(grad, columns):
    m = grad.shape[1]
    lane = iota(columns.shape, 1)
    own = pltpu.roll(columns, 128 - TURN_OWN - 1, 1)
    outside = jnp.where(lane < FILT, pltpu.roll(columns, 128 - TURN_G, 1), 0.0)
    return [
        grad[:, 0:128] + jnp.where(lane < 2, own, 0.0),
        grad[:, m - 128 : m] + jnp.where(lane == 127, own, 0.0),
        jnp.where(lane >= 128 - FILT, pltpu.roll(columns, 128 - TURN_G - 2 * FILT, 1), outside),
    ]


def y_kernel(left_ref, right_ref, lo_ref, hi_ref, xlo_ref, xhi_ref, grad_ref,
             a_ref, b_ref, lo_ext, hi_ext, cols_ref, seam_ref, turned_ref):
    n, m = grad_ref.shape
    right, left = right_ref[0:LO_ROWS], left_ref[0:HI_ROWS]
    a, b = seam_inputs(left, hi_ref[...], lo_ref[...], right)
    lane = iota((8, n), 1)
    d = seam(
        1.0, a, b,
        lambda f: jnp.where(lane == n - 1, 0.0, pltpu.roll(f, n - 1, 1)),
        lambda f: jnp.where(lane == 0, 0.0, pltpu.roll(f, 1, 1)),
    )
    for k, value in enumerate(d["v"]):
        seam_ref[k] = value
    put_lines(turned_ref, d["e"])
    turned_ref[24:TURN_G] = jnp.zeros((TURN_G - 24, n), F32)
    gb0, gb1, ga = d["gb0"], d["gb1"], d["ga"]
    top = iota((8, n), 0)
    at = TURN_G
    turned_ref[at : at + 8] = right[0:8] + jnp.where(top == 0, gb0[2:3], jnp.where(top == 1, gb1[2:3], 0.0))
    turned_ref[at + 8 : at + 16] = right[8:16]
    turned_ref[at + 16 : at + 24] = left[0:8]
    turned_ref[at + 24 : at + 32] = left[8:16] + jnp.where(top == 7, ga[0:1], 0.0)
    turned_ref[TURN_OWN : TURN_OWN + 8] = jnp.where(
        top == 0, ga[2:3], jnp.where(top == 1, gb0[0:1], jnp.where(top == 2, gb1[0:1], 0.0))
    )
    none = jnp.zeros((8, n), F32)
    for k, (last, first) in enumerate(((none, d["b_e1z"]), (none, d["b_h1n"]), (d["a_h1z"], d["b_h1z"]))):
        for z in range(2):
            p = TURN_X + 4 * (2 * k + z)
            turned_ref[p : p + 1] = last[2 + z : 3 + z]
            turned_ref[p + 1 : p + 2] = first[z : z + 1]
            turned_ref[p + 2 : p + 3] = last[z : z + 1]
            turned_ref[p + 3 : p + 4] = first[2 + z : 3 + z]
    turned_ref[TURN_X + 24 : 128] = jnp.zeros((128 - TURN_X - 24, n), F32)
    columns = turned_ref[...].T
    cols_ref[...] = columns

    lane = iota((8, 128), 1)
    right_tile, left_tile = right_ref[LO_ROWS : LO_ROWS + 8], left_ref[LO_ROWS : LO_ROWS + 8]
    rest = []
    for k in range(LO_ROWS // 8):
        part = jnp.where(lane < REACH, pltpu.roll(right_tile, (128 - GROUP * k) % 128, 1), 0.0)
        rest.append(jnp.where(lane >= 128 - REACH, pltpu.roll(left_tile, (128 - REACH - GROUP * k) % 128, 1), part))
    rest = jnp.concatenate(rest, axis=0)
    for ref, mine, strip, halo in (
        (lo_ext, xlo_ref, slice(0, FILT), rest[0:LO_REST]),
        (hi_ext, xhi_ref, slice(n - FILT, n), rest[LO_REST : LO_REST + HI_REST]),
    ):
        count = mine.shape[0]
        for k, tile in enumerate(extended(grad_ref[strip], columns[strip])):
            ref[0:FILT, 128 * k : 128 * k + 128] = tile
        ref[FILT:count, 0:m] = mine[FILT:count]
        ref[FILT : FILT + halo.shape[0], m : m + 128] = halo
    hi_ext[HI_ROWS - 1 : HI_ROWS, m : m + 128] = jnp.zeros((1, 128), F32)
    one = iota((1, 128), 1)
    first, last = columns[0:1], columns[n - 1 : n]

    def add(ref, k, row, at, halo=True):
        inner = pltpu.roll(row, (127 - at) % 128, 1)
        ref[k : k + 1, 0:128] += jnp.where(one < (1 if halo else 2), inner, 0.0)
        ref[k : k + 1, m - 128 : m] += jnp.where(one == 127, inner, 0.0)
        if halo:
            outer = pltpu.roll(row, (125 - at) % 128, 1)
            ref[k : k + 1, m : m + 128] += jnp.where((one == 127) | (one == 0), outer, 0.0)

    for z in range(2):
        add(lo_ext, LO_E1Z + z, first, TURN_X + 4 * z)
        add(hi_ext, HI_H1T + z, last, TURN_X + 8 + 4 * z)
        add(hi_ext, HI_H1Z + z, last, TURN_X + 16 + 4 * z)
        add(lo_ext, LO_E2T + z, first, 4 * (2 + z) + 1, False)
        add(lo_ext, LO_E2Z + z, first, 4 * (4 + z) + 1, False)

    first_even = even("gx")
    low = lo_ext[...]
    high = jnp.concatenate([hi_ext[...], jnp.zeros((LO_ROWS - HI_ROWS, m + 128), F32)], axis=0)
    for ref, part in ((a_ref, jnp.where(first_even, high, low)), (b_ref, jnp.where(first_even, low, high))):
        ref[0:LO_ROWS] = part[:, 0:128]
        ref[LO_ROWS : 2 * LO_ROWS] = part[:, 128:256]
        tiles = [part[8 * k : 8 * k + 8, m : m + 128] for k in range(LO_ROWS // 8)]
        ref[2 * LO_ROWS : 2 * LO_ROWS + 8] = side_by_side(tiles[:3], 2 * REACH, 128 - REACH)
        ref[2 * LO_ROWS + 8 : 2 * LO_ROWS + 16] = side_by_side(tiles[3:], 2 * REACH, 128 - REACH)


def cyclic(d, count):
    return jnp.where(d > count // 2, d - count, jnp.where(d < -(count // 2), d + count, d))


def patch_kernel(cols_ref, seam_ref, e2_ref, h2_ref, grad_ref, across_high, across_low, around_ref,
                 e_hbm, h_hbm, out_hbm, e_rows, h_rows, inner_ref,
                 e_ref, h_ref, turned_ref, sems):
    n, m = grad_ref.shape
    lane = iota((n, 128), 1)
    columns = cols_ref[...]
    copies = []

    def patch(columns, src, ref, dst, rows):
        for c in range(3):
            for z in range(2):
                p = 4 * (2 * c + z)
                moved = pltpu.roll(columns, (126 - p) % 128, 1)
                ref[c, z, :, 0:128] = src[c, z, :, 0:128] + jnp.where(lane < 2, moved, 0.0)
                ref[c, z, :, m - 128 : m] = src[c, z, :, m - 128 : m] + jnp.where(lane >= 126, moved, 0.0)
                rows[c, z, 0:8] = ref[c, z, 0:8]
                rows[c, z, 8:16] = ref[c, z, n - 8 : n]
                copies.append(pltpu.make_async_copy(ref.at[c, z], dst.at[c, z], sems.at[len(copies)]))
                copies[-1].start()

    patch(columns, e2_ref, e_ref, e_hbm, e_rows)
    row = iota((8, n), 1)
    up = lambda f: jnp.where(row == n - 1, 0.0, pltpu.roll(f, n - 1, 1))
    put_lines(turned_ref, seam_magnetic(1.0, [seam_ref[k] for k in range(15)], up))
    turned_ref[24:128] = jnp.zeros((104, n), F32)
    patch(turned_ref[...].T, h2_ref, h_ref, h_hbm, h_rows)
    grad_ext = jnp.concatenate(extended(grad_ref[...], columns), axis=1)
    part = dot3(halves(grad_ext), (across_high[...], across_low[...]))
    inner_ref[...] = dot3(halves(around_ref[...]), halves(part))
    rows = pl.ds(EDGE, n - 2 * EDGE)
    copies.append(pltpu.make_async_copy(inner_ref.at[rows], out_hbm.at[rows], sems.at[len(copies)]))
    copies[-1].start()
    for copy in copies:
        copy.wait()


def x_kernel(ra_ref, rb_ref, lo_ref, hi_ref, e_rows, h_rows, inner_ref, across_high, across_low, along_ref, near_ref,
             e_in, h_in, out_in, e_hbm, h_hbm, out_hbm, ends_ref, out_ref, sems):
    n, m = inner_ref.shape
    wide = lo_ref.shape[1]
    first_even = even("gx")
    tile_lane = iota((8, 128), 1)

    def unfold(message):
        outer = []
        for k in range(LO_ROWS // 8):
            at = 2 * LO_ROWS + 8 * (k // 3)
            moved = pltpu.roll(message[at : at + 8], 128 - REACH - 2 * REACH * (k % 3), 1)
            outer.append(jnp.where((tile_lane < REACH) | (tile_lane >= 128 - REACH), moved, 0.0))
        return jnp.concatenate([message[0:LO_ROWS], message[LO_ROWS : 2 * LO_ROWS], jnp.concatenate(outer, axis=0)], axis=1)

    right = unfold(jnp.where(first_even, ra_ref[...], rb_ref[...]))
    left = unfold(jnp.where(first_even, rb_ref[...], ra_ref[...]))
    a, b = seam_inputs(left, hi_ref[...], lo_ref[...], right)
    raw = jnp.concatenate([left[0:FILT], right[0:FILT]], axis=0)
    part = dot3(halves(raw), (across_high[...], across_low[...]))
    far = dot3(halves(along_ref[...]), halves(part))
    d = seam(-1.0, a, b, lambda f: pltpu.roll(f, wide - 1, 1), lambda f: pltpu.roll(f, 1, 1))
    gb0, gb1, ga = d["gb0"], d["gb1"], d["ga"]
    top = iota((8, wide), 0)
    change = jnp.zeros((8, wide), F32)
    for k, row in enumerate((ga[0:1], gb0[0:1], gb1[0:1], ga[2:3], gb0[2:3], gb1[2:3])):
        change = jnp.where(top == k, row, change)
    taps = filter_taps()
    moved = change[:, 0:m] * taps[0]
    for k in range(1, FILT + 1):
        moved = moved + taps[k] * (pltpu.roll(change, k, 1)[:, 0:m] + pltpu.roll(change, wide - k, 1)[:, 0:m])
    for side, at in ((0, 0), (1, n - EDGE)):
        rows = inner_ref[at : at + EDGE]
        for k in range(3 * side, 3 * side + 3):
            rows = rows + near_ref[k] * moved[k : k + 1]
        out_ref[side] = rows
    out_ref[0, 0:FILT] += far[0:FILT]
    out_ref[1, EDGE - FILT : EDGE] += far[FILT : 2 * FILT]
    copies = []
    for side, at in ((0, 0), (1, n - EDGE)):
        copies.append(pltpu.make_async_copy(out_ref.at[side], out_hbm.at[pl.ds(at, EDGE)], sems.at[side]))
        copies[-1].start()
    sub = iota((8, m), 0)
    magnetic = seam_magnetic(-1.0, d["v"], lambda f: pltpu.roll(f, wide - 1, 1))
    for f, (field, rows, dst) in enumerate(((d["e"], e_rows, e_hbm), (magnetic, h_rows, h_hbm))):
        for c, name in enumerate(("n", "t", "z")):
            before, end, begin, after = (value[:, 0:m] for value in field[name])
            for z in range(2):
                ends_ref[0, f, c, z] = rows[c, z, 0:8] + jnp.where(
                    sub == 0, begin[z : z + 1], jnp.where(sub == 1, after[z : z + 1], 0.0)
                )
                ends_ref[1, f, c, z] = rows[c, z, 8:16] + jnp.where(
                    sub == 6, before[2 + z : 3 + z], jnp.where(sub == 7, end[2 + z : 3 + z], 0.0)
                )
        for side, at in ((0, 0), (1, n - 8)):
            dst_rows = dst.at[:, :, pl.ds(at, 8)]
            copies.append(pltpu.make_async_copy(ends_ref.at[side, f], dst_rows, sems.at[len(copies)]))
            copies[-1].start()
    for copy in copies:
        copy.wait()


def swap_pairs(count, which):
    if which == 0:
        return [(i, i ^ 1) for i in range(count)]
    return [(i, (i - 1) % count if i % 2 == 0 else (i + 1) % count) for i in range(count)]


def call(kernel, shapes, ins, scratch=(), far=(), sems=0, far_out=(), aliases=None):
    vmem = pl.BlockSpec(memory_space=pltpu.VMEM)
    hbm = pl.BlockSpec(memory_space=pltpu.HBM)
    ins = [pltpu.with_memory_space_constraint(x, pltpu.HBM) if k in far else x for k, x in enumerate(ins)]
    scratches = [s if hasattr(s, "dtype") else pltpu.VMEM(s, F32) for s in scratch]
    if sems:
        scratches.append(pltpu.SemaphoreType.DMA((sems,)))
    return pl.pallas_call(
        kernel,
        out_shape=[s if hasattr(s, "dtype") else jax.ShapeDtypeStruct(s, F32) for s in shapes],
        in_specs=[hbm if k in far else vmem for k in range(len(ins))],
        out_specs=[hbm if k in far_out else vmem for k in range(len(shapes))],
        scratch_shapes=scratches,
        input_output_aliases=aliases or {},
        compiler_params=pltpu.CompilerParams(vmem_limit_bytes=24 * 1024 * 1024),
    )(*ins)


def body(adj_e, adj_h, fwd_e, labels, eps_table, density):
    n, m = labels.shape
    block = adj_e.shape
    nz = block[1]
    gx, gy = lax.axis_size("gx"), lax.axis_size("gy")
    message = (LO_ROWS + 8, n)
    labels_in = jax.ShapeDtypeStruct((n, m), jnp.int32)
    up, down, ylo, yhi, *fetched = call(
        first_kernel,
        [message, message, (LO_ROWS, n), (HI_ROWS, n), block, block, fwd_e.shape, labels_in, (n, m), (NMAT, m)],
        [adj_e, adj_h, fwd_e, labels, density, eps_table],
        [pltpu.SMEM((NMAT,), F32)],
        range(6),
        7,
    )
    left = lax.ppermute(up, "gy", [(i, (i + 1) % gy) for i in range(gy)])
    right = lax.ppermute(down, "gy", [(i, (i - 1) % gy) for i in range(gy)])
    wide = m + 128
    bands = jax.ShapeDtypeStruct((wide, m), jnp.bfloat16)
    xlo, xhi, grad, e2, h2, across_high, across_low, along, around, near = call(
        solve_kernel,
        [(LO_ROWS, m), (HI_ROWS, m), (n, m), block, block, bands, bands, (2 * FILT, 2 * FILT), (n, n), (6, EDGE, m)],
        fetched,
    )
    message = (2 * LO_ROWS + 16, 128)
    xa, xb, lo_ext, hi_ext, cols, seams = call(
        y_kernel,
        [message, message, (LO_ROWS, wide), (HI_ROWS, wide), (n, 128), (15, 8, n)],
        [left, right, ylo, yhi, xlo, xhi, grad],
        [(128, n)],
    )
    got_a = lax.ppermute(xa, "gx", swap_pairs(gx, 0))
    got_b = lax.ppermute(xb, "gx", swap_pairs(gx, 1))
    ends = (3, nz, 16, m)
    electric, magnetic, filtered, e_rows, h_rows, inner = call(
        patch_kernel,
        [block, block, (n, m), ends, ends, (n, m)],
        [cols, seams, e2, h2, grad, across_high, across_low, around],
        [block, block, (128, n)],
        sems=13,
        far_out=(0, 1, 2),
    )
    return tuple(
        call(
            x_kernel,
            [block, block, (n, m)],
            [got_a, got_b, lo_ext, hi_ext, e_rows, h_rows, inner, across_high, across_low, along, near]
            + [electric, magnetic, filtered],
            [(2, 2, 3, nz, 8, m), (2, EDGE, m)],
            (11, 12, 13),
            6,
            (0, 1, 2),
            {11: 0, 12: 1, 13: 2},
        )
    )


def solution(mesh):
    return jax.shard_map(
        body,
        mesh=mesh,
        in_specs=(
            P("design", None, "gx", "gy"),
            P("design", None, "gx", "gy"),
            P("design", None, None, "gx", "gy"),
            P(("design", "gx"), "gy"),
            P(),
            P(("design", "gx"), "gy"),
        ),
        out_specs=(
            P("design", None, "gx", "gy"),
            P("design", None, "gx", "gy"),
            P(("design", "gx"), "gy"),
        ),
        check_vma=False,
    )
```

```python
import math

import jax
import jax.numpy as jnp
from jax import lax
from jax.experimental import pallas as pl
from jax.experimental.pallas import tpu as pltpu
from jax.sharding import PartitionSpec as P

STEPS = 2
NMAT = 8
FILT = 16

courant = 0.5
spread_ratio = 0.6

F32 = jnp.float32

LO_G, LO_E1T, LO_E1Z, LO_E2T, LO_E2Z = 0, 16, 18, 20, 22
LO_F0T, LO_F0Z, LO_F1T, LO_F1N, LO_F1Z = 24, 26, 28, 30, 32
LO_W1T, LO_W1Z, LO_R0, LO_R1, LO_ROWS = 34, 36, 38, 39, 40
HI_G, HI_H0T, HI_H0Z, HI_H1T, HI_H1Z = 0, 16, 18, 20, 22
HI_WT, HI_WN, HI_WZ, HI_R, HI_ROWS = 24, 26, 28, 30, 32
PACK_F1, PACK_R, PACK_PAIR, PACK_F0, PACK_END = 16, 34, 37, 53, 57
LO_LANES = (
    list(range(FILT))
    + [PACK_PAIR + 2 * j + 1 for j in range(8)]
    + [PACK_F0 + j for j in range(4)]
    + [PACK_F1 + 3 * k + 1 for k in range(6)]
    + [PACK_F1 + 3 * k + 2 for k in (0, 1, 4, 5)]
    + [PACK_R + 1, PACK_R + 2]
)
HI_LANES = (
    list(range(128 - FILT, 128))
    + [PACK_PAIR + 2 * j for j in range(8)]
    + [PACK_F1 + 3 * k for k in range(6)]
    + [PACK_R, PACK_END]
)
REACH = FILT + 2
GROUP = 24
EDGE = 24
LO_REST, HI_REST = LO_ROWS - FILT, HI_ROWS - FILT - 1

TURN_G, TURN_OWN, TURN_X = 48, 80, 88


def filter_taps():
    spread = spread_ratio * FILT
    norm = math.sqrt(sum(math.exp(-d * d / (spread * spread)) for d in range(-FILT, FILT + 1)))
    return [math.exp(-d * d / (2.0 * spread * spread)) / norm for d in range(FILT + 1)]


def tap(distance):
    spread = spread_ratio * FILT
    norm = math.sqrt(sum(math.exp(-d * d / (spread * spread)) for d in range(-FILT, FILT + 1)))
    far = distance.astype(F32)
    value = jnp.exp(-far * far / (2.0 * spread * spread)) / norm
    return jnp.where(jnp.abs(distance) <= FILT, value, F32(0.0))


def exact_dot(a, b):
    return jnp.dot(a, b, precision=lax.Precision.HIGHEST, preferred_element_type=F32)


def iota(shape, dim):
    return lax.broadcasted_iota(jnp.int32, shape, dim)


def updates(n, m, nz):
    row, col = iota((n, m), 0), iota((n, m), 1)

    def lx(f):
        return jnp.where(row == 0, 0.0, pltpu.roll(f, 1, 0))

    def ux(f):
        return jnp.where(row == n - 1, 0.0, pltpu.roll(f, n - 1, 0))

    def ly(f):
        return jnp.where(col == 0, 0.0, pltpu.roll(f, 1, 1))

    def uy(f):
        return jnp.where(col == m - 1, 0.0, pltpu.roll(f, m - 1, 1))

    def turn(h, ratio):
        out = [[None] * nz for _ in range(3)]
        for z in range(nz):
            hx, hy, hz = h[0][z], h[1][z], h[2][z]
            dzx = hx - h[0][z - 1] if z > 0 else hx
            dzy = hy - h[1][z - 1] if z > 0 else hy
            out[0][z] = ratio * ((hz - ly(hz)) - dzy)
            out[1][z] = ratio * (dzx - (hz - lx(hz)))
            out[2][z] = ratio * ((hy - lx(hy)) - (hx - ly(hx)))
        return out

    def magnetic(e, h):
        out = [[None] * nz for _ in range(3)]
        for z in range(nz):
            ex, ey, ez = e[0][z], e[1][z], e[2][z]
            dzx = e[0][z + 1] - ex if z < nz - 1 else -ex
            dzy = e[1][z + 1] - ey if z < nz - 1 else -ey
            out[0][z] = h[0][z] + courant * ((uy(ez) - ez) - dzy)
            out[1][z] = h[1][z] + courant * (dzx - (ux(ez) - ez))
            out[2][z] = h[2][z] + courant * ((ux(ey) - ey) - (uy(ex) - ex))
        return out

    return turn, magnetic


def less(e, change):
    return [[a - b for a, b in zip(one, other, strict=True)] for one, other in zip(e, change, strict=True)]


def product(e, f):
    total = None
    for c in range(3):
        for z in range(len(e[c])):
            term = e[c][z] * f[c][z]
            total = term if total is None else total + term
    return total


def local_solve(e0, h0, saved, ratio):
    turn, magnetic = updates(*ratio.shape, len(e0[0]))
    e1 = less(e0, turn(h0, ratio))
    h1 = magnetic(e1, h0)
    fwd = [saved(0)]
    grad = product(e1, fwd[0])
    e2 = less(e1, turn(h1, ratio))
    fwd.append(saved(1))
    grad = grad + product(e2, fwd[1])
    return e1, h1, e2, grad, fwd


def depth_shifts(shape):
    odd = iota(shape, 0) % 2 == 1
    return (
        lambda f: jnp.where(odd, 0.0, pltpu.roll(f, 7, 0)),
        lambda f: jnp.where(odd, pltpu.roll(f, 1, 0), 0.0),
    )


def seam_magnetic(sgn, v, up):
    half = sgn * courant
    uz, _ = depth_shifts(v[0].shape)
    e2t, e2n, e2z, f2t, f2z, g2t, g2n, g2z, ah1t, ah1z, bh1t, bh1n, bh1z, e2t_b, e2z_b = v
    none = jnp.zeros_like(e2t)
    return {
        "t": (
            half * g2z,
            ah1t + half * ((e2z_b - g2z) - (uz(g2n) - g2n)),
            bh1t + half * ((f2z - e2z) - (uz(e2n) - e2n)),
            -half * f2z,
        ),
        "n": (
            none,
            half * ((uz(g2t) - g2t) - (up(g2z) - g2z)),
            bh1n + half * ((uz(e2t) - e2t) - (up(e2z) - e2z)),
            half * ((uz(f2t) - f2t) - (up(f2z) - f2z)),
        ),
        "z": (
            -half * g2t,
            ah1z + half * ((up(g2n) - g2n) - (e2t_b - g2t)),
            bh1z + half * ((up(e2n) - e2n) - (f2t - e2t)),
            half * f2t,
        ),
    }


def seam(sgn, a, b, up, down):
    odd = iota(a["h0t"].shape, 0) % 2 == 1
    half = sgn * courant
    uz, lz = depth_shifts(a["h0t"].shape)
    rb, rb1, ra = sgn * b["r0"], sgn * b["r1"], sgn * a["r"]
    d = {}
    e1t = rb * a["h0z"]
    e1z = -rb * a["h0t"]
    e1t_b = b["e1t"] + e1t
    e1z_b = b["e1z"] + e1z
    ah1t = half * e1z_b
    ah1z = -half * e1t_b
    h1t_a = a["h1t"] + ah1t
    h1z_a = a["h1z"] + ah1z
    bh1t = -half * e1z
    bh1n = half * ((uz(e1t) - e1t) - (up(e1z) - e1z))
    bh1z = half * e1t
    e2t = e1t - rb * ((bh1z - h1z_a) - (bh1n - lz(bh1n)))
    e2n = -rb * ((bh1t - lz(bh1t)) - (bh1z - down(bh1z)))
    e2z = e1z - rb * ((bh1n - down(bh1n)) - (bh1t - h1t_a))
    f2t = rb1 * bh1z
    f2z = -rb1 * bh1t
    at = ah1z
    an = (ah1t - lz(ah1t)) - (ah1z - down(ah1z))
    az = -ah1t
    g2t, g2n, g2z = -ra * at, -ra * an, -ra * az
    gb0 = b["f0t"] * e1t + b["f0z"] * e1z + b["f1t"] * e2t + b["f1n"] * e2n + b["f1z"] * e2z
    gb1 = sgn * (b["w1t"] * bh1z - b["w1z"] * bh1t)
    ga = -sgn * (a["wt"] * at + a["wn"] * an + a["wz"] * az)
    e2t_b = b["e2t"] + e2t
    e2z_b = b["e2z"] + e2z
    d["b_e1z"], d["b_h1n"], d["b_h1z"], d["a_h1z"] = e1z, bh1n, bh1z, ah1z
    none = jnp.zeros_like(e1t)
    d["e"] = {"t": (none, g2t, e2t, f2t), "n": (none, g2n, e2n, none), "z": (none, g2z, e2z, f2z)}
    d["v"] = (e2t, e2n, e2z, f2t, f2z, g2t, g2n, g2z, ah1t, ah1z, bh1t, bh1n, bh1z, e2t_b, e2z_b)
    d["gb0"], d["gb1"], d["ga"] = (g + pltpu.roll(g, 7, 0) for g in (gb0, gb1, ga))
    return d


def two(first, second, at, count=2):
    if count == 1:
        one, other = first[at : at + 1], second[at : at + 1]
        parts = [one, one, other, other]
    else:
        parts = [first[at : at + 2], second[at : at + 2]]
    parts.append(jnp.zeros((4, first.shape[1]), F32))
    return jnp.concatenate(parts, axis=0)


def seam_inputs(left_hi, my_hi, my_lo, right_lo):
    a = {
        "h0t": two(left_hi, my_hi, HI_H0T),
        "h0z": two(left_hi, my_hi, HI_H0Z),
        "h1t": two(left_hi, my_hi, HI_H1T),
        "h1z": two(left_hi, my_hi, HI_H1Z),
        "wt": two(left_hi, my_hi, HI_WT),
        "wn": two(left_hi, my_hi, HI_WN),
        "wz": two(left_hi, my_hi, HI_WZ),
        "r": two(left_hi, my_hi, HI_R, 1),
    }
    b = {
        "e1t": two(my_lo, right_lo, LO_E1T),
        "e1z": two(my_lo, right_lo, LO_E1Z),
        "e2t": two(my_lo, right_lo, LO_E2T),
        "e2z": two(my_lo, right_lo, LO_E2Z),
        "f0t": two(my_lo, right_lo, LO_F0T),
        "f0z": two(my_lo, right_lo, LO_F0Z),
        "f1t": two(my_lo, right_lo, LO_F1T),
        "f1n": two(my_lo, right_lo, LO_F1N),
        "f1z": two(my_lo, right_lo, LO_F1Z),
        "w1t": two(my_lo, right_lo, LO_W1T),
        "w1z": two(my_lo, right_lo, LO_W1Z),
        "r0": two(my_lo, right_lo, LO_R0, 1),
        "r1": two(my_lo, right_lo, LO_R1, 1),
    }
    return a, b


def even(axis):
    return lax.axis_index(axis) % 2 == 0


def ratio_of(labels, density, table):
    eps = jnp.broadcast_to(table[0], labels.shape)
    for k in range(1, NMAT):
        eps = jnp.where(labels == k, table[k], eps)
    return courant / (eps + density)


def planes(ref, *lead):
    return [[ref[(*lead, c, z)] for z in range(ref.shape[-3])] for c in range(3)]


def edge_lists(t, nrm, e1, h0, h1, e2, fwd, ratio):
    zs = range(len(e1[0]))
    lo = (
        [(e1[c][z], 0) for c in (t, 2) for z in zs]
        + [(e2[c][z], 0) for c in (t, 2) for z in zs]
        + [(fwd[0][c][z], 0) for c in (t, 2) for z in zs]
        + [(fwd[1][c][z], 0) for c in (t, nrm, 2) for z in zs]
        + [((ratio, fwd[1][c][z]), 1) for c in (t, 2) for z in zs]
        + [(ratio, 0), (ratio, 1)]
    )
    hi = (
        [(h0[c][z], -1) for c in (t, 2) for z in zs]
        + [(h1[c][z], -1) for c in (t, 2) for z in zs]
        + [((ratio, fwd[1][c][z]), -1) for c in (t, nrm, 2) for z in zs]
        + [(ratio, -1)]
    )
    return lo, hi


def fold(plane):
    m = plane.shape[1]
    lane = iota((plane.shape[0], 128), 1)
    return jnp.where(lane < 64, plane[:, 0:128], plane[:, m - 128 : m])


def place(pack, values, base, count=3):
    lane = iota(pack.shape, 1)
    return jnp.where((lane >= base) & (lane < base + count), pltpu.roll(values, base + 1, 1), pack)


def unpack_rows(packed, lanes, ref):
    ref[0:FILT] = packed[lanes[0] : lanes[0] + FILT]
    for k in range(FILT, len(lanes)):
        ref[k : k + 1] = packed[lanes[k] : lanes[k] + 1]


def line(item, at):
    if isinstance(item, tuple):
        return line(item[0], at) * line(item[1], at)
    at = at % item.shape[0]
    return item[at : at + 1]


def side_by_side(tiles, width, first):
    lane = iota((8, 128), 1)
    out = None
    for k, tile in enumerate(tiles):
        moved = pltpu.roll(tile, (width * k - first) % 128, 1)
        out = moved if out is None else jnp.where(lane < width * k, out, moved)
    return out


def first_kernel(e_hbm, h_hbm, f_hbm, lab_hbm, den_hbm, eps_hbm,
                 up_ref, down_ref, lo_ref, hi_ref, e_ref, h_ref, f_ref, lab_ref, den_ref, table_ref,
                 tab_ref, sems):
    n, m = lab_hbm.shape
    nz = e_hbm.shape[1]
    copies = []
    for src, dst in ((h_hbm, h_ref), (lab_hbm, lab_ref), (den_hbm, den_ref), (eps_hbm, tab_ref), (e_hbm, e_ref),
                     (f_hbm.at[0], f_ref.at[0]), (f_hbm.at[1], f_ref.at[1])):
        copies.append(pltpu.make_async_copy(src, dst, sems.at[len(copies)]))
        copies[-1].start()

    def folded(ref, *lead):
        return [[fold(plane) for plane in comp] for comp in planes(ref, *lead)]

    turn, magnetic = updates(n, 128, nz)
    sides = [(c, z) for c in (0, 2) for z in range(nz)]
    lane = iota((n, 128), 1)
    for copy in copies[1:4]:
        copy.wait()
    ratio = ratio_of(fold(lab_ref[...]), fold(den_ref[...]), tab_ref)
    copies[0].wait()
    h0 = folded(h_ref)
    change = turn(h0, ratio)
    copies[4].wait()
    e1 = less(folded(e_ref), change)
    h1 = magnetic(e1, h0)
    e2 = less(e1, turn(h1, ratio))
    pack = place(jnp.zeros((n, 128), F32), ratio, PACK_R)
    for k, (first, last) in enumerate(((e1, h0), (e2, h1))):
        for j, (c, z) in enumerate(sides):
            pack = place(pack, jnp.where(lane < 64, first[c][z], last[c][z]), PACK_PAIR + 8 * k + 2 * j, 2)
    copies[5].wait()
    fwd = [folded(f_ref, 0)]
    grad = product(e1, fwd[0])
    for j, (c, z) in enumerate(sides):
        pack = jnp.where(lane == PACK_F0 + j, pltpu.roll(fwd[0][c][z], PACK_F0 + j, 1), pack)
    copies[6].wait()
    fwd.append(folded(f_ref, 1))
    grad = grad + product(e2, fwd[1])
    pack = jnp.where((lane < FILT) | (lane >= 128 - FILT), grad, pack)
    scale = jnp.where(lane == 0, 1.0, ratio)
    for k, (c, z) in enumerate((c, z) for c in range(3) for z in range(nz)):
        pack = place(pack, fwd[1][c][z] * scale, PACK_F1 + 3 * k)
    packed = pack.T
    unpack_rows(packed, LO_LANES, lo_ref)
    unpack_rows(packed, HI_LANES, hi_ref)
    lo, hi = edge_lists(1, 0, e1, h0, h1, e2, fwd, ratio)
    rest = [line(*entry) for entry in lo + hi]
    rest = jnp.concatenate(rest + [jnp.zeros((1, 128), F32)], axis=0)
    tiles = [rest[8 * k : 8 * k + 8] for k in range(rest.shape[0] // 8)]
    down_ref[0:LO_ROWS] = lo_ref[...]
    down_ref[LO_ROWS : LO_ROWS + 8] = side_by_side(tiles, GROUP, 0)
    up_ref[0:HI_ROWS] = hi_ref[...]
    up_ref[HI_ROWS:LO_ROWS] = jnp.zeros((LO_ROWS - HI_ROWS, n), F32)
    up_ref[LO_ROWS : LO_ROWS + 8] = side_by_side(tiles, GROUP, 128 - REACH)
    for k in range(NMAT):
        table_ref[k : k + 1] = jnp.full((1, m), tab_ref[k], F32)


def solve_kernel(e_ref, h_ref, f_ref, lab_ref, den_ref, table_ref,
                 lo_ref, hi_ref, grad_ref, e2_ref, h2_ref, across_ref, along_ref, around_ref, near_ref):
    n, m = lab_ref.shape
    nz = e_ref.shape[1]
    ratio = ratio_of(lab_ref[...], den_ref[...], [table_ref[k : k + 1] for k in range(NMAT)])
    h0 = planes(h_ref)
    e1, h1, e2, grad, fwd = local_solve(planes(e_ref), h0, lambda step: planes(f_ref, step), ratio)
    grad_ref[...] = grad
    lo, hi = edge_lists(1, 0, e1, h0, h1, e2, fwd, ratio)
    for ref, group, strip in ((hi_ref, hi, grad[n - FILT : n]), (lo_ref, lo, grad[0:FILT])):
        ref[0:FILT] = strip
        for k, (item, at) in enumerate(group):
            ref[FILT + k : FILT + k + 1] = line(item, at)
    hi_ref[HI_ROWS - 1 : HI_ROWS] = jnp.zeros((1, m), F32)
    _, magnetic = updates(n, m, nz)
    h2 = magnetic(e2, h1)
    for c in range(3):
        for z in range(nz):
            e2_ref[c, z] = e2[c][z]
            h2_ref[c, z] = h2[c][z]
    wide = across_ref.shape[0]
    across_ref[...] = tap(cyclic(iota((wide, m), 0) - iota((wide, m), 1), wide))
    around_ref[...] = tap(iota((n, n), 0) - iota((n, n), 1))
    k, r = iota(along_ref.shape, 1), iota(along_ref.shape, 0)
    same = (k < FILT) == (r < FILT)
    along_ref[...] = jnp.where(same, tap(k - r + jnp.where(r < FILT, -FILT, FILT)), 0.0)
    r = iota((EDGE, m), 0)
    for k in range(3):
        near_ref[k] = tap(r - (k - 1))
        near_ref[3 + k] = tap(r - EDGE - (k - 1))


def put_lines(ref, lines):
    for c, name in enumerate(("t", "n", "z")):
        before, end, begin, after = lines[name]
        for z in range(2):
            p = 4 * (2 * c + z)
            ref[p : p + 1] = before[2 + z : 3 + z]
            ref[p + 1 : p + 2] = end[2 + z : 3 + z]
            ref[p + 2 : p + 3] = begin[z : z + 1]
            ref[p + 3 : p + 4] = after[z : z + 1]


def extended(grad, columns):
    m = grad.shape[1]
    lane = iota(columns.shape, 1)
    own = pltpu.roll(columns, 128 - TURN_OWN - 1, 1)
    outside = jnp.where(lane < FILT, pltpu.roll(columns, 128 - TURN_G, 1), 0.0)
    return [
        grad[:, 0:128] + jnp.where(lane < 2, own, 0.0),
        grad[:, m - 128 : m] + jnp.where(lane == 127, own, 0.0),
        jnp.where(lane >= 128 - FILT, pltpu.roll(columns, 128 - TURN_G - 2 * FILT, 1), outside),
    ]


def y_kernel(left_ref, right_ref, lo_ref, hi_ref, xlo_ref, xhi_ref, grad_ref,
             a_ref, b_ref, lo_ext, hi_ext, cols_ref, seam_ref, turned_ref):
    n, m = grad_ref.shape
    right, left = right_ref[0:LO_ROWS], left_ref[0:HI_ROWS]
    a, b = seam_inputs(left, hi_ref[...], lo_ref[...], right)
    lane = iota((8, n), 1)
    d = seam(
        1.0, a, b,
        lambda f: jnp.where(lane == n - 1, 0.0, pltpu.roll(f, n - 1, 1)),
        lambda f: jnp.where(lane == 0, 0.0, pltpu.roll(f, 1, 1)),
    )
    for k, value in enumerate(d["v"]):
        seam_ref[k] = value
    put_lines(turned_ref, d["e"])
    turned_ref[24:TURN_G] = jnp.zeros((TURN_G - 24, n), F32)
    gb0, gb1, ga = d["gb0"], d["gb1"], d["ga"]
    top = iota((8, n), 0)
    at = TURN_G
    turned_ref[at : at + 8] = right[0:8] + jnp.where(top == 0, gb0[2:3], jnp.where(top == 1, gb1[2:3], 0.0))
    turned_ref[at + 8 : at + 16] = right[8:16]
    turned_ref[at + 16 : at + 24] = left[0:8]
    turned_ref[at + 24 : at + 32] = left[8:16] + jnp.where(top == 7, ga[0:1], 0.0)
    turned_ref[TURN_OWN : TURN_OWN + 8] = jnp.where(
        top == 0, ga[2:3], jnp.where(top == 1, gb0[0:1], jnp.where(top == 2, gb1[0:1], 0.0))
    )
    none = jnp.zeros((8, n), F32)
    for k, (last, first) in enumerate(((none, d["b_e1z"]), (none, d["b_h1n"]), (d["a_h1z"], d["b_h1z"]))):
        for z in range(2):
            p = TURN_X + 4 * (2 * k + z)
            turned_ref[p : p + 1] = last[2 + z : 3 + z]
            turned_ref[p + 1 : p + 2] = first[z : z + 1]
            turned_ref[p + 2 : p + 3] = last[z : z + 1]
            turned_ref[p + 3 : p + 4] = first[2 + z : 3 + z]
    turned_ref[TURN_X + 24 : 128] = jnp.zeros((128 - TURN_X - 24, n), F32)
    columns = turned_ref[...].T
    cols_ref[...] = columns

    lane = iota((8, 128), 1)
    right_tile, left_tile = right_ref[LO_ROWS : LO_ROWS + 8], left_ref[LO_ROWS : LO_ROWS + 8]
    rest = []
    for k in range(LO_ROWS // 8):
        part = jnp.where(lane < REACH, pltpu.roll(right_tile, (128 - GROUP * k) % 128, 1), 0.0)
        rest.append(jnp.where(lane >= 128 - REACH, pltpu.roll(left_tile, (128 - REACH - GROUP * k) % 128, 1), part))
    rest = jnp.concatenate(rest, axis=0)
    for ref, mine, strip, halo in (
        (lo_ext, xlo_ref, slice(0, FILT), rest[0:LO_REST]),
        (hi_ext, xhi_ref, slice(n - FILT, n), rest[LO_REST : LO_REST + HI_REST]),
    ):
        count = mine.shape[0]
        for k, tile in enumerate(extended(grad_ref[strip], columns[strip])):
            ref[0:FILT, 128 * k : 128 * k + 128] = tile
        ref[FILT:count, 0:m] = mine[FILT:count]
        ref[FILT : FILT + halo.shape[0], m : m + 128] = halo
    hi_ext[HI_ROWS - 1 : HI_ROWS, m : m + 128] = jnp.zeros((1, 128), F32)
    one = iota((1, 128), 1)
    first, last = columns[0:1], columns[n - 1 : n]

    def add(ref, k, row, at, halo=True):
        inner = pltpu.roll(row, (127 - at) % 128, 1)
        ref[k : k + 1, 0:128] += jnp.where(one < (1 if halo else 2), inner, 0.0)
        ref[k : k + 1, m - 128 : m] += jnp.where(one == 127, inner, 0.0)
        if halo:
            outer = pltpu.roll(row, (125 - at) % 128, 1)
            ref[k : k + 1, m : m + 128] += jnp.where((one == 127) | (one == 0), outer, 0.0)

    for z in range(2):
        add(lo_ext, LO_E1Z + z, first, TURN_X + 4 * z)
        add(hi_ext, HI_H1T + z, last, TURN_X + 8 + 4 * z)
        add(hi_ext, HI_H1Z + z, last, TURN_X + 16 + 4 * z)
        add(lo_ext, LO_E2T + z, first, 4 * (2 + z) + 1, False)
        add(lo_ext, LO_E2Z + z, first, 4 * (4 + z) + 1, False)

    first_even = even("gx")
    low = lo_ext[...]
    high = jnp.concatenate([hi_ext[...], jnp.zeros((LO_ROWS - HI_ROWS, m + 128), F32)], axis=0)
    for ref, part in ((a_ref, jnp.where(first_even, high, low)), (b_ref, jnp.where(first_even, low, high))):
        ref[0:LO_ROWS] = part[:, 0:128]
        ref[LO_ROWS : 2 * LO_ROWS] = part[:, 128:256]
        tiles = [part[8 * k : 8 * k + 8, m : m + 128] for k in range(LO_ROWS // 8)]
        ref[2 * LO_ROWS : 2 * LO_ROWS + 8] = side_by_side(tiles[:3], 2 * REACH, 128 - REACH)
        ref[2 * LO_ROWS + 8 : 2 * LO_ROWS + 16] = side_by_side(tiles[3:], 2 * REACH, 128 - REACH)


def cyclic(d, count):
    return jnp.where(d > count // 2, d - count, jnp.where(d < -(count // 2), d + count, d))


def patch_kernel(cols_ref, seam_ref, e2_ref, h2_ref, grad_ref, across_ref, around_ref,
                 e_hbm, h_hbm, out_hbm, e_rows, h_rows, inner_ref,
                 e_ref, h_ref, turned_ref, sems):
    n, m = grad_ref.shape
    lane = iota((n, 128), 1)
    columns = cols_ref[...]
    copies = []

    def patch(columns, src, ref, dst, rows):
        for c in range(3):
            for z in range(2):
                p = 4 * (2 * c + z)
                moved = pltpu.roll(columns, (126 - p) % 128, 1)
                ref[c, z, :, 0:128] = src[c, z, :, 0:128] + jnp.where(lane < 2, moved, 0.0)
                ref[c, z, :, m - 128 : m] = src[c, z, :, m - 128 : m] + jnp.where(lane >= 126, moved, 0.0)
                rows[c, z, 0:8] = ref[c, z, 0:8]
                rows[c, z, 8:16] = ref[c, z, n - 8 : n]
                copies.append(pltpu.make_async_copy(ref.at[c, z], dst.at[c, z], sems.at[len(copies)]))
                copies[-1].start()

    patch(columns, e2_ref, e_ref, e_hbm, e_rows)
    row = iota((8, n), 1)
    up = lambda f: jnp.where(row == n - 1, 0.0, pltpu.roll(f, n - 1, 1))
    put_lines(turned_ref, seam_magnetic(1.0, [seam_ref[k] for k in range(15)], up))
    turned_ref[24:128] = jnp.zeros((104, n), F32)
    patch(turned_ref[...].T, h2_ref, h_ref, h_hbm, h_rows)
    grad_ext = jnp.concatenate(extended(grad_ref[...], columns), axis=1)
    part = exact_dot(grad_ext, across_ref[...])
    inner_ref[...] = exact_dot(around_ref[...], part)
    rows = pl.ds(EDGE, n - 2 * EDGE)
    copies.append(pltpu.make_async_copy(inner_ref.at[rows], out_hbm.at[rows], sems.at[len(copies)]))
    copies[-1].start()
    for copy in copies:
        copy.wait()


def x_kernel(ra_ref, rb_ref, lo_ref, hi_ref, e_rows, h_rows, inner_ref, across_ref, along_ref, near_ref,
             e_in, h_in, out_in, e_hbm, h_hbm, out_hbm, ends_ref, out_ref, sems):
    n, m = inner_ref.shape
    wide = lo_ref.shape[1]
    first_even = even("gx")
    tile_lane = iota((8, 128), 1)

    def unfold(message):
        outer = []
        for k in range(LO_ROWS // 8):
            at = 2 * LO_ROWS + 8 * (k // 3)
            moved = pltpu.roll(message[at : at + 8], 128 - REACH - 2 * REACH * (k % 3), 1)
            outer.append(jnp.where((tile_lane < REACH) | (tile_lane >= 128 - REACH), moved, 0.0))
        return jnp.concatenate([message[0:LO_ROWS], message[LO_ROWS : 2 * LO_ROWS], jnp.concatenate(outer, axis=0)], axis=1)

    right = unfold(jnp.where(first_even, ra_ref[...], rb_ref[...]))
    left = unfold(jnp.where(first_even, rb_ref[...], ra_ref[...]))
    a, b = seam_inputs(left, hi_ref[...], lo_ref[...], right)
    raw = jnp.concatenate([left[0:FILT], right[0:FILT]], axis=0)
    part = exact_dot(raw, across_ref[...])
    far = exact_dot(along_ref[...], part)
    d = seam(-1.0, a, b, lambda f: pltpu.roll(f, wide - 1, 1), lambda f: pltpu.roll(f, 1, 1))
    gb0, gb1, ga = d["gb0"], d["gb1"], d["ga"]
    top = iota((8, wide), 0)
    change = jnp.zeros((8, wide), F32)
    for k, row in enumerate((ga[0:1], gb0[0:1], gb1[0:1], ga[2:3], gb0[2:3], gb1[2:3])):
        change = jnp.where(top == k, row, change)
    taps = filter_taps()
    moved = change[:, 0:m] * taps[0]
    for k in range(1, FILT + 1):
        moved = moved + taps[k] * (pltpu.roll(change, k, 1)[:, 0:m] + pltpu.roll(change, wide - k, 1)[:, 0:m])
    for side, at in ((0, 0), (1, n - EDGE)):
        rows = inner_ref[at : at + EDGE]
        for k in range(3 * side, 3 * side + 3):
            rows = rows + near_ref[k] * moved[k : k + 1]
        out_ref[side] = rows
    out_ref[0, 0:FILT] += far[0:FILT]
    out_ref[1, EDGE - FILT : EDGE] += far[FILT : 2 * FILT]
    copies = []
    for side, at in ((0, 0), (1, n - EDGE)):
        copies.append(pltpu.make_async_copy(out_ref.at[side], out_hbm.at[pl.ds(at, EDGE)], sems.at[side]))
        copies[-1].start()
    sub = iota((8, m), 0)
    magnetic = seam_magnetic(-1.0, d["v"], lambda f: pltpu.roll(f, wide - 1, 1))
    for f, (field, rows, dst) in enumerate(((d["e"], e_rows, e_hbm), (magnetic, h_rows, h_hbm))):
        for c, name in enumerate(("n", "t", "z")):
            before, end, begin, after = (value[:, 0:m] for value in field[name])
            for z in range(2):
                ends_ref[0, f, c, z] = rows[c, z, 0:8] + jnp.where(
                    sub == 0, begin[z : z + 1], jnp.where(sub == 1, after[z : z + 1], 0.0)
                )
                ends_ref[1, f, c, z] = rows[c, z, 8:16] + jnp.where(
                    sub == 6, before[2 + z : 3 + z], jnp.where(sub == 7, end[2 + z : 3 + z], 0.0)
                )
        for side, at in ((0, 0), (1, n - 8)):
            dst_rows = dst.at[:, :, pl.ds(at, 8)]
            copies.append(pltpu.make_async_copy(ends_ref.at[side, f], dst_rows, sems.at[len(copies)]))
            copies[-1].start()
    for copy in copies:
        copy.wait()


def swap_pairs(count, which):
    if which == 0:
        return [(i, i ^ 1) for i in range(count)]
    return [(i, (i - 1) % count if i % 2 == 0 else (i + 1) % count) for i in range(count)]


def call(kernel, shapes, ins, scratch=(), far=(), sems=0, far_out=(), aliases=None):
    vmem = pl.BlockSpec(memory_space=pltpu.VMEM)
    hbm = pl.BlockSpec(memory_space=pltpu.HBM)
    ins = [pltpu.with_memory_space_constraint(x, pltpu.HBM) if k in far else x for k, x in enumerate(ins)]
    scratches = [s if hasattr(s, "dtype") else pltpu.VMEM(s, F32) for s in scratch]
    if sems:
        scratches.append(pltpu.SemaphoreType.DMA((sems,)))
    return pl.pallas_call(
        kernel,
        out_shape=[s if hasattr(s, "dtype") else jax.ShapeDtypeStruct(s, F32) for s in shapes],
        in_specs=[hbm if k in far else vmem for k in range(len(ins))],
        out_specs=[hbm if k in far_out else vmem for k in range(len(shapes))],
        scratch_shapes=scratches,
        input_output_aliases=aliases or {},
        compiler_params=pltpu.CompilerParams(vmem_limit_bytes=24 * 1024 * 1024),
    )(*ins)


def body(adj_e, adj_h, fwd_e, labels, eps_table, density):
    n, m = labels.shape
    block = adj_e.shape
    nz = block[1]
    gx, gy = lax.axis_size("gx"), lax.axis_size("gy")
    message = (LO_ROWS + 8, n)
    labels_in = jax.ShapeDtypeStruct((n, m), jnp.int32)
    up, down, ylo, yhi, *fetched = call(
        first_kernel,
        [message, message, (LO_ROWS, n), (HI_ROWS, n), block, block, fwd_e.shape, labels_in, (n, m), (NMAT, m)],
        [adj_e, adj_h, fwd_e, labels, density, eps_table],
        [pltpu.SMEM((NMAT,), F32)],
        range(6),
        7,
    )
    left = lax.ppermute(up, "gy", [(i, (i + 1) % gy) for i in range(gy)])
    right = lax.ppermute(down, "gy", [(i, (i - 1) % gy) for i in range(gy)])
    wide = m + 128
    xlo, xhi, grad, e2, h2, across_ref, along, around, near = call(
        solve_kernel,
        [(LO_ROWS, m), (HI_ROWS, m), (n, m), block, block, (wide, m), (2 * FILT, 2 * FILT), (n, n), (6, EDGE, m)],
        fetched,
    )
    message = (2 * LO_ROWS + 16, 128)
    xa, xb, lo_ext, hi_ext, cols, seams = call(
        y_kernel,
        [message, message, (LO_ROWS, wide), (HI_ROWS, wide), (n, 128), (15, 8, n)],
        [left, right, ylo, yhi, xlo, xhi, grad],
        [(128, n)],
    )
    got_a = lax.ppermute(xa, "gx", swap_pairs(gx, 0))
    got_b = lax.ppermute(xb, "gx", swap_pairs(gx, 1))
    ends = (3, nz, 16, m)
    electric, magnetic, filtered, e_rows, h_rows, inner = call(
        patch_kernel,
        [block, block, (n, m), ends, ends, (n, m)],
        [cols, seams, e2, h2, grad, across_ref, around],
        [block, block, (128, n)],
        sems=13,
        far_out=(0, 1, 2),
    )
    return tuple(
        call(
            x_kernel,
            [block, block, (n, m)],
            [got_a, got_b, lo_ext, hi_ext, e_rows, h_rows, inner, across_ref, along, near]
            + [electric, magnetic, filtered],
            [(2, 2, 3, nz, 8, m), (2, EDGE, m)],
            (10, 11, 12),
            6,
            (0, 1, 2),
            {10: 0, 11: 1, 12: 2},
        )
    )


def solution(mesh):
    return jax.shard_map(
        body,
        mesh=mesh,
        in_specs=(
            P("design", None, "gx", "gy"),
            P("design", None, "gx", "gy"),
            P("design", None, None, "gx", "gy"),
            P(("design", "gx"), "gy"),
            P(),
            P(("design", "gx"), "gy"),
        ),
        out_specs=(
            P("design", None, "gx", "gy"),
            P("design", None, "gx", "gy"),
            P(("design", "gx"), "gy"),
        ),
        check_vma=False,
    )
```

```python
import math

import jax
import jax.numpy as jnp
from jax import lax
from jax.experimental import pallas as pl
from jax.experimental.pallas import tpu as pltpu
from jax.sharding import PartitionSpec as P

STEPS = 2
NMAT = 8
FILT = 16

courant = 0.5
spread_ratio = 0.6

F32 = jnp.float32

LO_G, LO_E1T, LO_E1Z, LO_E2T, LO_E2Z = 0, 16, 18, 20, 22
LO_F0T, LO_F0Z, LO_F1T, LO_F1N, LO_F1Z = 24, 26, 28, 30, 32
LO_W1T, LO_W1Z, LO_R0, LO_R1, LO_ROWS = 34, 36, 38, 39, 40
HI_G, HI_H0T, HI_H0Z, HI_H1T, HI_H1Z = 0, 16, 18, 20, 22
HI_WT, HI_WN, HI_WZ, HI_R, HI_ROWS = 24, 26, 28, 30, 32
PACK_F1, PACK_R, PACK_PAIR, PACK_F0, PACK_END = 16, 34, 37, 53, 57
LO_LANES = (
    list(range(FILT))
    + [PACK_PAIR + 2 * j + 1 for j in range(8)]
    + [PACK_F0 + j for j in range(4)]
    + [PACK_F1 + 3 * k + 1 for k in range(6)]
    + [PACK_F1 + 3 * k + 2 for k in (0, 1, 4, 5)]
    + [PACK_R + 1, PACK_R + 2]
)
HI_LANES = (
    list(range(128 - FILT, 128))
    + [PACK_PAIR + 2 * j for j in range(8)]
    + [PACK_F1 + 3 * k for k in range(6)]
    + [PACK_R, PACK_END]
)
REACH = FILT + 2
GROUP = 24
EDGE = 24
LO_REST, HI_REST = LO_ROWS - FILT, HI_ROWS - FILT - 1

TURN_G, TURN_OWN, TURN_X = 48, 80, 88


def filter_taps():
    spread = spread_ratio * FILT
    norm = math.sqrt(sum(math.exp(-d * d / (spread * spread)) for d in range(-FILT, FILT + 1)))
    return [math.exp(-d * d / (2.0 * spread * spread)) / norm for d in range(FILT + 1)]


def tap(distance):
    spread = spread_ratio * FILT
    norm = math.sqrt(sum(math.exp(-d * d / (spread * spread)) for d in range(-FILT, FILT + 1)))
    far = distance.astype(F32)
    value = jnp.exp(-far * far / (2.0 * spread * spread)) / norm
    return jnp.where(jnp.abs(distance) <= FILT, value, F32(0.0))


def exact_dot(a, b):
    return jnp.dot(a, b, precision=lax.Precision.HIGHEST, preferred_element_type=F32)


def iota(shape, dim):
    return lax.broadcasted_iota(jnp.int32, shape, dim)


def updates(n, m, nz):
    row, col = iota((n, m), 0), iota((n, m), 1)

    def lx(f):
        return jnp.where(row == 0, 0.0, pltpu.roll(f, 1, 0))

    def ux(f):
        return jnp.where(row == n - 1, 0.0, pltpu.roll(f, n - 1, 0))

    def ly(f):
        return jnp.where(col == 0, 0.0, pltpu.roll(f, 1, 1))

    def uy(f):
        return jnp.where(col == m - 1, 0.0, pltpu.roll(f, m - 1, 1))

    def turn(h, ratio):
        out = [[None] * nz for _ in range(3)]
        for z in range(nz):
            hx, hy, hz = h[0][z], h[1][z], h[2][z]
            dzx = hx - h[0][z - 1] if z > 0 else hx
            dzy = hy - h[1][z - 1] if z > 0 else hy
            out[0][z] = ratio * ((hz - ly(hz)) - dzy)
            out[1][z] = ratio * (dzx - (hz - lx(hz)))
            out[2][z] = ratio * ((hy - lx(hy)) - (hx - ly(hx)))
        return out

    def magnetic(e, h):
        out = [[None] * nz for _ in range(3)]
        for z in range(nz):
            ex, ey, ez = e[0][z], e[1][z], e[2][z]
            dzx = e[0][z + 1] - ex if z < nz - 1 else -ex
            dzy = e[1][z + 1] - ey if z < nz - 1 else -ey
            out[0][z] = h[0][z] + courant * ((uy(ez) - ez) - dzy)
            out[1][z] = h[1][z] + courant * (dzx - (ux(ez) - ez))
            out[2][z] = h[2][z] + courant * ((ux(ey) - ey) - (uy(ex) - ex))
        return out

    return turn, magnetic


def less(e, change):
    return [[a - b for a, b in zip(one, other, strict=True)] for one, other in zip(e, change, strict=True)]


def product(e, f):
    total = None
    for c in range(3):
        for z in range(len(e[c])):
            term = e[c][z] * f[c][z]
            total = term if total is None else total + term
    return total


def local_solve(e0, h0, saved, ratio):
    turn, magnetic = updates(*ratio.shape, len(e0[0]))
    e1 = less(e0, turn(h0, ratio))
    h1 = magnetic(e1, h0)
    fwd = [saved(0)]
    grad = product(e1, fwd[0])
    e2 = less(e1, turn(h1, ratio))
    fwd.append(saved(1))
    grad = grad + product(e2, fwd[1])
    return e1, h1, e2, grad, fwd


def depth_shifts(shape):
    odd = iota(shape, 0) % 2 == 1
    return (
        lambda f: jnp.where(odd, 0.0, pltpu.roll(f, 7, 0)),
        lambda f: jnp.where(odd, pltpu.roll(f, 1, 0), 0.0),
    )


def seam_magnetic(sgn, v, up):
    half = sgn * courant
    uz, _ = depth_shifts(v[0].shape)
    e2t, e2n, e2z, f2t, f2z, g2t, g2n, g2z, ah1t, ah1z, bh1t, bh1n, bh1z, e2t_b, e2z_b = v
    none = jnp.zeros_like(e2t)
    return {
        "t": (
            half * g2z,
            ah1t + half * ((e2z_b - g2z) - (uz(g2n) - g2n)),
            bh1t + half * ((f2z - e2z) - (uz(e2n) - e2n)),
            -half * f2z,
        ),
        "n": (
            none,
            half * ((uz(g2t) - g2t) - (up(g2z) - g2z)),
            bh1n + half * ((uz(e2t) - e2t) - (up(e2z) - e2z)),
            half * ((uz(f2t) - f2t) - (up(f2z) - f2z)),
        ),
        "z": (
            -half * g2t,
            ah1z + half * ((up(g2n) - g2n) - (e2t_b - g2t)),
            bh1z + half * ((up(e2n) - e2n) - (f2t - e2t)),
            half * f2t,
        ),
    }


def seam(sgn, a, b, up, down):
    odd = iota(a["h0t"].shape, 0) % 2 == 1
    half = sgn * courant
    uz, lz = depth_shifts(a["h0t"].shape)
    rb, rb1, ra = sgn * b["r0"], sgn * b["r1"], sgn * a["r"]
    d = {}
    e1t = rb * a["h0z"]
    e1z = -rb * a["h0t"]
    e1t_b = b["e1t"] + e1t
    e1z_b = b["e1z"] + e1z
    ah1t = half * e1z_b
    ah1z = -half * e1t_b
    h1t_a = a["h1t"] + ah1t
    h1z_a = a["h1z"] + ah1z
    bh1t = -half * e1z
    bh1n = half * ((uz(e1t) - e1t) - (up(e1z) - e1z))
    bh1z = half * e1t
    e2t = e1t - rb * ((bh1z - h1z_a) - (bh1n - lz(bh1n)))
    e2n = -rb * ((bh1t - lz(bh1t)) - (bh1z - down(bh1z)))
    e2z = e1z - rb * ((bh1n - down(bh1n)) - (bh1t - h1t_a))
    f2t = rb1 * bh1z
    f2z = -rb1 * bh1t
    at = ah1z
    an = (ah1t - lz(ah1t)) - (ah1z - down(ah1z))
    az = -ah1t
    g2t, g2n, g2z = -ra * at, -ra * an, -ra * az
    gb0 = b["f0t"] * e1t + b["f0z"] * e1z + b["f1t"] * e2t + b["f1n"] * e2n + b["f1z"] * e2z
    gb1 = sgn * (b["w1t"] * bh1z - b["w1z"] * bh1t)
    ga = -sgn * (a["wt"] * at + a["wn"] * an + a["wz"] * az)
    e2t_b = b["e2t"] + e2t
    e2z_b = b["e2z"] + e2z
    d["b_e1z"], d["b_h1n"], d["b_h1z"], d["a_h1z"] = e1z, bh1n, bh1z, ah1z
    none = jnp.zeros_like(e1t)
    d["e"] = {"t": (none, g2t, e2t, f2t), "n": (none, g2n, e2n, none), "z": (none, g2z, e2z, f2z)}
    d["v"] = (e2t, e2n, e2z, f2t, f2z, g2t, g2n, g2z, ah1t, ah1z, bh1t, bh1n, bh1z, e2t_b, e2z_b)
    d["gb0"], d["gb1"], d["ga"] = (g + pltpu.roll(g, 7, 0) for g in (gb0, gb1, ga))
    return d


def two(first, second, at, count=2):
    if count == 1:
        one, other = first[at : at + 1], second[at : at + 1]
        parts = [one, one, other, other]
    else:
        parts = [first[at : at + 2], second[at : at + 2]]
    parts.append(jnp.zeros((4, first.shape[1]), F32))
    return jnp.concatenate(parts, axis=0)


def seam_inputs(left_hi, my_hi, my_lo, right_lo):
    a = {
        "h0t": two(left_hi, my_hi, HI_H0T),
        "h0z": two(left_hi, my_hi, HI_H0Z),
        "h1t": two(left_hi, my_hi, HI_H1T),
        "h1z": two(left_hi, my_hi, HI_H1Z),
        "wt": two(left_hi, my_hi, HI_WT),
        "wn": two(left_hi, my_hi, HI_WN),
        "wz": two(left_hi, my_hi, HI_WZ),
        "r": two(left_hi, my_hi, HI_R, 1),
    }
    b = {
        "e1t": two(my_lo, right_lo, LO_E1T),
        "e1z": two(my_lo, right_lo, LO_E1Z),
        "e2t": two(my_lo, right_lo, LO_E2T),
        "e2z": two(my_lo, right_lo, LO_E2Z),
        "f0t": two(my_lo, right_lo, LO_F0T),
        "f0z": two(my_lo, right_lo, LO_F0Z),
        "f1t": two(my_lo, right_lo, LO_F1T),
        "f1n": two(my_lo, right_lo, LO_F1N),
        "f1z": two(my_lo, right_lo, LO_F1Z),
        "w1t": two(my_lo, right_lo, LO_W1T),
        "w1z": two(my_lo, right_lo, LO_W1Z),
        "r0": two(my_lo, right_lo, LO_R0, 1),
        "r1": two(my_lo, right_lo, LO_R1, 1),
    }
    return a, b


def even(axis):
    return lax.axis_index(axis) % 2 == 0


def ratio_of(labels, density, table):
    eps = jnp.broadcast_to(table[0], labels.shape)
    for k in range(1, NMAT):
        eps = jnp.where(labels == k, table[k], eps)
    return courant / (eps + density)


def planes(ref, *lead):
    return [[ref[(*lead, c, z)] for z in range(ref.shape[-3])] for c in range(3)]


def edge_lists(t, nrm, e1, h0, h1, e2, fwd, ratio):
    zs = range(len(e1[0]))
    lo = (
        [(e1[c][z], 0) for c in (t, 2) for z in zs]
        + [(e2[c][z], 0) for c in (t, 2) for z in zs]
        + [(fwd[0][c][z], 0) for c in (t, 2) for z in zs]
        + [(fwd[1][c][z], 0) for c in (t, nrm, 2) for z in zs]
        + [((ratio, fwd[1][c][z]), 1) for c in (t, 2) for z in zs]
        + [(ratio, 0), (ratio, 1)]
    )
    hi = (
        [(h0[c][z], -1) for c in (t, 2) for z in zs]
        + [(h1[c][z], -1) for c in (t, 2) for z in zs]
        + [((ratio, fwd[1][c][z]), -1) for c in (t, nrm, 2) for z in zs]
        + [(ratio, -1)]
    )
    return lo, hi


def fold(plane):
    m = plane.shape[1]
    lane = iota((plane.shape[0], 128), 1)
    return jnp.where(lane < 64, plane[:, 0:128], plane[:, m - 128 : m])


def place(pack, values, base, count=3):
    lane = iota(pack.shape, 1)
    return jnp.where((lane >= base) & (lane < base + count), pltpu.roll(values, base + 1, 1), pack)


def unpack_rows(packed, lanes, ref):
    ref[0:FILT] = packed[lanes[0] : lanes[0] + FILT]
    for k in range(FILT, len(lanes)):
        ref[k : k + 1] = packed[lanes[k] : lanes[k] + 1]


def line(item, at):
    if isinstance(item, tuple):
        return line(item[0], at) * line(item[1], at)
    at = at % item.shape[0]
    return item[at : at + 1]


def side_by_side(tiles, width, first):
    lane = iota((8, 128), 1)
    out = None
    for k, tile in enumerate(tiles):
        moved = pltpu.roll(tile, (width * k - first) % 128, 1)
        out = moved if out is None else jnp.where(lane < width * k, out, moved)
    return out


def first_kernel(e_hbm, h_hbm, f_hbm, lab_hbm, den_hbm, eps_hbm,
                 up_ref, down_ref, lo_ref, hi_ref, e_ref, h_ref, f_ref, lab_ref, den_ref, table_ref,
                 tab_ref, sems):
    n, m = lab_hbm.shape
    nz = e_hbm.shape[1]
    copies = []
    for src, dst in ((h_hbm, h_ref), (lab_hbm, lab_ref), (den_hbm, den_ref), (eps_hbm, tab_ref), (e_hbm, e_ref),
                     (f_hbm.at[0], f_ref.at[0]), (f_hbm.at[1], f_ref.at[1])):
        copies.append(pltpu.make_async_copy(src, dst, sems.at[len(copies)]))
        copies[-1].start()

    def folded(ref, *lead):
        return [[fold(plane) for plane in comp] for comp in planes(ref, *lead)]

    turn, magnetic = updates(n, 128, nz)
    sides = [(c, z) for c in (0, 2) for z in range(nz)]
    lane = iota((n, 128), 1)
    for copy in copies[1:4]:
        copy.wait()
    ratio = ratio_of(fold(lab_ref[...]), fold(den_ref[...]), tab_ref)
    copies[0].wait()
    h0 = folded(h_ref)
    change = turn(h0, ratio)
    copies[4].wait()
    e1 = less(folded(e_ref), change)
    h1 = magnetic(e1, h0)
    e2 = less(e1, turn(h1, ratio))
    pack = place(jnp.zeros((n, 128), F32), ratio, PACK_R)
    for k, (first, last) in enumerate(((e1, h0), (e2, h1))):
        for j, (c, z) in enumerate(sides):
            pack = place(pack, jnp.where(lane < 64, first[c][z], last[c][z]), PACK_PAIR + 8 * k + 2 * j, 2)
    copies[5].wait()
    fwd = [folded(f_ref, 0)]
    grad = product(e1, fwd[0])
    for j, (c, z) in enumerate(sides):
        pack = jnp.where(lane == PACK_F0 + j, pltpu.roll(fwd[0][c][z], PACK_F0 + j, 1), pack)
    copies[6].wait()
    fwd.append(folded(f_ref, 1))
    grad = grad + product(e2, fwd[1])
    pack = jnp.where((lane < FILT) | (lane >= 128 - FILT), grad, pack)
    scale = jnp.where(lane == 0, 1.0, ratio)
    for k, (c, z) in enumerate((c, z) for c in range(3) for z in range(nz)):
        pack = place(pack, fwd[1][c][z] * scale, PACK_F1 + 3 * k)
    packed = pack.T
    unpack_rows(packed, LO_LANES, lo_ref)
    unpack_rows(packed, HI_LANES, hi_ref)
    lo, hi = edge_lists(1, 0, e1, h0, h1, e2, fwd, ratio)
    rest = [line(*entry) for entry in lo + hi]
    rest = jnp.concatenate(rest + [jnp.zeros((1, 128), F32)], axis=0)
    tiles = [rest[8 * k : 8 * k + 8] for k in range(rest.shape[0] // 8)]
    down_ref[0:LO_ROWS] = lo_ref[...]
    down_ref[LO_ROWS : LO_ROWS + 8] = side_by_side(tiles, GROUP, 0)
    up_ref[0:HI_ROWS] = hi_ref[...]
    up_ref[HI_ROWS:LO_ROWS] = jnp.zeros((LO_ROWS - HI_ROWS, n), F32)
    up_ref[LO_ROWS : LO_ROWS + 8] = side_by_side(tiles, GROUP, 128 - REACH)
    for k in range(NMAT):
        table_ref[k : k + 1] = jnp.full((1, m), tab_ref[k], F32)


def solve_kernel(e_ref, h_ref, f_ref, lab_ref, den_ref, table_ref,
                 lo_ref, hi_ref, grad_ref, e2_ref, h2_ref, across_ref, along_ref, around_ref, near_ref):
    n, m = lab_ref.shape
    nz = e_ref.shape[1]
    ratio = ratio_of(lab_ref[...], den_ref[...], [table_ref[k : k + 1] for k in range(NMAT)])
    h0 = planes(h_ref)
    e1, h1, e2, grad, fwd = local_solve(planes(e_ref), h0, lambda step: planes(f_ref, step), ratio)
    grad_ref[...] = grad
    lo, hi = edge_lists(1, 0, e1, h0, h1, e2, fwd, ratio)
    for ref, group, strip in ((hi_ref, hi, grad[n - FILT : n]), (lo_ref, lo, grad[0:FILT])):
        ref[0:FILT] = strip
        for k, (item, at) in enumerate(group):
            ref[FILT + k : FILT + k + 1] = line(item, at)
    hi_ref[HI_ROWS - 1 : HI_ROWS] = jnp.zeros((1, m), F32)
    _, magnetic = updates(n, m, nz)
    h2 = magnetic(e2, h1)
    for c in range(3):
        for z in range(nz):
            e2_ref[c, z] = e2[c][z]
            h2_ref[c, z] = h2[c][z]
    wide = across_ref.shape[0]
    across_ref[...] = tap(cyclic(iota((wide, m), 0) - iota((wide, m), 1), wide))
    around_ref[...] = tap(iota((n, n), 0) - iota((n, n), 1))
    k, r = iota(along_ref.shape, 1), iota(along_ref.shape, 0)
    same = (k < FILT) == (r < FILT)
    along_ref[...] = jnp.where(same, tap(k - r + jnp.where(r < FILT, -FILT, FILT)), 0.0)
    r = iota((EDGE, m), 0)
    for k in range(3):
        near_ref[k] = tap(r - (k - 1))
        near_ref[3 + k] = tap(r - EDGE - (k - 1))


def put_lines(ref, lines):
    for c, name in enumerate(("t", "n", "z")):
        before, end, begin, after = lines[name]
        for z in range(2):
            p = 4 * (2 * c + z)
            ref[p : p + 1] = before[2 + z : 3 + z]
            ref[p + 1 : p + 2] = end[2 + z : 3 + z]
            ref[p + 2 : p + 3] = begin[z : z + 1]
            ref[p + 3 : p + 4] = after[z : z + 1]


def extended(grad, columns):
    m = grad.shape[1]
    lane = iota(columns.shape, 1)
    own = pltpu.roll(columns, 128 - TURN_OWN - 1, 1)
    outside = jnp.where(lane < FILT, pltpu.roll(columns, 128 - TURN_G, 1), 0.0)
    return [
        grad[:, 0:128] + jnp.where(lane < 2, own, 0.0),
        grad[:, m - 128 : m] + jnp.where(lane == 127, own, 0.0),
        jnp.where(lane >= 128 - FILT, pltpu.roll(columns, 128 - TURN_G - 2 * FILT, 1), outside),
    ]


def y_kernel(left_ref, right_ref, lo_ref, hi_ref, xlo_ref, xhi_ref, grad_ref,
             a_ref, b_ref, lo_ext, hi_ext, cols_ref, seam_ref, turned_ref):
    n, m = grad_ref.shape
    right, left = right_ref[0:LO_ROWS], left_ref[0:HI_ROWS]
    a, b = seam_inputs(left, hi_ref[...], lo_ref[...], right)
    lane = iota((8, n), 1)
    d = seam(
        1.0, a, b,
        lambda f: jnp.where(lane == n - 1, 0.0, pltpu.roll(f, n - 1, 1)),
        lambda f: jnp.where(lane == 0, 0.0, pltpu.roll(f, 1, 1)),
    )
    for k, value in enumerate(d["v"]):
        seam_ref[k] = value
    put_lines(turned_ref, d["e"])
    turned_ref[24:TURN_G] = jnp.zeros((TURN_G - 24, n), F32)
    gb0, gb1, ga = d["gb0"], d["gb1"], d["ga"]
    top = iota((8, n), 0)
    at = TURN_G
    turned_ref[at : at + 8] = right[0:8] + jnp.where(top == 0, gb0[2:3], jnp.where(top == 1, gb1[2:3], 0.0))
    turned_ref[at + 8 : at + 16] = right[8:16]
    turned_ref[at + 16 : at + 24] = left[0:8]
    turned_ref[at + 24 : at + 32] = left[8:16] + jnp.where(top == 7, ga[0:1], 0.0)
    turned_ref[TURN_OWN : TURN_OWN + 8] = jnp.where(
        top == 0, ga[2:3], jnp.where(top == 1, gb0[0:1], jnp.where(top == 2, gb1[0:1], 0.0))
    )
    none = jnp.zeros((8, n), F32)
    for k, (last, first) in enumerate(((none, d["b_e1z"]), (none, d["b_h1n"]), (d["a_h1z"], d["b_h1z"]))):
        for z in range(2):
            p = TURN_X + 4 * (2 * k + z)
            turned_ref[p : p + 1] = last[2 + z : 3 + z]
            turned_ref[p + 1 : p + 2] = first[z : z + 1]
            turned_ref[p + 2 : p + 3] = last[z : z + 1]
            turned_ref[p + 3 : p + 4] = first[2 + z : 3 + z]
    turned_ref[TURN_X + 24 : 128] = jnp.zeros((128 - TURN_X - 24, n), F32)
    columns = turned_ref[...].T
    cols_ref[...] = columns

    lane = iota((8, 128), 1)
    right_tile, left_tile = right_ref[LO_ROWS : LO_ROWS + 8], left_ref[LO_ROWS : LO_ROWS + 8]
    rest = []
    for k in range(LO_ROWS // 8):
        part = jnp.where(lane < REACH, pltpu.roll(right_tile, (128 - GROUP * k) % 128, 1), 0.0)
        rest.append(jnp.where(lane >= 128 - REACH, pltpu.roll(left_tile, (128 - REACH - GROUP * k) % 128, 1), part))
    rest = jnp.concatenate(rest, axis=0)
    for ref, mine, strip, halo in (
        (lo_ext, xlo_ref, slice(0, FILT), rest[0:LO_REST]),
        (hi_ext, xhi_ref, slice(n - FILT, n), rest[LO_REST : LO_REST + HI_REST]),
    ):
        count = mine.shape[0]
        for k, tile in enumerate(extended(grad_ref[strip], columns[strip])):
            ref[0:FILT, 128 * k : 128 * k + 128] = tile
        ref[FILT:count, 0:m] = mine[FILT:count]
        ref[FILT : FILT + halo.shape[0], m : m + 128] = halo
    hi_ext[HI_ROWS - 1 : HI_ROWS, m : m + 128] = jnp.zeros((1, 128), F32)
    one = iota((1, 128), 1)
    first, last = columns[0:1], columns[n - 1 : n]

    def add(ref, k, row, at, halo=True):
        inner = pltpu.roll(row, (127 - at) % 128, 1)
        ref[k : k + 1, 0:128] += jnp.where(one < (1 if halo else 2), inner, 0.0)
        ref[k : k + 1, m - 128 : m] += jnp.where(one == 127, inner, 0.0)
        if halo:
            outer = pltpu.roll(row, (125 - at) % 128, 1)
            ref[k : k + 1, m : m + 128] += jnp.where((one == 127) | (one == 0), outer, 0.0)

    for z in range(2):
        add(lo_ext, LO_E1Z + z, first, TURN_X + 4 * z)
        add(hi_ext, HI_H1T + z, last, TURN_X + 8 + 4 * z)
        add(hi_ext, HI_H1Z + z, last, TURN_X + 16 + 4 * z)
        add(lo_ext, LO_E2T + z, first, 4 * (2 + z) + 1, False)
        add(lo_ext, LO_E2Z + z, first, 4 * (4 + z) + 1, False)

    first_even = even("gx")
    low = lo_ext[...]
    high = jnp.concatenate([hi_ext[...], jnp.zeros((LO_ROWS - HI_ROWS, m + 128), F32)], axis=0)
    for ref, part in ((a_ref, jnp.where(first_even, high, low)), (b_ref, jnp.where(first_even, low, high))):
        ref[0:LO_ROWS] = part[:, 0:128]
        ref[LO_ROWS : 2 * LO_ROWS] = part[:, 128:256]
        tiles = [part[8 * k : 8 * k + 8, m : m + 128] for k in range(LO_ROWS // 8)]
        ref[2 * LO_ROWS : 2 * LO_ROWS + 8] = side_by_side(tiles[:3], 2 * REACH, 128 - REACH)
        ref[2 * LO_ROWS + 8 : 2 * LO_ROWS + 16] = side_by_side(tiles[3:], 2 * REACH, 128 - REACH)


def cyclic(d, count):
    return jnp.where(d > count // 2, d - count, jnp.where(d < -(count // 2), d + count, d))


def patch_kernel(cols_ref, seam_ref, e2_ref, h2_ref, grad_ref, across_ref, around_ref,
                 e_hbm, h_hbm, out_hbm, e_rows, h_rows, inner_ref,
                 e_ref, h_ref, turned_ref, sems):
    n, m = grad_ref.shape
    lane = iota((n, 128), 1)
    columns = cols_ref[...]
    copies = []

    def patch(columns, src, ref, dst, rows):
        for c in range(3):
            for z in range(2):
                p = 4 * (2 * c + z)
                moved = pltpu.roll(columns, (126 - p) % 128, 1)
                ref[c, z, :, 0:128] = src[c, z, :, 0:128] + jnp.where(lane < 2, moved, 0.0)
                ref[c, z, :, m - 128 : m] = src[c, z, :, m - 128 : m] + jnp.where(lane >= 126, moved, 0.0)
                rows[c, z, 0:8] = ref[c, z, 0:8]
                rows[c, z, 8:16] = ref[c, z, n - 8 : n]
                copies.append(pltpu.make_async_copy(ref.at[c, z], dst.at[c, z], sems.at[len(copies)]))
                copies[-1].start()

    patch(columns, e2_ref, e_ref, e_hbm, e_rows)
    row = iota((8, n), 1)
    up = lambda f: jnp.where(row == n - 1, 0.0, pltpu.roll(f, n - 1, 1))
    put_lines(turned_ref, seam_magnetic(1.0, [seam_ref[k] for k in range(15)], up))
    turned_ref[24:128] = jnp.zeros((104, n), F32)
    patch(turned_ref[...].T, h2_ref, h_ref, h_hbm, h_rows)
    grad_ext = jnp.concatenate(extended(grad_ref[...], columns), axis=1)
    part = exact_dot(grad_ext, across_ref[...])
    inner_ref[...] = exact_dot(around_ref[...], part)
    rows = pl.ds(EDGE, n - 2 * EDGE)
    copies.append(pltpu.make_async_copy(inner_ref.at[rows], out_hbm.at[rows], sems.at[len(copies)]))
    copies[-1].start()
    for copy in copies:
        copy.wait()


def x_kernel(ra_ref, rb_ref, lo_ref, hi_ref, e_rows, h_rows, inner_ref, across_ref, along_ref, near_ref,
             e_in, h_in, out_in, e_hbm, h_hbm, out_hbm, ends_ref, out_ref, sems):
    n, m = inner_ref.shape
    wide = lo_ref.shape[1]
    first_even = even("gx")
    tile_lane = iota((8, 128), 1)

    def unfold(message):
        outer = []
        for k in range(LO_ROWS // 8):
            at = 2 * LO_ROWS + 8 * (k // 3)
            moved = pltpu.roll(message[at : at + 8], 128 - REACH - 2 * REACH * (k % 3), 1)
            outer.append(jnp.where((tile_lane < REACH) | (tile_lane >= 128 - REACH), moved, 0.0))
        return jnp.concatenate([message[0:LO_ROWS], message[LO_ROWS : 2 * LO_ROWS], jnp.concatenate(outer, axis=0)], axis=1)

    right = unfold(jnp.where(first_even, ra_ref[...], rb_ref[...]))
    left = unfold(jnp.where(first_even, rb_ref[...], ra_ref[...]))
    a, b = seam_inputs(left, hi_ref[...], lo_ref[...], right)
    raw = jnp.concatenate([left[0:FILT], right[0:FILT]], axis=0)
    part = exact_dot(raw, across_ref[...])
    far = exact_dot(along_ref[...], part)
    d = seam(-1.0, a, b, lambda f: pltpu.roll(f, wide - 1, 1), lambda f: pltpu.roll(f, 1, 1))
    copies = []
    sub = iota((8, m), 0)
    magnetic = seam_magnetic(-1.0, d["v"], lambda f: pltpu.roll(f, wide - 1, 1))
    for f, (field, rows, dst) in enumerate(((d["e"], e_rows, e_hbm), (magnetic, h_rows, h_hbm))):
        for c, name in enumerate(("n", "t", "z")):
            before, end, begin, after = (value[:, 0:m] for value in field[name])
            for z in range(2):
                ends_ref[0, f, c, z] = rows[c, z, 0:8] + jnp.where(
                    sub == 0, begin[z : z + 1], jnp.where(sub == 1, after[z : z + 1], 0.0)
                )
                ends_ref[1, f, c, z] = rows[c, z, 8:16] + jnp.where(
                    sub == 6, before[2 + z : 3 + z], jnp.where(sub == 7, end[2 + z : 3 + z], 0.0)
                )
        for side, at in ((0, 0), (1, n - 8)):
            dst_rows = dst.at[:, :, pl.ds(at, 8)]
            copies.append(pltpu.make_async_copy(ends_ref.at[side, f], dst_rows, sems.at[len(copies)]))
            copies[-1].start()
    gb0, gb1, ga = d["gb0"], d["gb1"], d["ga"]
    top = iota((8, wide), 0)
    change = jnp.zeros((8, wide), F32)
    for k, row in enumerate((ga[0:1], gb0[0:1], gb1[0:1], ga[2:3], gb0[2:3], gb1[2:3])):
        change = jnp.where(top == k, row, change)
    taps = filter_taps()
    moved = change[:, 0:m] * taps[0]
    for k in range(1, FILT + 1):
        moved = moved + taps[k] * (pltpu.roll(change, k, 1)[:, 0:m] + pltpu.roll(change, wide - k, 1)[:, 0:m])
    for side, at in ((0, 0), (1, n - EDGE)):
        rows = inner_ref[at : at + EDGE]
        for k in range(3 * side, 3 * side + 3):
            rows = rows + near_ref[k] * moved[k : k + 1]
        out_ref[side] = rows
    out_ref[0, 0:FILT] += far[0:FILT]
    out_ref[1, EDGE - FILT : EDGE] += far[FILT : 2 * FILT]
    for side, at in ((0, 0), (1, n - EDGE)):
        copies.append(pltpu.make_async_copy(out_ref.at[side], out_hbm.at[pl.ds(at, EDGE)], sems.at[len(copies)]))
        copies[-1].start()
    for copy in copies:
        copy.wait()


def swap_pairs(count, which):
    if which == 0:
        return [(i, i ^ 1) for i in range(count)]
    return [(i, (i - 1) % count if i % 2 == 0 else (i + 1) % count) for i in range(count)]


def call(kernel, shapes, ins, scratch=(), far=(), sems=0, far_out=(), aliases=None):
    vmem = pl.BlockSpec(memory_space=pltpu.VMEM)
    hbm = pl.BlockSpec(memory_space=pltpu.HBM)
    ins = [pltpu.with_memory_space_constraint(x, pltpu.HBM) if k in far else x for k, x in enumerate(ins)]
    scratches = [s if hasattr(s, "dtype") else pltpu.VMEM(s, F32) for s in scratch]
    if sems:
        scratches.append(pltpu.SemaphoreType.DMA((sems,)))
    return pl.pallas_call(
        kernel,
        out_shape=[s if hasattr(s, "dtype") else jax.ShapeDtypeStruct(s, F32) for s in shapes],
        in_specs=[hbm if k in far else vmem for k in range(len(ins))],
        out_specs=[hbm if k in far_out else vmem for k in range(len(shapes))],
        scratch_shapes=scratches,
        input_output_aliases=aliases or {},
        compiler_params=pltpu.CompilerParams(vmem_limit_bytes=24 * 1024 * 1024),
    )(*ins)


def body(adj_e, adj_h, fwd_e, labels, eps_table, density):
    n, m = labels.shape
    block = adj_e.shape
    nz = block[1]
    gx, gy = lax.axis_size("gx"), lax.axis_size("gy")
    message = (LO_ROWS + 8, n)
    labels_in = jax.ShapeDtypeStruct((n, m), jnp.int32)
    up, down, ylo, yhi, *fetched = call(
        first_kernel,
        [message, message, (LO_ROWS, n), (HI_ROWS, n), block, block, fwd_e.shape, labels_in, (n, m), (NMAT, m)],
        [adj_e, adj_h, fwd_e, labels, density, eps_table],
        [pltpu.SMEM((NMAT,), F32)],
        range(6),
        7,
    )
    left = lax.ppermute(up, "gy", [(i, (i + 1) % gy) for i in range(gy)])
    right = lax.ppermute(down, "gy", [(i, (i - 1) % gy) for i in range(gy)])
    wide = m + 128
    xlo, xhi, grad, e2, h2, across_ref, along, around, near = call(
        solve_kernel,
        [(LO_ROWS, m), (HI_ROWS, m), (n, m), block, block, (wide, m), (2 * FILT, 2 * FILT), (n, n), (6, EDGE, m)],
        fetched,
    )
    message = (2 * LO_ROWS + 16, 128)
    xa, xb, lo_ext, hi_ext, cols, seams = call(
        y_kernel,
        [message, message, (LO_ROWS, wide), (HI_ROWS, wide), (n, 128), (15, 8, n)],
        [left, right, ylo, yhi, xlo, xhi, grad],
        [(128, n)],
    )
    got_a = lax.ppermute(xa, "gx", swap_pairs(gx, 0))
    got_b = lax.ppermute(xb, "gx", swap_pairs(gx, 1))
    ends = (3, nz, 16, m)
    electric, magnetic, filtered, e_rows, h_rows, inner = call(
        patch_kernel,
        [block, block, (n, m), ends, ends, (n, m)],
        [cols, seams, e2, h2, grad, across_ref, around],
        [block, block, (128, n)],
        sems=13,
        far_out=(0, 1, 2),
    )
    return tuple(
        call(
            x_kernel,
            [block, block, (n, m)],
            [got_a, got_b, lo_ext, hi_ext, e_rows, h_rows, inner, across_ref, along, near]
            + [electric, magnetic, filtered],
            [(2, 2, 3, nz, 8, m), (2, EDGE, m)],
            (10, 11, 12),
            6,
            (0, 1, 2),
            {10: 0, 11: 1, 12: 2},
        )
    )


def solution(mesh):
    return jax.shard_map(
        body,
        mesh=mesh,
        in_specs=(
            P("design", None, "gx", "gy"),
            P("design", None, "gx", "gy"),
            P("design", None, None, "gx", "gy"),
            P(("design", "gx"), "gy"),
            P(),
            P(("design", "gx"), "gy"),
        ),
        out_specs=(
            P("design", None, "gx", "gy"),
            P("design", None, "gx", "gy"),
            P(("design", "gx"), "gy"),
        ),
        check_vma=False,
    )
```

```python
import math

import jax
import jax.numpy as jnp
from jax import lax
from jax.experimental import pallas as pl
from jax.experimental.pallas import tpu as pltpu
from jax.sharding import PartitionSpec as P

STEPS = 2
NMAT = 8
FILT = 16

courant = 0.5
spread_ratio = 0.6

F32 = jnp.float32

LO_G, LO_E1T, LO_E1Z, LO_E2T, LO_E2Z = 0, 16, 18, 20, 22
LO_F0T, LO_F0Z, LO_F1T, LO_F1N, LO_F1Z = 24, 26, 28, 30, 32
LO_W1T, LO_W1Z, LO_R0, LO_R1, LO_ROWS = 34, 36, 38, 39, 40
HI_G, HI_H0T, HI_H0Z, HI_H1T, HI_H1Z = 0, 16, 18, 20, 22
HI_WT, HI_WN, HI_WZ, HI_R, HI_ROWS = 24, 26, 28, 30, 32
PACK_F1, PACK_R, PACK_PAIR, PACK_F0, PACK_END = 16, 34, 37, 53, 57
LO_LANES = (
    list(range(FILT))
    + [PACK_PAIR + 2 * j + 1 for j in range(8)]
    + [PACK_F0 + j for j in range(4)]
    + [PACK_F1 + 3 * k + 1 for k in range(6)]
    + [PACK_F1 + 3 * k + 2 for k in (0, 1, 4, 5)]
    + [PACK_R + 1, PACK_R + 2]
)
HI_LANES = (
    list(range(128 - FILT, 128))
    + [PACK_PAIR + 2 * j for j in range(8)]
    + [PACK_F1 + 3 * k for k in range(6)]
    + [PACK_R, PACK_END]
)
REACH = FILT + 2
GROUP = 24
EDGE = 24
LO_REST, HI_REST = LO_ROWS - FILT, HI_ROWS - FILT - 1

TURN_G, TURN_OWN, TURN_X = 48, 80, 88


def filter_taps():
    spread = spread_ratio * FILT
    norm = math.sqrt(sum(math.exp(-d * d / (spread * spread)) for d in range(-FILT, FILT + 1)))
    return [math.exp(-d * d / (2.0 * spread * spread)) / norm for d in range(FILT + 1)]


def tap(distance):
    spread = spread_ratio * FILT
    norm = math.sqrt(sum(math.exp(-d * d / (spread * spread)) for d in range(-FILT, FILT + 1)))
    far = distance.astype(F32)
    value = jnp.exp(-far * far / (2.0 * spread * spread)) / norm
    return jnp.where(jnp.abs(distance) <= FILT, value, F32(0.0))


def thirds(x):
    high = x.astype(jnp.bfloat16)
    rest = x - high.astype(F32)
    middle = rest.astype(jnp.bfloat16)
    return high, middle, (rest - middle.astype(F32)).astype(jnp.bfloat16)


def narrow_dot(a, b):
    return jnp.dot(a, b, preferred_element_type=F32)


def exact_dot(a, b):
    return jnp.dot(a, b, precision=lax.Precision.HIGHEST, preferred_element_type=F32)


def iota(shape, dim):
    return lax.broadcasted_iota(jnp.int32, shape, dim)


def updates(n, m, nz):
    row, col = iota((n, m), 0), iota((n, m), 1)

    def lx(f):
        return jnp.where(row == 0, 0.0, pltpu.roll(f, 1, 0))

    def ux(f):
        return jnp.where(row == n - 1, 0.0, pltpu.roll(f, n - 1, 0))

    def ly(f):
        return jnp.where(col == 0, 0.0, pltpu.roll(f, 1, 1))

    def uy(f):
        return jnp.where(col == m - 1, 0.0, pltpu.roll(f, m - 1, 1))

    def turn(h, ratio):
        out = [[None] * nz for _ in range(3)]
        for z in range(nz):
            hx, hy, hz = h[0][z], h[1][z], h[2][z]
            dzx = hx - h[0][z - 1] if z > 0 else hx
            dzy = hy - h[1][z - 1] if z > 0 else hy
            out[0][z] = ratio * ((hz - ly(hz)) - dzy)
            out[1][z] = ratio * (dzx - (hz - lx(hz)))
            out[2][z] = ratio * ((hy - lx(hy)) - (hx - ly(hx)))
        return out

    def magnetic(e, h):
        out = [[None] * nz for _ in range(3)]
        for z in range(nz):
            ex, ey, ez = e[0][z], e[1][z], e[2][z]
            dzx = e[0][z + 1] - ex if z < nz - 1 else -ex
            dzy = e[1][z + 1] - ey if z < nz - 1 else -ey
            out[0][z] = h[0][z] + courant * ((uy(ez) - ez) - dzy)
            out[1][z] = h[1][z] + courant * (dzx - (ux(ez) - ez))
            out[2][z] = h[2][z] + courant * ((ux(ey) - ey) - (uy(ex) - ex))
        return out

    return turn, magnetic


def less(e, change):
    return [[a - b for a, b in zip(one, other, strict=True)] for one, other in zip(e, change, strict=True)]


def product(e, f):
    total = None
    for c in range(3):
        for z in range(len(e[c])):
            term = e[c][z] * f[c][z]
            total = term if total is None else total + term
    return total


def local_solve(e0, h0, saved, ratio):
    turn, magnetic = updates(*ratio.shape, len(e0[0]))
    e1 = less(e0, turn(h0, ratio))
    h1 = magnetic(e1, h0)
    fwd = [saved(0)]
    grad = product(e1, fwd[0])
    e2 = less(e1, turn(h1, ratio))
    fwd.append(saved(1))
    grad = grad + product(e2, fwd[1])
    return e1, h1, e2, grad, fwd


def depth_shifts(shape):
    odd = iota(shape, 0) % 2 == 1
    return (
        lambda f: jnp.where(odd, 0.0, pltpu.roll(f, 7, 0)),
        lambda f: jnp.where(odd, pltpu.roll(f, 1, 0), 0.0),
    )


def seam_magnetic(sgn, v, up):
    half = sgn * courant
    uz, _ = depth_shifts(v[0].shape)
    e2t, e2n, e2z, f2t, f2z, g2t, g2n, g2z, ah1t, ah1z, bh1t, bh1n, bh1z, e2t_b, e2z_b = v
    none = jnp.zeros_like(e2t)
    return {
        "t": (
            half * g2z,
            ah1t + half * ((e2z_b - g2z) - (uz(g2n) - g2n)),
            bh1t + half * ((f2z - e2z) - (uz(e2n) - e2n)),
            -half * f2z,
        ),
        "n": (
            none,
            half * ((uz(g2t) - g2t) - (up(g2z) - g2z)),
            bh1n + half * ((uz(e2t) - e2t) - (up(e2z) - e2z)),
            half * ((uz(f2t) - f2t) - (up(f2z) - f2z)),
        ),
        "z": (
            -half * g2t,
            ah1z + half * ((up(g2n) - g2n) - (e2t_b - g2t)),
            bh1z + half * ((up(e2n) - e2n) - (f2t - e2t)),
            half * f2t,
        ),
    }


def seam(sgn, a, b, up, down):
    odd = iota(a["h0t"].shape, 0) % 2 == 1
    half = sgn * courant
    uz, lz = depth_shifts(a["h0t"].shape)
    rb, rb1, ra = sgn * b["r0"], sgn * b["r1"], sgn * a["r"]
    d = {}
    e1t = rb * a["h0z"]
    e1z = -rb * a["h0t"]
    e1t_b = b["e1t"] + e1t
    e1z_b = b["e1z"] + e1z
    ah1t = half * e1z_b
    ah1z = -half * e1t_b
    h1t_a = a["h1t"] + ah1t
    h1z_a = a["h1z"] + ah1z
    bh1t = -half * e1z
    bh1n = half * ((uz(e1t) - e1t) - (up(e1z) - e1z))
    bh1z = half * e1t
    e2t = e1t - rb * ((bh1z - h1z_a) - (bh1n - lz(bh1n)))
    e2n = -rb * ((bh1t - lz(bh1t)) - (bh1z - down(bh1z)))
    e2z = e1z - rb * ((bh1n - down(bh1n)) - (bh1t - h1t_a))
    f2t = rb1 * bh1z
    f2z = -rb1 * bh1t
    at = ah1z
    an = (ah1t - lz(ah1t)) - (ah1z - down(ah1z))
    az = -ah1t
    g2t, g2n, g2z = -ra * at, -ra * an, -ra * az
    gb0 = b["f0t"] * e1t + b["f0z"] * e1z + b["f1t"] * e2t + b["f1n"] * e2n + b["f1z"] * e2z
    gb1 = sgn * (b["w1t"] * bh1z - b["w1z"] * bh1t)
    ga = -sgn * (a["wt"] * at + a["wn"] * an + a["wz"] * az)
    e2t_b = b["e2t"] + e2t
    e2z_b = b["e2z"] + e2z
    d["b_e1z"], d["b_h1n"], d["b_h1z"], d["a_h1z"] = e1z, bh1n, bh1z, ah1z
    none = jnp.zeros_like(e1t)
    d["e"] = {"t": (none, g2t, e2t, f2t), "n": (none, g2n, e2n, none), "z": (none, g2z, e2z, f2z)}
    d["v"] = (e2t, e2n, e2z, f2t, f2z, g2t, g2n, g2z, ah1t, ah1z, bh1t, bh1n, bh1z, e2t_b, e2z_b)
    d["gb0"], d["gb1"], d["ga"] = (g + pltpu.roll(g, 7, 0) for g in (gb0, gb1, ga))
    return d


def two(first, second, at, count=2):
    if count == 1:
        one, other = first[at : at + 1], second[at : at + 1]
        parts = [one, one, other, other]
    else:
        parts = [first[at : at + 2], second[at : at + 2]]
    parts.append(jnp.zeros((4, first.shape[1]), F32))
    return jnp.concatenate(parts, axis=0)


def seam_inputs(left_hi, my_hi, my_lo, right_lo):
    a = {
        "h0t": two(left_hi, my_hi, HI_H0T),
        "h0z": two(left_hi, my_hi, HI_H0Z),
        "h1t": two(left_hi, my_hi, HI_H1T),
        "h1z": two(left_hi, my_hi, HI_H1Z),
        "wt": two(left_hi, my_hi, HI_WT),
        "wn": two(left_hi, my_hi, HI_WN),
        "wz": two(left_hi, my_hi, HI_WZ),
        "r": two(left_hi, my_hi, HI_R, 1),
    }
    b = {
        "e1t": two(my_lo, right_lo, LO_E1T),
        "e1z": two(my_lo, right_lo, LO_E1Z),
        "e2t": two(my_lo, right_lo, LO_E2T),
        "e2z": two(my_lo, right_lo, LO_E2Z),
        "f0t": two(my_lo, right_lo, LO_F0T),
        "f0z": two(my_lo, right_lo, LO_F0Z),
        "f1t": two(my_lo, right_lo, LO_F1T),
        "f1n": two(my_lo, right_lo, LO_F1N),
        "f1z": two(my_lo, right_lo, LO_F1Z),
        "w1t": two(my_lo, right_lo, LO_W1T),
        "w1z": two(my_lo, right_lo, LO_W1Z),
        "r0": two(my_lo, right_lo, LO_R0, 1),
        "r1": two(my_lo, right_lo, LO_R1, 1),
    }
    return a, b


def even(axis):
    return lax.axis_index(axis) % 2 == 0


def ratio_of(labels, density, table):
    eps = jnp.broadcast_to(table[0], labels.shape)
    for k in range(1, NMAT):
        eps = jnp.where(labels == k, table[k], eps)
    return courant / (eps + density)


def planes(ref, *lead):
    return [[ref[(*lead, c, z)] for z in range(ref.shape[-3])] for c in range(3)]


def edge_lists(t, nrm, e1, h0, h1, e2, fwd, ratio):
    zs = range(len(e1[0]))
    lo = (
        [(e1[c][z], 0) for c in (t, 2) for z in zs]
        + [(e2[c][z], 0) for c in (t, 2) for z in zs]
        + [(fwd[0][c][z], 0) for c in (t, 2) for z in zs]
        + [(fwd[1][c][z], 0) for c in (t, nrm, 2) for z in zs]
        + [((ratio, fwd[1][c][z]), 1) for c in (t, 2) for z in zs]
        + [(ratio, 0), (ratio, 1)]
    )
    hi = (
        [(h0[c][z], -1) for c in (t, 2) for z in zs]
        + [(h1[c][z], -1) for c in (t, 2) for z in zs]
        + [((ratio, fwd[1][c][z]), -1) for c in (t, nrm, 2) for z in zs]
        + [(ratio, -1)]
    )
    return lo, hi


def fold(plane):
    m = plane.shape[1]
    lane = iota((plane.shape[0], 128), 1)
    return jnp.where(lane < 64, plane[:, 0:128], plane[:, m - 128 : m])


def place(pack, values, base, count=3):
    lane = iota((1, 128), 1)
    return jnp.where((lane >= base) & (lane < base + count), pltpu.roll(values, base + 1, 1), pack)


def unpack_rows(packed, lanes, ref):
    ref[0:FILT] = packed[lanes[0] : lanes[0] + FILT]
    for k in range(FILT, len(lanes)):
        ref[k : k + 1] = packed[lanes[k] : lanes[k] + 1]


def line(item, at):
    if isinstance(item, tuple):
        return line(item[0], at) * line(item[1], at)
    at = at % item.shape[0]
    return item[at : at + 1]


def side_by_side(tiles, width, first):
    lane = iota((8, 128), 1)
    out = None
    for k, tile in enumerate(tiles):
        moved = pltpu.roll(tile, (width * k - first) % 128, 1)
        out = moved if out is None else jnp.where(lane < width * k, out, moved)
    return out


def first_kernel(e_hbm, h_hbm, f_hbm, lab_hbm, den_hbm, eps_hbm,
                 up_ref, down_ref, lo_ref, hi_ref, e_ref, h_ref, f_ref, lab_ref, den_ref, table_ref,
                 tab_ref, sems):
    n, m = lab_hbm.shape
    nz = e_hbm.shape[1]
    copies = []
    for src, dst in ((h_hbm, h_ref), (lab_hbm, lab_ref), (den_hbm, den_ref), (eps_hbm, tab_ref), (e_hbm, e_ref),
                     (f_hbm.at[0], f_ref.at[0]), (f_hbm.at[1], f_ref.at[1])):
        copies.append(pltpu.make_async_copy(src, dst, sems.at[len(copies)]))
        copies[-1].start()

    def folded(ref, *lead):
        return [[fold(plane) for plane in comp] for comp in planes(ref, *lead)]

    turn, magnetic = updates(n, 128, nz)
    sides = [(c, z) for c in (0, 2) for z in range(nz)]
    lane = iota((n, 128), 1)
    for copy in copies[1:4]:
        copy.wait()
    ratio = ratio_of(fold(lab_ref[...]), fold(den_ref[...]), tab_ref)
    copies[0].wait()
    h0 = folded(h_ref)
    change = turn(h0, ratio)
    copies[4].wait()
    e1 = less(folded(e_ref), change)
    h1 = magnetic(e1, h0)
    e2 = less(e1, turn(h1, ratio))
    pack = place(jnp.zeros((n, 128), F32), ratio, PACK_R)
    for k, (first, last) in enumerate(((e1, h0), (e2, h1))):
        for j, (c, z) in enumerate(sides):
            pack = place(pack, jnp.where(lane < 64, first[c][z], last[c][z]), PACK_PAIR + 8 * k + 2 * j, 2)
    copies[5].wait()
    fwd = [folded(f_ref, 0)]
    grad = product(e1, fwd[0])
    for j, (c, z) in enumerate(sides):
        pack = jnp.where(lane == PACK_F0 + j, pltpu.roll(fwd[0][c][z], PACK_F0 + j, 1), pack)
    copies[6].wait()
    fwd.append(folded(f_ref, 1))
    grad = grad + product(e2, fwd[1])
    pack = jnp.where((lane < FILT) | (lane >= 128 - FILT), grad, pack)
    scale = jnp.where(lane == 0, 1.0, ratio)
    for k, (c, z) in enumerate((c, z) for c in range(3) for z in range(nz)):
        pack = place(pack, fwd[1][c][z] * scale, PACK_F1 + 3 * k)
    packed = pack.T
    unpack_rows(packed, LO_LANES, lo_ref)
    unpack_rows(packed, HI_LANES, hi_ref)
    lo, hi = edge_lists(1, 0, e1, h0, h1, e2, fwd, ratio)
    rest = [line(*entry) for entry in lo + hi]
    rest = jnp.concatenate(rest + [jnp.zeros((1, 128), F32)], axis=0)
    tiles = [rest[8 * k : 8 * k + 8] for k in range(rest.shape[0] // 8)]
    down_ref[0:LO_ROWS] = lo_ref[...]
    down_ref[LO_ROWS : LO_ROWS + 8] = side_by_side(tiles, GROUP, 0)
    up_ref[0:HI_ROWS] = hi_ref[...]
    up_ref[HI_ROWS:LO_ROWS] = jnp.zeros((LO_ROWS - HI_ROWS, n), F32)
    up_ref[LO_ROWS : LO_ROWS + 8] = side_by_side(tiles, GROUP, 128 - REACH)
    for k in range(NMAT):
        table_ref[k : k + 1] = jnp.full((1, m), tab_ref[k], F32)


def solve_kernel(e_ref, h_ref, f_ref, lab_ref, den_ref, table_ref,
                 lo_ref, hi_ref, grad_ref, e2_ref, h2_ref, across_ref, across_thirds, along_ref, around_ref, near_ref):
    n, m = lab_ref.shape
    nz = e_ref.shape[1]
    ratio = ratio_of(lab_ref[...], den_ref[...], [table_ref[k : k + 1] for k in range(NMAT)])
    h0 = planes(h_ref)
    e1, h1, e2, grad, fwd = local_solve(planes(e_ref), h0, lambda step: planes(f_ref, step), ratio)
    grad_ref[...] = grad
    lo, hi = edge_lists(1, 0, e1, h0, h1, e2, fwd, ratio)
    for ref, group, strip in ((hi_ref, hi, grad[n - FILT : n]), (lo_ref, lo, grad[0:FILT])):
        ref[0:FILT] = strip
        for k, (item, at) in enumerate(group):
            ref[FILT + k : FILT + k + 1] = line(item, at)
    hi_ref[HI_ROWS - 1 : HI_ROWS] = jnp.zeros((1, m), F32)
    _, magnetic = updates(n, m, nz)
    h2 = magnetic(e2, h1)
    for c in range(3):
        for z in range(nz):
            e2_ref[c, z] = e2[c][z]
            h2_ref[c, z] = h2[c][z]
    wide = across_ref.shape[0]
    across = tap(cyclic(iota((wide, m), 0) - iota((wide, m), 1), wide))
    across_ref[...] = across
    for k, third in enumerate(thirds(across)):
        across_thirds[k] = third
    around_ref[...] = tap(iota((n, n), 0) - iota((n, n), 1))
    k, r = iota((2 * FILT, 2 * FILT), 1), iota((2 * FILT, 2 * FILT), 0)
    same = (k < FILT) == (r < FILT)
    high, middle, low = thirds(jnp.where(same, tap(k - r + jnp.where(r < FILT, -FILT, FILT)), 0.0))
    along_ref[...] = jnp.concatenate([high, middle, low, high, middle, high], axis=1)
    r = iota((EDGE, m), 0)
    for k in range(3):
        near_ref[k] = tap(r - (k - 1))
        near_ref[3 + k] = tap(r - EDGE - (k - 1))


def put_lines(ref, lines):
    for c, name in enumerate(("t", "n", "z")):
        before, end, begin, after = lines[name]
        for z in range(2):
            p = 4 * (2 * c + z)
            ref[p : p + 1] = before[2 + z : 3 + z]
            ref[p + 1 : p + 2] = end[2 + z : 3 + z]
            ref[p + 2 : p + 3] = begin[z : z + 1]
            ref[p + 3 : p + 4] = after[z : z + 1]


def extended(grad, columns):
    m = grad.shape[1]
    lane = iota(columns.shape, 1)
    own = pltpu.roll(columns, 128 - TURN_OWN - 1, 1)
    outside = jnp.where(lane < FILT, pltpu.roll(columns, 128 - TURN_G, 1), 0.0)
    return [
        grad[:, 0:128] + jnp.where(lane < 2, own, 0.0),
        grad[:, m - 128 : m] + jnp.where(lane == 127, own, 0.0),
        jnp.where(lane >= 128 - FILT, pltpu.roll(columns, 128 - TURN_G - 2 * FILT, 1), outside),
    ]


def y_kernel(left_ref, right_ref, lo_ref, hi_ref, xlo_ref, xhi_ref, grad_ref,
             a_ref, b_ref, lo_ext, hi_ext, cols_ref, seam_ref, turned_ref):
    n, m = grad_ref.shape
    right, left = right_ref[0:LO_ROWS], left_ref[0:HI_ROWS]
    a, b = seam_inputs(left, hi_ref[...], lo_ref[...], right)
    lane = iota((8, n), 1)
    d = seam(
        1.0, a, b,
        lambda f: jnp.where(lane == n - 1, 0.0, pltpu.roll(f, n - 1, 1)),
        lambda f: jnp.where(lane == 0, 0.0, pltpu.roll(f, 1, 1)),
    )
    for k, value in enumerate(d["v"]):
        seam_ref[k] = value
    put_lines(turned_ref, d["e"])
    turned_ref[24:TURN_G] = jnp.zeros((TURN_G - 24, n), F32)
    gb0, gb1, ga = d["gb0"], d["gb1"], d["ga"]
    top = iota((8, n), 0)
    at = TURN_G
    turned_ref[at : at + 8] = right[0:8] + jnp.where(top == 0, gb0[2:3], jnp.where(top == 1, gb1[2:3], 0.0))
    turned_ref[at + 8 : at + 16] = right[8:16]
    turned_ref[at + 16 : at + 24] = left[0:8]
    turned_ref[at + 24 : at + 32] = left[8:16] + jnp.where(top == 7, ga[0:1], 0.0)
    turned_ref[TURN_OWN : TURN_OWN + 8] = jnp.where(
        top == 0, ga[2:3], jnp.where(top == 1, gb0[0:1], jnp.where(top == 2, gb1[0:1], 0.0))
    )
    none = jnp.zeros((8, n), F32)
    for k, (last, first) in enumerate(((none, d["b_e1z"]), (none, d["b_h1n"]), (d["a_h1z"], d["b_h1z"]))):
        for z in range(2):
            p = TURN_X + 4 * (2 * k + z)
            turned_ref[p : p + 1] = last[2 + z : 3 + z]
            turned_ref[p + 1 : p + 2] = first[z : z + 1]
            turned_ref[p + 2 : p + 3] = last[z : z + 1]
            turned_ref[p + 3 : p + 4] = first[2 + z : 3 + z]
    turned_ref[TURN_X + 24 : 128] = jnp.zeros((128 - TURN_X - 24, n), F32)
    columns = turned_ref[...].T
    cols_ref[...] = columns

    lane = iota((8, 128), 1)
    right_tile, left_tile = right_ref[LO_ROWS : LO_ROWS + 8], left_ref[LO_ROWS : LO_ROWS + 8]
    rest = []
    for k in range(LO_ROWS // 8):
        part = jnp.where(lane < REACH, pltpu.roll(right_tile, (128 - GROUP * k) % 128, 1), 0.0)
        rest.append(jnp.where(lane >= 128 - REACH, pltpu.roll(left_tile, (128 - REACH - GROUP * k) % 128, 1), part))
    rest = jnp.concatenate(rest, axis=0)
    for ref, mine, strip, halo in (
        (lo_ext, xlo_ref, slice(0, FILT), rest[0:LO_REST]),
        (hi_ext, xhi_ref, slice(n - FILT, n), rest[LO_REST : LO_REST + HI_REST]),
    ):
        count = mine.shape[0]
        for k, tile in enumerate(extended(grad_ref[strip], columns[strip])):
            ref[0:FILT, 128 * k : 128 * k + 128] = tile
        ref[FILT:count, 0:m] = mine[FILT:count]
        ref[FILT : FILT + halo.shape[0], m : m + 128] = halo
    hi_ext[HI_ROWS - 1 : HI_ROWS, m : m + 128] = jnp.zeros((1, 128), F32)
    one = iota((1, 128), 1)
    first, last = columns[0:1], columns[n - 1 : n]

    def add(ref, k, row, at, halo=True):
        inner = pltpu.roll(row, (127 - at) % 128, 1)
        ref[k : k + 1, 0:128] += jnp.where(one < (1 if halo else 2), inner, 0.0)
        ref[k : k + 1, m - 128 : m] += jnp.where(one == 127, inner, 0.0)
        if halo:
            outer = pltpu.roll(row, (125 - at) % 128, 1)
            ref[k : k + 1, m : m + 128] += jnp.where((one == 127) | (one == 0), outer, 0.0)

    for z in range(2):
        add(lo_ext, LO_E1Z + z, first, TURN_X + 4 * z)
        add(hi_ext, HI_H1T + z, last, TURN_X + 8 + 4 * z)
        add(hi_ext, HI_H1Z + z, last, TURN_X + 16 + 4 * z)
        add(lo_ext, LO_E2T + z, first, 4 * (2 + z) + 1, False)
        add(lo_ext, LO_E2Z + z, first, 4 * (4 + z) + 1, False)

    first_even = even("gx")
    low = lo_ext[...]
    high = jnp.concatenate([hi_ext[...], jnp.zeros((LO_ROWS - HI_ROWS, m + 128), F32)], axis=0)
    for ref, part in ((a_ref, jnp.where(first_even, high, low)), (b_ref, jnp.where(first_even, low, high))):
        ref[0:LO_ROWS] = part[:, 0:128]
        ref[LO_ROWS : 2 * LO_ROWS] = part[:, 128:256]
        tiles = [part[8 * k : 8 * k + 8, m : m + 128] for k in range(LO_ROWS // 8)]
        ref[2 * LO_ROWS : 2 * LO_ROWS + 8] = side_by_side(tiles[:3], 2 * REACH, 128 - REACH)
        ref[2 * LO_ROWS + 8 : 2 * LO_ROWS + 16] = side_by_side(tiles[3:], 2 * REACH, 128 - REACH)


def cyclic(d, count):
    return jnp.where(d > count // 2, d - count, jnp.where(d < -(count // 2), d + count, d))


def patch_kernel(cols_ref, seam_ref, e2_ref, h2_ref, grad_ref, across_ref, around_ref,
                 e_hbm, h_hbm, out_hbm, e_rows, h_rows, inner_ref,
                 e_ref, h_ref, turned_ref, sems):
    n, m = grad_ref.shape
    lane = iota((n, 128), 1)
    columns = cols_ref[...]
    copies = []

    def patch(columns, src, ref, dst, rows):
        for c in range(3):
            for z in range(2):
                p = 4 * (2 * c + z)
                moved = pltpu.roll(columns, (126 - p) % 128, 1)
                ref[c, z, :, 0:128] = src[c, z, :, 0:128] + jnp.where(lane < 2, moved, 0.0)
                ref[c, z, :, m - 128 : m] = src[c, z, :, m - 128 : m] + jnp.where(lane >= 126, moved, 0.0)
                rows[c, z, 0:8] = ref[c, z, 0:8]
                rows[c, z, 8:16] = ref[c, z, n - 8 : n]
                copies.append(pltpu.make_async_copy(ref.at[c, z], dst.at[c, z], sems.at[len(copies)]))
                copies[-1].start()

    patch(columns, e2_ref, e_ref, e_hbm, e_rows)
    row = iota((8, n), 1)
    up = lambda f: jnp.where(row == n - 1, 0.0, pltpu.roll(f, n - 1, 1))
    put_lines(turned_ref, seam_magnetic(1.0, [seam_ref[k] for k in range(15)], up))
    turned_ref[24:128] = jnp.zeros((104, n), F32)
    patch(turned_ref[...].T, h2_ref, h_ref, h_hbm, h_rows)
    grad_ext = jnp.concatenate(extended(grad_ref[...], columns), axis=1)
    part = exact_dot(grad_ext, across_ref[...])
    inner_ref[...] = exact_dot(around_ref[...], part)
    rows = pl.ds(EDGE, n - 2 * EDGE)
    copies.append(pltpu.make_async_copy(inner_ref.at[rows], out_hbm.at[rows], sems.at[len(copies)]))
    copies[-1].start()
    for copy in copies:
        copy.wait()


def x_kernel(ra_ref, rb_ref, lo_ref, hi_ref, e_rows, h_rows, inner_ref, across_thirds, along_ref, near_ref,
             e_in, h_in, out_in, e_hbm, h_hbm, out_hbm, ends_ref, out_ref, sems):
    n, m = inner_ref.shape
    wide = lo_ref.shape[1]
    first_even = even("gx")
    tile_lane = iota((8, 128), 1)

    def unfold(message):
        outer = []
        for k in range(LO_ROWS // 8):
            at = 2 * LO_ROWS + 8 * (k // 3)
            moved = pltpu.roll(message[at : at + 8], 128 - REACH - 2 * REACH * (k % 3), 1)
            outer.append(jnp.where((tile_lane < REACH) | (tile_lane >= 128 - REACH), moved, 0.0))
        return jnp.concatenate([message[0:LO_ROWS], message[LO_ROWS : 2 * LO_ROWS], jnp.concatenate(outer, axis=0)], axis=1)

    right = unfold(jnp.where(first_even, ra_ref[...], rb_ref[...]))
    left = unfold(jnp.where(first_even, rb_ref[...], ra_ref[...]))
    a, b = seam_inputs(left, hi_ref[...], lo_ref[...], right)
    raw = jnp.concatenate([left[0:FILT], right[0:FILT]], axis=0)
    high, middle, low = thirds(raw)
    one = narrow_dot(jnp.concatenate([high, middle, low], axis=0), across_thirds[0])
    two_ = narrow_dot(jnp.concatenate([high, middle], axis=0), across_thirds[1])
    three = narrow_dot(high, across_thirds[2])
    k = 2 * FILT
    part = ((one[2 * k : 3 * k] + two_[k : 2 * k] + three) + (one[k : 2 * k] + two_[0:k])) + one[0:k]
    high, middle, low = thirds(part)
    far = narrow_dot(along_ref[...], jnp.concatenate([low, middle, high, middle, high, high], axis=0))
    d = seam(-1.0, a, b, lambda f: pltpu.roll(f, wide - 1, 1), lambda f: pltpu.roll(f, 1, 1))
    copies = []
    sub = iota((8, m), 0)
    magnetic = seam_magnetic(-1.0, d["v"], lambda f: pltpu.roll(f, wide - 1, 1))
    for f, (field, rows, dst) in enumerate(((d["e"], e_rows, e_hbm), (magnetic, h_rows, h_hbm))):
        for c, name in enumerate(("n", "t", "z")):
            before, end, begin, after = (value[:, 0:m] for value in field[name])
            for z in range(2):
                ends_ref[0, f, c, z] = rows[c, z, 0:8] + jnp.where(
                    sub == 0, begin[z : z + 1], jnp.where(sub == 1, after[z : z + 1], 0.0)
                )
                ends_ref[1, f, c, z] = rows[c, z, 8:16] + jnp.where(
                    sub == 6, before[2 + z : 3 + z], jnp.where(sub == 7, end[2 + z : 3 + z], 0.0)
                )
        for side, at in ((0, 0), (1, n - 8)):
            dst_rows = dst.at[:, :, pl.ds(at, 8)]
            copies.append(pltpu.make_async_copy(ends_ref.at[side, f], dst_rows, sems.at[len(copies)]))
            copies[-1].start()
    gb0, gb1, ga = d["gb0"], d["gb1"], d["ga"]
    top = iota((8, wide), 0)
    change = jnp.zeros((8, wide), F32)
    for k, row in enumerate((ga[0:1], gb0[0:1], gb1[0:1], ga[2:3], gb0[2:3], gb1[2:3])):
        change = jnp.where(top == k, row, change)
    taps = filter_taps()
    terms = [change[:, 0:m] * taps[0]]
    for k in range(1, FILT + 1):
        terms.append(taps[k] * (pltpu.roll(change, k, 1)[:, 0:m] + pltpu.roll(change, wide - k, 1)[:, 0:m]))
    while len(terms) > 1:
        terms = [x + y for x, y in zip(terms[::2], terms[1::2])] + terms[len(terms) // 2 * 2 :]
    moved = terms[0]
    for side, at in ((0, 0), (1, n - EDGE)):
        rows = inner_ref[at : at + EDGE]
        for k in range(3 * side, 3 * side + 3):
            rows = rows + near_ref[k] * moved[k : k + 1]
        gap, here = jnp.zeros((EDGE - FILT, m), F32), far[FILT * side : FILT * side + FILT]
        out_ref[side] = rows + jnp.concatenate([gap, here] if side else [here, gap], axis=0)
    for side, at in ((0, 0), (1, n - EDGE)):
        copies.append(pltpu.make_async_copy(out_ref.at[side], out_hbm.at[pl.ds(at, EDGE)], sems.at[len(copies)]))
        copies[-1].start()
    for copy in copies:
        copy.wait()


def swap_pairs(count, which):
    if which == 0:
        return [(i, i ^ 1) for i in range(count)]
    return [(i, (i - 1) % count if i % 2 == 0 else (i + 1) % count) for i in range(count)]


def call(kernel, shapes, ins, scratch=(), far=(), sems=0, far_out=(), aliases=None):
    vmem = pl.BlockSpec(memory_space=pltpu.VMEM)
    hbm = pl.BlockSpec(memory_space=pltpu.HBM)
    ins = [pltpu.with_memory_space_constraint(x, pltpu.HBM) if k in far else x for k, x in enumerate(ins)]
    scratches = [s if hasattr(s, "dtype") else pltpu.VMEM(s, F32) for s in scratch]
    if sems:
        scratches.append(pltpu.SemaphoreType.DMA((sems,)))
    return pl.pallas_call(
        kernel,
        out_shape=[s if hasattr(s, "dtype") else jax.ShapeDtypeStruct(s, F32) for s in shapes],
        in_specs=[hbm if k in far else vmem for k in range(len(ins))],
        out_specs=[hbm if k in far_out else vmem for k in range(len(shapes))],
        scratch_shapes=scratches,
        input_output_aliases=aliases or {},
        compiler_params=pltpu.CompilerParams(vmem_limit_bytes=24 * 1024 * 1024),
    )(*ins)


def body(adj_e, adj_h, fwd_e, labels, eps_table, density):
    n, m = labels.shape
    block = adj_e.shape
    nz = block[1]
    gx, gy = lax.axis_size("gx"), lax.axis_size("gy")
    message = (LO_ROWS + 8, n)
    labels_in = jax.ShapeDtypeStruct((n, m), jnp.int32)
    up, down, ylo, yhi, *fetched = call(
        first_kernel,
        [message, message, (LO_ROWS, n), (HI_ROWS, n), block, block, fwd_e.shape, labels_in, (n, m), (NMAT, m)],
        [adj_e, adj_h, fwd_e, labels, density, eps_table],
        [pltpu.SMEM((NMAT,), F32)],
        range(6),
        7,
    )
    left = lax.ppermute(up, "gy", [(i, (i + 1) % gy) for i in range(gy)])
    right = lax.ppermute(down, "gy", [(i, (i - 1) % gy) for i in range(gy)])
    wide = m + 128
    bands = jax.ShapeDtypeStruct((3, wide, m), jnp.bfloat16)
    along_bands = jax.ShapeDtypeStruct((2 * FILT, 12 * FILT), jnp.bfloat16)
    xlo, xhi, grad, e2, h2, across_ref, across_thirds, along, around, near = call(
        solve_kernel,
        [(LO_ROWS, m), (HI_ROWS, m), (n, m), block, block, (wide, m), bands, along_bands, (n, n), (6, EDGE, m)],
        fetched,
    )
    message = (2 * LO_ROWS + 16, 128)
    xa, xb, lo_ext, hi_ext, cols, seams = call(
        y_kernel,
        [message, message, (LO_ROWS, wide), (HI_ROWS, wide), (n, 128), (15, 8, n)],
        [left, right, ylo, yhi, xlo, xhi, grad],
        [(128, n)],
    )
    got_a = lax.ppermute(xa, "gx", swap_pairs(gx, 0))
    got_b = lax.ppermute(xb, "gx", swap_pairs(gx, 1))
    ends = (3, nz, 16, m)
    electric, magnetic, filtered, e_rows, h_rows, inner = call(
        patch_kernel,
        [block, block, (n, m), ends, ends, (n, m)],
        [cols, seams, e2, h2, grad, across_ref, around],
        [block, block, (128, n)],
        sems=13,
        far_out=(0, 1, 2),
    )
    return tuple(
        call(
            x_kernel,
            [block, block, (n, m)],
            [got_a, got_b, lo_ext, hi_ext, e_rows, h_rows, inner, across_thirds, along, near]
            + [electric, magnetic, filtered],
            [(2, 2, 3, nz, 8, m), (2, EDGE, m)],
            (10, 11, 12),
            6,
            (0, 1, 2),
            {10: 0, 11: 1, 12: 2},
        )
    )


def solution(mesh):
    return jax.shard_map(
        body,
        mesh=mesh,
        in_specs=(
            P("design", None, "gx", "gy"),
            P("design", None, "gx", "gy"),
            P("design", None, None, "gx", "gy"),
            P(("design", "gx"), "gy"),
            P(),
            P(("design", "gx"), "gy"),
        ),
        out_specs=(
            P("design", None, "gx", "gy"),
            P("design", None, "gx", "gy"),
            P(("design", "gx"), "gy"),
        ),
        check_vma=False,
    )
```

```python
import math

import jax
import jax.numpy as jnp
from jax import lax
from jax.experimental import pallas as pl
from jax.experimental.pallas import tpu as pltpu
from jax.sharding import PartitionSpec as P

STEPS = 2
NMAT = 8
FILT = 16

courant = 0.5
spread_ratio = 0.6

F32 = jnp.float32

LO_G, LO_E1T, LO_E1Z, LO_E2T, LO_E2Z = 0, 16, 18, 20, 22
LO_F0T, LO_F0Z, LO_F1T, LO_F1N, LO_F1Z = 24, 26, 28, 30, 32
LO_W1T, LO_W1Z, LO_R0, LO_R1, LO_ROWS = 34, 36, 38, 39, 40
HI_G, HI_H0T, HI_H0Z, HI_H1T, HI_H1Z = 0, 16, 18, 20, 22
HI_WT, HI_WN, HI_WZ, HI_R, HI_ROWS = 24, 26, 28, 30, 32
PACK_F1, PACK_R, PACK_PAIR, PACK_F0, PACK_END = 16, 34, 37, 53, 57
LO_LANES = (
    list(range(FILT))
    + [PACK_PAIR + 2 * j + 1 for j in range(8)]
    + [PACK_F0 + j for j in range(4)]
    + [PACK_F1 + 3 * k + 1 for k in range(6)]
    + [PACK_F1 + 3 * k + 2 for k in (0, 1, 4, 5)]
    + [PACK_R + 1, PACK_R + 2]
)
HI_LANES = (
    list(range(128 - FILT, 128))
    + [PACK_PAIR + 2 * j for j in range(8)]
    + [PACK_F1 + 3 * k for k in range(6)]
    + [PACK_R, PACK_END]
)
REACH = FILT + 2
GROUP = 24
EDGE = 24
LO_REST, HI_REST = LO_ROWS - FILT, HI_ROWS - FILT - 1

TURN_G, TURN_OWN, TURN_X = 48, 80, 88


def filter_taps():
    spread = spread_ratio * FILT
    norm = math.sqrt(sum(math.exp(-d * d / (spread * spread)) for d in range(-FILT, FILT + 1)))
    return [math.exp(-d * d / (2.0 * spread * spread)) / norm for d in range(FILT + 1)]


def tap(distance):
    spread = spread_ratio * FILT
    norm = math.sqrt(sum(math.exp(-d * d / (spread * spread)) for d in range(-FILT, FILT + 1)))
    far = distance.astype(F32)
    value = jnp.exp(-far * far / (2.0 * spread * spread)) / norm
    return jnp.where(jnp.abs(distance) <= FILT, value, F32(0.0))


def thirds(x):
    high = x.astype(jnp.bfloat16)
    rest = x - high.astype(F32)
    middle = rest.astype(jnp.bfloat16)
    return high, middle, (rest - middle.astype(F32)).astype(jnp.bfloat16)


def narrow_dot(a, b):
    return jnp.dot(a, b, preferred_element_type=F32)


def exact_dot(a, b):
    return jnp.dot(a, b, precision=lax.Precision.HIGHEST, preferred_element_type=F32)


def iota(shape, dim):
    return lax.broadcasted_iota(jnp.int32, shape, dim)


def updates(n, m, nz):
    row, col = iota((n, m), 0), iota((n, m), 1)

    def lx(f):
        return jnp.where(row == 0, 0.0, pltpu.roll(f, 1, 0))

    def ux(f):
        return jnp.where(row == n - 1, 0.0, pltpu.roll(f, n - 1, 0))

    def ly(f):
        return jnp.where(col == 0, 0.0, pltpu.roll(f, 1, 1))

    def uy(f):
        return jnp.where(col == m - 1, 0.0, pltpu.roll(f, m - 1, 1))

    def turn(h, ratio):
        out = [[None] * nz for _ in range(3)]
        for z in range(nz):
            hx, hy, hz = h[0][z], h[1][z], h[2][z]
            dzx = hx - h[0][z - 1] if z > 0 else hx
            dzy = hy - h[1][z - 1] if z > 0 else hy
            out[0][z] = ratio * ((hz - ly(hz)) - dzy)
            out[1][z] = ratio * (dzx - (hz - lx(hz)))
            out[2][z] = ratio * ((hy - lx(hy)) - (hx - ly(hx)))
        return out

    def magnetic(e, h):
        out = [[None] * nz for _ in range(3)]
        for z in range(nz):
            ex, ey, ez = e[0][z], e[1][z], e[2][z]
            dzx = e[0][z + 1] - ex if z < nz - 1 else -ex
            dzy = e[1][z + 1] - ey if z < nz - 1 else -ey
            out[0][z] = h[0][z] + courant * ((uy(ez) - ez) - dzy)
            out[1][z] = h[1][z] + courant * (dzx - (ux(ez) - ez))
            out[2][z] = h[2][z] + courant * ((ux(ey) - ey) - (uy(ex) - ex))
        return out

    return turn, magnetic


def less(e, change):
    return [[a - b for a, b in zip(one, other, strict=True)] for one, other in zip(e, change, strict=True)]


def product(e, f):
    total = None
    for c in range(3):
        for z in range(len(e[c])):
            term = e[c][z] * f[c][z]
            total = term if total is None else total + term
    return total


def local_solve(e0, h0, saved, ratio):
    turn, magnetic = updates(*ratio.shape, len(e0[0]))
    e1 = less(e0, turn(h0, ratio))
    h1 = magnetic(e1, h0)
    fwd = [saved(0)]
    grad = product(e1, fwd[0])
    e2 = less(e1, turn(h1, ratio))
    fwd.append(saved(1))
    grad = grad + product(e2, fwd[1])
    return e1, h1, e2, grad, fwd


def depth_shifts(shape):
    odd = iota(shape, 0) % 2 == 1
    return (
        lambda f: jnp.where(odd, 0.0, pltpu.roll(f, 7, 0)),
        lambda f: jnp.where(odd, pltpu.roll(f, 1, 0), 0.0),
    )


def seam_magnetic(sgn, v, up):
    half = sgn * courant
    uz, _ = depth_shifts(v[0].shape)
    e2t, e2n, e2z, f2t, f2z, g2t, g2n, g2z, ah1t, ah1z, bh1t, bh1n, bh1z, e2t_b, e2z_b = v
    none = jnp.zeros_like(e2t)
    return {
        "t": (
            half * g2z,
            ah1t + half * ((e2z_b - g2z) - (uz(g2n) - g2n)),
            bh1t + half * ((f2z - e2z) - (uz(e2n) - e2n)),
            -half * f2z,
        ),
        "n": (
            none,
            half * ((uz(g2t) - g2t) - (up(g2z) - g2z)),
            bh1n + half * ((uz(e2t) - e2t) - (up(e2z) - e2z)),
            half * ((uz(f2t) - f2t) - (up(f2z) - f2z)),
        ),
        "z": (
            -half * g2t,
            ah1z + half * ((up(g2n) - g2n) - (e2t_b - g2t)),
            bh1z + half * ((up(e2n) - e2n) - (f2t - e2t)),
            half * f2t,
        ),
    }


def seam(sgn, a, b, up, down):
    odd = iota(a["h0t"].shape, 0) % 2 == 1
    half = sgn * courant
    uz, lz = depth_shifts(a["h0t"].shape)
    rb, rb1, ra = sgn * b["r0"], sgn * b["r1"], sgn * a["r"]
    d = {}
    e1t = rb * a["h0z"]
    e1z = -rb * a["h0t"]
    e1t_b = b["e1t"] + e1t
    e1z_b = b["e1z"] + e1z
    ah1t = half * e1z_b
    ah1z = -half * e1t_b
    h1t_a = a["h1t"] + ah1t
    h1z_a = a["h1z"] + ah1z
    bh1t = -half * e1z
    bh1n = half * ((uz(e1t) - e1t) - (up(e1z) - e1z))
    bh1z = half * e1t
    e2t = e1t - rb * ((bh1z - h1z_a) - (bh1n - lz(bh1n)))
    e2n = -rb * ((bh1t - lz(bh1t)) - (bh1z - down(bh1z)))
    e2z = e1z - rb * ((bh1n - down(bh1n)) - (bh1t - h1t_a))
    f2t = rb1 * bh1z
    f2z = -rb1 * bh1t
    at = ah1z
    an = (ah1t - lz(ah1t)) - (ah1z - down(ah1z))
    az = -ah1t
    g2t, g2n, g2z = -ra * at, -ra * an, -ra * az
    gb0 = b["f0t"] * e1t + b["f0z"] * e1z + b["f1t"] * e2t + b["f1n"] * e2n + b["f1z"] * e2z
    gb1 = sgn * (b["w1t"] * bh1z - b["w1z"] * bh1t)
    ga = -sgn * (a["wt"] * at + a["wn"] * an + a["wz"] * az)
    e2t_b = b["e2t"] + e2t
    e2z_b = b["e2z"] + e2z
    d["b_e1z"], d["b_h1n"], d["b_h1z"], d["a_h1z"] = e1z, bh1n, bh1z, ah1z
    none = jnp.zeros_like(e1t)
    d["e"] = {"t": (none, g2t, e2t, f2t), "n": (none, g2n, e2n, none), "z": (none, g2z, e2z, f2z)}
    d["v"] = (e2t, e2n, e2z, f2t, f2z, g2t, g2n, g2z, ah1t, ah1z, bh1t, bh1n, bh1z, e2t_b, e2z_b)
    d["gb0"], d["gb1"], d["ga"] = (g + pltpu.roll(g, 7, 0) for g in (gb0, gb1, ga))
    return d


def two(first, second, at, count=2):
    if count == 1:
        one, other = first[at : at + 1], second[at : at + 1]
        parts = [one, one, other, other]
    else:
        parts = [first[at : at + 2], second[at : at + 2]]
    parts.append(jnp.zeros((4, first.shape[1]), F32))
    return jnp.concatenate(parts, axis=0)


def seam_inputs(left_hi, my_hi, my_lo, right_lo):
    a = {
        "h0t": two(left_hi, my_hi, HI_H0T),
        "h0z": two(left_hi, my_hi, HI_H0Z),
        "h1t": two(left_hi, my_hi, HI_H1T),
        "h1z": two(left_hi, my_hi, HI_H1Z),
        "wt": two(left_hi, my_hi, HI_WT),
        "wn": two(left_hi, my_hi, HI_WN),
        "wz": two(left_hi, my_hi, HI_WZ),
        "r": two(left_hi, my_hi, HI_R, 1),
    }
    b = {
        "e1t": two(my_lo, right_lo, LO_E1T),
        "e1z": two(my_lo, right_lo, LO_E1Z),
        "e2t": two(my_lo, right_lo, LO_E2T),
        "e2z": two(my_lo, right_lo, LO_E2Z),
        "f0t": two(my_lo, right_lo, LO_F0T),
        "f0z": two(my_lo, right_lo, LO_F0Z),
        "f1t": two(my_lo, right_lo, LO_F1T),
        "f1n": two(my_lo, right_lo, LO_F1N),
        "f1z": two(my_lo, right_lo, LO_F1Z),
        "w1t": two(my_lo, right_lo, LO_W1T),
        "w1z": two(my_lo, right_lo, LO_W1Z),
        "r0": two(my_lo, right_lo, LO_R0, 1),
        "r1": two(my_lo, right_lo, LO_R1, 1),
    }
    return a, b


def even(axis):
    return lax.axis_index(axis) % 2 == 0


def ratio_of(labels, density, table):
    eps = jnp.broadcast_to(table[0], labels.shape)
    for k in range(1, NMAT):
        eps = jnp.where(labels == k, table[k], eps)
    return courant / (eps + density)


def planes(ref, *lead):
    return [[ref[(*lead, c, z)] for z in range(ref.shape[-3])] for c in range(3)]


def edge_lists(t, nrm, e1, h0, h1, e2, fwd, ratio):
    zs = range(len(e1[0]))
    lo = (
        [(e1[c][z], 0) for c in (t, 2) for z in zs]
        + [(e2[c][z], 0) for c in (t, 2) for z in zs]
        + [(fwd[0][c][z], 0) for c in (t, 2) for z in zs]
        + [(fwd[1][c][z], 0) for c in (t, nrm, 2) for z in zs]
        + [((ratio, fwd[1][c][z]), 1) for c in (t, 2) for z in zs]
        + [(ratio, 0), (ratio, 1)]
    )
    hi = (
        [(h0[c][z], -1) for c in (t, 2) for z in zs]
        + [(h1[c][z], -1) for c in (t, 2) for z in zs]
        + [((ratio, fwd[1][c][z]), -1) for c in (t, nrm, 2) for z in zs]
        + [(ratio, -1)]
    )
    return lo, hi


def fold(plane):
    m = plane.shape[1]
    lane = iota((plane.shape[0], 128), 1)
    return jnp.where(lane < 64, plane[:, 0:128], plane[:, m - 128 : m])


def place(pack, values, base, count=3):
    lane = iota((1, 128), 1)
    return jnp.where((lane >= base) & (lane < base + count), pltpu.roll(values, base + 1, 1), pack)


def unpack_rows(packed, lanes, ref):
    ref[0:FILT] = packed[lanes[0] : lanes[0] + FILT]
    for k in range(FILT, len(lanes)):
        ref[k : k + 1] = packed[lanes[k] : lanes[k] + 1]


def line(item, at):
    if isinstance(item, tuple):
        return line(item[0], at) * line(item[1], at)
    at = at % item.shape[0]
    return item[at : at + 1]


def side_by_side(tiles, width, first):
    lane = iota((8, 128), 1)
    out = None
    for k, tile in enumerate(tiles):
        moved = pltpu.roll(tile, (width * k - first) % 128, 1)
        out = moved if out is None else jnp.where(lane < width * k, out, moved)
    return out


def first_kernel(e_hbm, h_hbm, f_hbm, lab_hbm, den_hbm, eps_hbm,
                 up_ref, down_ref, lo_ref, hi_ref, e_ref, h_ref, f_ref, lab_ref, den_ref, table_ref,
                 tab_ref, sems):
    n, m = lab_hbm.shape
    nz = e_hbm.shape[1]
    copies = []
    for src, dst in ((h_hbm, h_ref), (lab_hbm, lab_ref), (den_hbm, den_ref), (eps_hbm, tab_ref), (e_hbm, e_ref),
                     (f_hbm.at[0], f_ref.at[0]), (f_hbm.at[1], f_ref.at[1])):
        copies.append(pltpu.make_async_copy(src, dst, sems.at[len(copies)]))
        copies[-1].start()

    def folded(ref, *lead):
        return [[fold(plane) for plane in comp] for comp in planes(ref, *lead)]

    turn, magnetic = updates(n, 128, nz)
    sides = [(c, z) for c in (0, 2) for z in range(nz)]
    lane = iota((n, 128), 1)
    for copy in copies[1:4]:
        copy.wait()
    ratio = ratio_of(fold(lab_ref[...]), fold(den_ref[...]), tab_ref)
    copies[0].wait()
    h0 = folded(h_ref)
    change = turn(h0, ratio)
    copies[4].wait()
    e1 = less(folded(e_ref), change)
    h1 = magnetic(e1, h0)
    e2 = less(e1, turn(h1, ratio))
    pack = place(jnp.zeros((n, 128), F32), ratio, PACK_R)
    copies[5].wait()
    fwd = [folded(f_ref, 0)]
    grad = product(e1, fwd[0])
    for k, (first, last) in enumerate(((e1, h0), (e2, h1))):
        for j, (c, z) in enumerate(sides):
            pack = place(pack, jnp.where(lane < 64, first[c][z], last[c][z]), PACK_PAIR + 8 * k + 2 * j, 2)
    for j, (c, z) in enumerate(sides):
        pack = jnp.where(lane == PACK_F0 + j, pltpu.roll(fwd[0][c][z], PACK_F0 + j, 1), pack)
    copies[6].wait()
    fwd.append(folded(f_ref, 1))
    grad = grad + product(e2, fwd[1])
    pack = jnp.where((lane < FILT) | (lane >= 128 - FILT), grad, pack)
    scale = jnp.where(lane == 0, 1.0, ratio)
    for k, (c, z) in enumerate((c, z) for c in range(3) for z in range(nz)):
        pack = place(pack, fwd[1][c][z] * scale, PACK_F1 + 3 * k)
    packed = pack.T
    unpack_rows(packed, LO_LANES, lo_ref)
    unpack_rows(packed, HI_LANES, hi_ref)
    lo, hi = edge_lists(1, 0, e1, h0, h1, e2, fwd, ratio)
    rest = [line(*entry) for entry in lo + hi]
    rest = jnp.concatenate(rest + [jnp.zeros((1, 128), F32)], axis=0)
    tiles = [rest[8 * k : 8 * k + 8] for k in range(rest.shape[0] // 8)]
    down_ref[0:LO_ROWS] = lo_ref[...]
    down_ref[LO_ROWS : LO_ROWS + 8] = side_by_side(tiles, GROUP, 0)
    up_ref[0:HI_ROWS] = hi_ref[...]
    up_ref[HI_ROWS:LO_ROWS] = jnp.zeros((LO_ROWS - HI_ROWS, n), F32)
    up_ref[LO_ROWS : LO_ROWS + 8] = side_by_side(tiles, GROUP, 128 - REACH)
    for k in range(NMAT):
        table_ref[k : k + 1] = jnp.full((1, m), tab_ref[k], F32)


def solve_kernel(e_ref, h_ref, f_ref, lab_ref, den_ref, table_ref,
                 lo_ref, hi_ref, grad_ref, e2_ref, h2_ref, across_ref, across_thirds, along_ref, around_ref, near_ref):
    n, m = lab_ref.shape
    nz = e_ref.shape[1]
    ratio = ratio_of(lab_ref[...], den_ref[...], [table_ref[k : k + 1] for k in range(NMAT)])
    h0 = planes(h_ref)
    e1, h1, e2, grad, fwd = local_solve(planes(e_ref), h0, lambda step: planes(f_ref, step), ratio)
    grad_ref[...] = grad
    lo, hi = edge_lists(1, 0, e1, h0, h1, e2, fwd, ratio)
    for ref, group, strip in ((hi_ref, hi, grad[n - FILT : n]), (lo_ref, lo, grad[0:FILT])):
        ref[0:FILT] = strip
        for k, (item, at) in enumerate(group):
            ref[FILT + k : FILT + k + 1] = line(item, at)
    hi_ref[HI_ROWS - 1 : HI_ROWS] = jnp.zeros((1, m), F32)
    _, magnetic = updates(n, m, nz)
    h2 = magnetic(e2, h1)
    for c in range(3):
        for z in range(nz):
            e2_ref[c, z] = e2[c][z]
            h2_ref[c, z] = h2[c][z]
    wide = across_ref.shape[0]
    across = tap(cyclic(iota((wide, m), 0) - iota((wide, m), 1), wide))
    across_ref[...] = across
    for k, third in enumerate(thirds(across)):
        across_thirds[k] = third
    around_ref[...] = tap(iota((n, n), 0) - iota((n, n), 1))
    k, r = iota((2 * FILT, 2 * FILT), 1), iota((2 * FILT, 2 * FILT), 0)
    same = (k < FILT) == (r < FILT)
    high, middle, low = thirds(jnp.where(same, tap(k - r + jnp.where(r < FILT, -FILT, FILT)), 0.0))
    along_ref[...] = jnp.concatenate([high, middle, low, high, middle, high], axis=1)
    r = iota((EDGE, m), 0)
    for k in range(3):
        near_ref[k] = tap(r - (k - 1))
        near_ref[3 + k] = tap(r - EDGE - (k - 1))


def put_lines(ref, lines):
    for c, name in enumerate(("t", "n", "z")):
        before, end, begin, after = lines[name]
        for z in range(2):
            p = 4 * (2 * c + z)
            ref[p : p + 1] = before[2 + z : 3 + z]
            ref[p + 1 : p + 2] = end[2 + z : 3 + z]
            ref[p + 2 : p + 3] = begin[z : z + 1]
            ref[p + 3 : p + 4] = after[z : z + 1]


def extended(grad, columns):
    m = grad.shape[1]
    lane = iota(columns.shape, 1)
    own = pltpu.roll(columns, 128 - TURN_OWN - 1, 1)
    outside = jnp.where(lane < FILT, pltpu.roll(columns, 128 - TURN_G, 1), 0.0)
    return [
        grad[:, 0:128] + jnp.where(lane < 2, own, 0.0),
        grad[:, m - 128 : m] + jnp.where(lane == 127, own, 0.0),
        jnp.where(lane >= 128 - FILT, pltpu.roll(columns, 128 - TURN_G - 2 * FILT, 1), outside),
    ]


def y_kernel(left_ref, right_ref, lo_ref, hi_ref, xlo_ref, xhi_ref, grad_ref,
             a_ref, b_ref, lo_ext, hi_ext, cols_ref, seam_ref, turned_ref):
    n, m = grad_ref.shape
    right, left = right_ref[0:LO_ROWS], left_ref[0:HI_ROWS]
    a, b = seam_inputs(left, hi_ref[...], lo_ref[...], right)
    lane = iota((8, n), 1)
    d = seam(
        1.0, a, b,
        lambda f: jnp.where(lane == n - 1, 0.0, pltpu.roll(f, n - 1, 1)),
        lambda f: jnp.where(lane == 0, 0.0, pltpu.roll(f, 1, 1)),
    )
    for k, value in enumerate(d["v"]):
        seam_ref[k] = value
    put_lines(turned_ref, d["e"])
    turned_ref[24:TURN_G] = jnp.zeros((TURN_G - 24, n), F32)
    gb0, gb1, ga = d["gb0"], d["gb1"], d["ga"]
    top = iota((8, n), 0)
    at = TURN_G
    turned_ref[at : at + 8] = right[0:8] + jnp.where(top == 0, gb0[2:3], jnp.where(top == 1, gb1[2:3], 0.0))
    turned_ref[at + 8 : at + 16] = right[8:16]
    turned_ref[at + 16 : at + 24] = left[0:8]
    turned_ref[at + 24 : at + 32] = left[8:16] + jnp.where(top == 7, ga[0:1], 0.0)
    turned_ref[TURN_OWN : TURN_OWN + 8] = jnp.where(
        top == 0, ga[2:3], jnp.where(top == 1, gb0[0:1], jnp.where(top == 2, gb1[0:1], 0.0))
    )
    none = jnp.zeros((8, n), F32)
    for k, (last, first) in enumerate(((none, d["b_e1z"]), (none, d["b_h1n"]), (d["a_h1z"], d["b_h1z"]))):
        for z in range(2):
            p = TURN_X + 4 * (2 * k + z)
            turned_ref[p : p + 1] = last[2 + z : 3 + z]
            turned_ref[p + 1 : p + 2] = first[z : z + 1]
            turned_ref[p + 2 : p + 3] = last[z : z + 1]
            turned_ref[p + 3 : p + 4] = first[2 + z : 3 + z]
    turned_ref[TURN_X + 24 : 128] = jnp.zeros((128 - TURN_X - 24, n), F32)
    columns = turned_ref[...].T
    cols_ref[...] = columns

    lane = iota((8, 128), 1)
    right_tile, left_tile = right_ref[LO_ROWS : LO_ROWS + 8], left_ref[LO_ROWS : LO_ROWS + 8]
    rest = []
    for k in range(LO_ROWS // 8):
        part = jnp.where(lane < REACH, pltpu.roll(right_tile, (128 - GROUP * k) % 128, 1), 0.0)
        rest.append(jnp.where(lane >= 128 - REACH, pltpu.roll(left_tile, (128 - REACH - GROUP * k) % 128, 1), part))
    rest = jnp.concatenate(rest, axis=0)
    for ref, mine, strip, halo in (
        (lo_ext, xlo_ref, slice(0, FILT), rest[0:LO_REST]),
        (hi_ext, xhi_ref, slice(n - FILT, n), rest[LO_REST : LO_REST + HI_REST]),
    ):
        count = mine.shape[0]
        for k, tile in enumerate(extended(grad_ref[strip], columns[strip])):
            ref[0:FILT, 128 * k : 128 * k + 128] = tile
        ref[FILT:count, 0:m] = mine[FILT:count]
        ref[FILT : FILT + halo.shape[0], m : m + 128] = halo
    hi_ext[HI_ROWS - 1 : HI_ROWS, m : m + 128] = jnp.zeros((1, 128), F32)
    one = iota((1, 128), 1)
    first, last = columns[0:1], columns[n - 1 : n]

    def add(ref, k, row, at, halo=True):
        inner = pltpu.roll(row, (127 - at) % 128, 1)
        ref[k : k + 1, 0:128] += jnp.where(one < (1 if halo else 2), inner, 0.0)
        ref[k : k + 1, m - 128 : m] += jnp.where(one == 127, inner, 0.0)
        if halo:
            outer = pltpu.roll(row, (125 - at) % 128, 1)
            ref[k : k + 1, m : m + 128] += jnp.where((one == 127) | (one == 0), outer, 0.0)

    for z in range(2):
        add(lo_ext, LO_E1Z + z, first, TURN_X + 4 * z)
        add(hi_ext, HI_H1T + z, last, TURN_X + 8 + 4 * z)
        add(hi_ext, HI_H1Z + z, last, TURN_X + 16 + 4 * z)
        add(lo_ext, LO_E2T + z, first, 4 * (2 + z) + 1, False)
        add(lo_ext, LO_E2Z + z, first, 4 * (4 + z) + 1, False)

    first_even = even("gx")
    low = lo_ext[...]
    high = jnp.concatenate([hi_ext[...], jnp.zeros((LO_ROWS - HI_ROWS, m + 128), F32)], axis=0)
    for ref, part in ((a_ref, jnp.where(first_even, high, low)), (b_ref, jnp.where(first_even, low, high))):
        ref[0:LO_ROWS] = part[:, 0:128]
        ref[LO_ROWS : 2 * LO_ROWS] = part[:, 128:256]
        tiles = [part[8 * k : 8 * k + 8, m : m + 128] for k in range(LO_ROWS // 8)]
        ref[2 * LO_ROWS : 2 * LO_ROWS + 8] = side_by_side(tiles[:3], 2 * REACH, 128 - REACH)
        ref[2 * LO_ROWS + 8 : 2 * LO_ROWS + 16] = side_by_side(tiles[3:], 2 * REACH, 128 - REACH)


def cyclic(d, count):
    return jnp.where(d > count // 2, d - count, jnp.where(d < -(count // 2), d + count, d))


def patch_kernel(cols_ref, seam_ref, e2_ref, h2_ref, grad_ref, across_ref, around_ref,
                 e_hbm, h_hbm, out_hbm, e_rows, h_rows, inner_ref,
                 e_ref, h_ref, turned_ref, sems):
    n, m = grad_ref.shape
    lane = iota((n, 128), 1)
    columns = cols_ref[...]
    copies = []

    def patch(columns, src, ref, dst, rows):
        for c in range(3):
            for z in range(2):
                p = 4 * (2 * c + z)
                moved = pltpu.roll(columns, (126 - p) % 128, 1)
                ref[c, z, :, 0:128] = src[c, z, :, 0:128] + jnp.where(lane < 2, moved, 0.0)
                ref[c, z, :, m - 128 : m] = src[c, z, :, m - 128 : m] + jnp.where(lane >= 126, moved, 0.0)
                rows[c, z, 0:8] = ref[c, z, 0:8]
                rows[c, z, 8:16] = ref[c, z, n - 8 : n]
                copies.append(pltpu.make_async_copy(ref.at[c, z], dst.at[c, z], sems.at[len(copies)]))
                copies[-1].start()

    patch(columns, e2_ref, e_ref, e_hbm, e_rows)
    row = iota((8, n), 1)
    up = lambda f: jnp.where(row == n - 1, 0.0, pltpu.roll(f, n - 1, 1))
    put_lines(turned_ref, seam_magnetic(1.0, [seam_ref[k] for k in range(15)], up))
    turned_ref[24:128] = jnp.zeros((104, n), F32)
    patch(turned_ref[...].T, h2_ref, h_ref, h_hbm, h_rows)
    grad_ext = jnp.concatenate(extended(grad_ref[...], columns), axis=1)
    part = exact_dot(grad_ext, across_ref[...])
    inner_ref[...] = exact_dot(around_ref[...], part)
    rows = pl.ds(EDGE, n - 2 * EDGE)
    copies.append(pltpu.make_async_copy(inner_ref.at[rows], out_hbm.at[rows], sems.at[len(copies)]))
    copies[-1].start()
    for copy in copies:
        copy.wait()


def x_kernel(ra_ref, rb_ref, lo_ref, hi_ref, e_rows, h_rows, inner_ref, across_thirds, along_ref, near_ref,
             e_in, h_in, out_in, e_hbm, h_hbm, out_hbm, ends_ref, out_ref, sems):
    n, m = inner_ref.shape
    wide = lo_ref.shape[1]
    first_even = even("gx")
    tile_lane = iota((8, 128), 1)

    def unfold(message):
        outer = []
        for k in range(LO_ROWS // 8):
            at = 2 * LO_ROWS + 8 * (k // 3)
            moved = pltpu.roll(message[at : at + 8], 128 - REACH - 2 * REACH * (k % 3), 1)
            outer.append(jnp.where((tile_lane < REACH) | (tile_lane >= 128 - REACH), moved, 0.0))
        return jnp.concatenate([message[0:LO_ROWS], message[LO_ROWS : 2 * LO_ROWS], jnp.concatenate(outer, axis=0)], axis=1)

    right = unfold(jnp.where(first_even, ra_ref[...], rb_ref[...]))
    left = unfold(jnp.where(first_even, rb_ref[...], ra_ref[...]))
    a, b = seam_inputs(left, hi_ref[...], lo_ref[...], right)
    raw = jnp.concatenate([left[0:FILT], right[0:FILT]], axis=0)
    high, middle, low = thirds(raw)
    one = narrow_dot(jnp.concatenate([high, middle, low], axis=0), across_thirds[0])
    two_ = narrow_dot(jnp.concatenate([high, middle], axis=0), across_thirds[1])
    three = narrow_dot(high, across_thirds[2])
    k = 2 * FILT
    part = ((one[2 * k : 3 * k] + two_[k : 2 * k] + three) + (one[k : 2 * k] + two_[0:k])) + one[0:k]
    high, middle, low = thirds(part)
    far = narrow_dot(along_ref[...], jnp.concatenate([low, middle, high, middle, high, high], axis=0))
    d = seam(-1.0, a, b, lambda f: pltpu.roll(f, wide - 1, 1), lambda f: pltpu.roll(f, 1, 1))
    copies = []
    sub = iota((8, m), 0)
    magnetic = seam_magnetic(-1.0, d["v"], lambda f: pltpu.roll(f, wide - 1, 1))
    for f, (field, rows, dst) in enumerate(((d["e"], e_rows, e_hbm), (magnetic, h_rows, h_hbm))):
        for c, name in enumerate(("n", "t", "z")):
            before, end, begin, after = (value[:, 0:m] for value in field[name])
            for z in range(2):
                ends_ref[0, f, c, z] = rows[c, z, 0:8] + jnp.where(
                    sub == 0, begin[z : z + 1], jnp.where(sub == 1, after[z : z + 1], 0.0)
                )
                ends_ref[1, f, c, z] = rows[c, z, 8:16] + jnp.where(
                    sub == 6, before[2 + z : 3 + z], jnp.where(sub == 7, end[2 + z : 3 + z], 0.0)
                )
        for side, at in ((0, 0), (1, n - 8)):
            dst_rows = dst.at[:, :, pl.ds(at, 8)]
            copies.append(pltpu.make_async_copy(ends_ref.at[side, f], dst_rows, sems.at[len(copies)]))
            copies[-1].start()
    gb0, gb1, ga = d["gb0"], d["gb1"], d["ga"]
    top = iota((8, wide), 0)
    change = jnp.zeros((8, wide), F32)
    for k, row in enumerate((ga[0:1], gb0[0:1], gb1[0:1], ga[2:3], gb0[2:3], gb1[2:3])):
        change = jnp.where(top == k, row, change)
    taps = filter_taps()
    terms = [change[:, 0:m] * taps[0]]
    for k in range(1, FILT + 1):
        terms.append(taps[k] * (pltpu.roll(change, k, 1)[:, 0:m] + pltpu.roll(change, wide - k, 1)[:, 0:m]))
    while len(terms) > 1:
        terms = [x + y for x, y in zip(terms[::2], terms[1::2])] + terms[len(terms) // 2 * 2 :]
    moved = terms[0]
    for side, at in ((0, 0), (1, n - EDGE)):
        rows = inner_ref[at : at + EDGE]
        for k in range(3 * side, 3 * side + 3):
            rows = rows + near_ref[k] * moved[k : k + 1]
        gap, here = jnp.zeros((EDGE - FILT, m), F32), far[FILT * side : FILT * side + FILT]
        out_ref[side] = rows + jnp.concatenate([gap, here] if side else [here, gap], axis=0)
    for side, at in ((0, 0), (1, n - EDGE)):
        copies.append(pltpu.make_async_copy(out_ref.at[side], out_hbm.at[pl.ds(at, EDGE)], sems.at[len(copies)]))
        copies[-1].start()
    for copy in copies:
        copy.wait()


def swap_pairs(count, which):
    if which == 0:
        return [(i, i ^ 1) for i in range(count)]
    return [(i, (i - 1) % count if i % 2 == 0 else (i + 1) % count) for i in range(count)]


def call(kernel, shapes, ins, scratch=(), far=(), sems=0, far_out=(), aliases=None):
    vmem = pl.BlockSpec(memory_space=pltpu.VMEM)
    hbm = pl.BlockSpec(memory_space=pltpu.HBM)
    ins = [pltpu.with_memory_space_constraint(x, pltpu.HBM) if k in far else x for k, x in enumerate(ins)]
    scratches = [s if hasattr(s, "dtype") else pltpu.VMEM(s, F32) for s in scratch]
    if sems:
        scratches.append(pltpu.SemaphoreType.DMA((sems,)))
    return pl.pallas_call(
        kernel,
        out_shape=[s if hasattr(s, "dtype") else jax.ShapeDtypeStruct(s, F32) for s in shapes],
        in_specs=[hbm if k in far else vmem for k in range(len(ins))],
        out_specs=[hbm if k in far_out else vmem for k in range(len(shapes))],
        scratch_shapes=scratches,
        input_output_aliases=aliases or {},
        compiler_params=pltpu.CompilerParams(vmem_limit_bytes=24 * 1024 * 1024),
    )(*ins)


def body(adj_e, adj_h, fwd_e, labels, eps_table, density):
    n, m = labels.shape
    block = adj_e.shape
    nz = block[1]
    gx, gy = lax.axis_size("gx"), lax.axis_size("gy")
    message = (LO_ROWS + 8, n)
    labels_in = jax.ShapeDtypeStruct((n, m), jnp.int32)
    up, down, ylo, yhi, *fetched = call(
        first_kernel,
        [message, message, (LO_ROWS, n), (HI_ROWS, n), block, block, fwd_e.shape, labels_in, (n, m), (NMAT, m)],
        [adj_e, adj_h, fwd_e, labels, density, eps_table],
        [pltpu.SMEM((NMAT,), F32)],
        range(6),
        7,
    )
    left = lax.ppermute(up, "gy", [(i, (i + 1) % gy) for i in range(gy)])
    right = lax.ppermute(down, "gy", [(i, (i - 1) % gy) for i in range(gy)])
    wide = m + 128
    bands = jax.ShapeDtypeStruct((3, wide, m), jnp.bfloat16)
    along_bands = jax.ShapeDtypeStruct((2 * FILT, 12 * FILT), jnp.bfloat16)
    xlo, xhi, grad, e2, h2, across_ref, across_thirds, along, around, near = call(
        solve_kernel,
        [(LO_ROWS, m), (HI_ROWS, m), (n, m), block, block, (wide, m), bands, along_bands, (n, n), (6, EDGE, m)],
        fetched,
    )
    message = (2 * LO_ROWS + 16, 128)
    xa, xb, lo_ext, hi_ext, cols, seams = call(
        y_kernel,
        [message, message, (LO_ROWS, wide), (HI_ROWS, wide), (n, 128), (15, 8, n)],
        [left, right, ylo, yhi, xlo, xhi, grad],
        [(128, n)],
    )
    got_a = lax.ppermute(xa, "gx", swap_pairs(gx, 0))
    got_b = lax.ppermute(xb, "gx", swap_pairs(gx, 1))
    ends = (3, nz, 16, m)
    electric, magnetic, filtered, e_rows, h_rows, inner = call(
        patch_kernel,
        [block, block, (n, m), ends, ends, (n, m)],
        [cols, seams, e2, h2, grad, across_ref, around],
        [block, block, (128, n)],
        sems=13,
        far_out=(0, 1, 2),
    )
    return tuple(
        call(
            x_kernel,
            [block, block, (n, m)],
            [got_a, got_b, lo_ext, hi_ext, e_rows, h_rows, inner, across_thirds, along, near]
            + [electric, magnetic, filtered],
            [(2, 2, 3, nz, 8, m), (2, EDGE, m)],
            (10, 11, 12),
            6,
            (0, 1, 2),
            {10: 0, 11: 1, 12: 2},
        )
    )


def solution(mesh):
    return jax.shard_map(
        body,
        mesh=mesh,
        in_specs=(
            P("design", None, "gx", "gy"),
            P("design", None, "gx", "gy"),
            P("design", None, None, "gx", "gy"),
            P(("design", "gx"), "gy"),
            P(),
            P(("design", "gx"), "gy"),
        ),
        out_specs=(
            P("design", None, "gx", "gy"),
            P("design", None, "gx", "gy"),
            P(("design", "gx"), "gy"),
        ),
        check_vma=False,
    )
```
